128 devices in a mesh: gx: 8 (over z, core), gy: 16 (over y, x).
Axes of the slice: x: 4, y: 4, z: 4, core: 2. Of those that a mesh axis runs over, the one named last changes fastest.
Arguments:
- right_side: float32 [3, 2, 16, 128, 1024], P(None, None, None, 'gy', 'gx'), may hold values from -14 to 14
- materials: int32 [16, 128, 1024], P(None, 'gy', 'gx'), may hold values from 0 to 7
- sigma_diag: float32 [3, 8], replicated, may hold values from 0.1 to 10
- sigma_off: float32 [3, 8], replicated, may hold values from -0.45 to 0.45
Outputs:
- solution: float32 [3, 2, 16, 128, 1024], P(None, None, None, 'gy', 'gx')
- hessenberg: float32 [3, 2], replicated
The draws below stay inside these ranges and needn't reach their ends.
All inputs are finite; a program needn't handle non-finite values.
Results may differ from the reference program's by a relative error of at most 0.0001.
Values sent between devices are 32-bit elements; how exact they have to be, the bound alone decides.
No kernel may reach another device: no remote copies, remote signals or barrier semaphores. Data moves between devices by JAX's collectives and lax.ppermute only.
A program may use at most 128 MiB of HBM per device.

```python
import math
import jax
import jax.numpy as jnp
from jax import lax

NZ = 16
NMAT = 8
ITERS = 2
NX = 1024
NY = 128


def draw_right_side(key, part):
    key = jax.random.fold_in(key, 17)
    noise_key = jax.random.fold_in(key, 0)
    full_shape = (3, 2, NZ, NY, NX)
    east_position = jnp.arange(NX, dtype=jnp.float32) / NX
    north_position = jnp.arange(NY, dtype=jnp.float32) / NY
    envelope = jnp.power(10.0, 0.5 * east_position[None, :] + 0.5 * north_position[:, None]) / 3.0
    noise_part = jnp.clip(jax.random.normal(noise_key, full_shape, jnp.float32), -4.0, 4.0)
    return noise_part * envelope


def plant(entries, key, smallest, largest):
    shape = entries.shape
    place = [jax.random.randint(jax.random.fold_in(key, axis), (), 0, shape[axis]) for axis in range(len(shape))]
    entries = entries.at[tuple(place)].set(smallest)
    longest = shape.index(max(shape))
    place[longest] = (place[longest] + 1) % shape[longest]
    return entries.at[tuple(place)].set(largest)


def setup_inputs(seed: int = 0) -> dict:
    key_list = jax.random.split(jax.random.key(seed), 5)
    return {
        "right_side": draw_right_side(jax.random.fold_in(key_list[4], 71), 0),
        "materials": plant(jax.random.randint(key_list[1], (NZ, NY, NX), 0, NMAT), jax.random.fold_in(key_list[1], 1), 0, NMAT - 1).astype(jnp.int32),
        "sigma_diag": jnp.clip(jnp.exp(jax.random.uniform(key_list[2], (3, NMAT), jnp.float32, math.log(0.1), math.log(10.0))), 0.1, 10.0),
        "sigma_off": jnp.clip(jax.random.uniform(key_list[3], (3, NMAT), jnp.float32, -0.45, 0.45), -0.45, 0.45),
    }


omega_shift = 2.0
edge_center = 4.0
node_center = 6.0
nodal_shift = 4.0
edge_first = 0.7
edge_second = 0.6
node_first = 0.8
node_second = 0.5
epsilon = 1e-06

def forward_depth(values):
    zero_layer = jnp.zeros_like(values[..., :1, :, :])
    return jnp.concatenate([values[..., 1:, :, :], zero_layer], axis=-3) - values

def backward_depth(values):
    zero_layer = jnp.zeros_like(values[..., :1, :, :])
    return jnp.concatenate([zero_layer, values[..., :-1, :, :]], axis=-3) - values

def forward_east(values):
    return jnp.roll(values, -1, axis=-1) - values

def backward_east(values):
    return jnp.roll(values, 1, axis=-1) - values

def forward_north(values):
    return jnp.roll(values, -1, axis=-2) - values

def backward_north(values):
    return jnp.roll(values, 1, axis=-2) - values

def tensor_table(sigma_diag, sigma_off):
    along_east = sigma_diag[0]
    along_north = sigma_diag[1]
    along_depth = sigma_diag[2]
    return jnp.stack([along_east, along_north, along_depth, sigma_off[0] * jnp.sqrt(along_east * along_north), sigma_off[1] * jnp.sqrt(along_east * along_depth), sigma_off[2] * jnp.sqrt(along_north * along_depth)])

def tensor_apply(tensor, values):
    along_one = values[0]
    along_two = values[1]
    along_three = values[2]
    return jnp.stack([tensor[0][None] * along_one + tensor[3][None] * along_two + tensor[4][None] * along_three, tensor[3][None] * along_one + tensor[1][None] * along_two + tensor[5][None] * along_three, tensor[4][None] * along_one + tensor[5][None] * along_two + tensor[2][None] * along_three])

def rotate_quarter(values):
    return jnp.stack([-values[:, 1], values[:, 0]], axis=1)

def curl_curl(values):
    edge_east = values[0]
    edge_north = values[1]
    edge_depth = values[2]
    flux_east = forward_north(edge_depth) - forward_depth(edge_north)
    flux_north = forward_depth(edge_east) - forward_east(edge_depth)
    flux_depth = forward_east(edge_north) - forward_north(edge_east)
    return jnp.stack([backward_north(flux_depth) - backward_depth(flux_north), backward_depth(flux_east) - backward_east(flux_depth), backward_east(flux_north) - backward_north(flux_east)])

def apply_operator(values, tensor):
    return curl_curl(values) + omega_shift * rotate_quarter(tensor_apply(tensor, values))

def edge_inverse(residual, tensor):
    shift_part = omega_shift * tensor[0:3][:, None]
    denominator = edge_center * edge_center + shift_part * shift_part
    real_part = (edge_center * residual[:, 0:1] + shift_part * residual[:, 1:2]) / denominator
    imag_part = (edge_center * residual[:, 1:2] - shift_part * residual[:, 0:1]) / denominator
    return jnp.concatenate([real_part, imag_part], axis=1)

def node_inverse(nodal_source, tensor):
    shift_part = nodal_shift * (tensor[0] + tensor[1] + tensor[2])
    denominator = node_center * node_center + shift_part * shift_part
    real_part = (node_center * nodal_source[0] + shift_part * nodal_source[1]) / denominator
    imag_part = (node_center * nodal_source[1] - shift_part * nodal_source[0]) / denominator
    return jnp.stack([real_part, imag_part])

def gradient(nodal_values):
    return jnp.stack([forward_east(nodal_values), forward_north(nodal_values), forward_depth(nodal_values)])

def divergence(values):
    return backward_east(values[0]) + backward_north(values[1]) + backward_depth(values[2])

def nodal_operator(nodal_values, tensor):
    slopes = gradient(nodal_values)
    return divergence(slopes + omega_shift * rotate_quarter(tensor_apply(tensor, slopes)))

def precondition(vector, tensor):
    first_pass = edge_first * edge_inverse(vector, tensor)
    remainder = vector - apply_operator(first_pass, tensor)
    correction = edge_inverse(remainder, tensor)
    smoothed = first_pass + edge_second * correction
    leftover = remainder - edge_second * apply_operator(correction, tensor)
    nodal_source = divergence(leftover)
    coarse = node_first * node_inverse(nodal_source, tensor)
    coarse = coarse + node_second * node_inverse(nodal_source - nodal_operator(coarse, tensor), tensor)
    return smoothed + gradient(coarse)

def least_squares(hessenberg, initial_norm):
    gram_matrix = jnp.dot(hessenberg.T, hessenberg, precision=lax.Precision.HIGHEST)
    target = initial_norm * hessenberg[0]
    factor = jnp.linalg.cholesky(gram_matrix)
    extent = hessenberg.shape[1]
    middle = []
    for position in range(extent):
        partial_value = target[position]
        for earlier in range(position):
            partial_value = partial_value - factor[position, earlier] * middle[earlier]
        middle.append(partial_value / factor[position, position])
    weights = list(middle)
    for position in range(extent - 1, -1, -1):
        partial_value = middle[position]
        for later_index in range(position + 1, extent):
            partial_value = partial_value - factor[later_index, position] * weights[later_index]
        weights[position] = partial_value / factor[position, position]
    return weights

def reference(right_side, materials, sigma_diag, sigma_off):
    material_table = tensor_table(sigma_diag, sigma_off)
    cell_tensor = material_table[:, materials]
    shifted_east = jnp.roll(cell_tensor, -1, axis=-1)
    edge_tensor = 0.25 * (cell_tensor + shifted_east + jnp.roll(cell_tensor, -1, axis=-2) + jnp.roll(shifted_east, -1, axis=-2))
    initial_norm = jnp.sqrt(jnp.sum(right_side * right_side) + epsilon)
    krylov = [right_side / initial_norm]
    updates = []
    hessenberg = jnp.zeros((ITERS + 1, ITERS), jnp.float32)
    for column in range(ITERS):
        update = precondition(krylov[column], edge_tensor)
        updates.append(update)
        applied = apply_operator(update, edge_tensor)
        factors = []
        for earlier in range(column + 1):
            factors.append(jnp.sum(krylov[earlier] * applied))
        for earlier in range(column + 1):
            applied = applied - factors[earlier] * krylov[earlier]
            hessenberg = hessenberg.at[earlier, column].set(factors[earlier])
        height = jnp.sqrt(jnp.sum(applied * applied) + epsilon)
        hessenberg = hessenberg.at[column + 1, column].set(height)
        if column + 1 < ITERS:
            krylov.append(applied / height)
    weights = least_squares(hessenberg, initial_norm)
    solution = weights[0] * updates[0]
    for column in range(1, ITERS):
        solution = solution + weights[column] * updates[column]
    return (solution, hessenberg)
```

```python
import jax
import jax.numpy as jnp
from jax import lax
from jax.experimental import pallas as pl
from jax.experimental.pallas import tpu as pltpu
from jax.sharding import PartitionSpec as P

epsilon = 1e-06
LANES = 128
SUBS = 8
REACH = 4
HALO = 2 * REACH
ROWS = SUBS + 2 * HALO
STRIP = 16
VMEM_LIMIT = 56 * 2**20


class Field:
    def __init__(self, parts):
        self.parts = tuple(parts)

    def zip(self, other, op):
        if isinstance(other, Field):
            return Field(op(a, b) for a, b in zip(self.parts, other.parts))
        return Field(op(a, other) for a in self.parts)

    def __add__(self, other):
        return self.zip(other, lambda a, b: a + b)

    def __sub__(self, other):
        return self.zip(other, lambda a, b: a - b)

    def __mul__(self, other):
        return self.zip(other, lambda a, b: a * b)

    __rmul__ = __mul__

    def __rtruediv__(self, top):
        return Field(top / a for a in self.parts)


class Shifts:
    def __init__(self):
        lane = lax.broadcasted_iota(jnp.int32, (SUBS, LANES), 1)
        sub = lax.broadcasted_iota(jnp.int32, (SUBS, LANES), 0)
        self.first_lane = lane == 0
        self.last_lane = lane == LANES - 1
        self.first_sub = sub == 0
        self.last_sub = sub == SUBS - 1

    def east(self, field):
        r = [pltpu.roll(t, LANES - 1, 1) for t in field.parts]
        return Field(jnp.where(self.last_lane, r[k ^ 1], r[k]) for k in range(4))

    def west(self, field):
        r = [pltpu.roll(t, 1, 1) for t in field.parts]
        return Field(jnp.where(self.first_lane, r[k ^ 1], r[k]) for k in range(4))

    def above(self, field):
        r = [pltpu.roll(t, SUBS - 1, 0) for t in field.parts]
        low = [jnp.where(self.last_sub, r[2 + k], r[k]) for k in range(2)]
        return Field(low + [jnp.where(self.last_sub, 0.0, r[2 + k]) for k in range(2)])

    def below(self, field):
        r = [pltpu.roll(t, 1, 0) for t in field.parts]
        low = [jnp.where(self.first_sub, 0.0, r[k]) for k in range(2)]
        return Field(low + [jnp.where(self.first_sub, r[k], r[2 + k]) for k in range(2)])


def get(ref, row, c):
    return Field(ref[row, c, k] for k in range(4))


def put(ref, row, c, field):
    for k in range(4):
        ref[row, c, k] = field.parts[k]


def loop(start, stop, body):
    lax.fori_loop(start, stop, lambda i, c: (body(i), c)[1], 0)


def pack_kernel(rhs_ref, mat_ref, out_ref):
    for y in range(SUBS):
        for z in range(2):
            rows = pl.ds(z * 64 + y, SUBS, stride=SUBS)
            for c in range(6):
                out_ref[y, c, z] = rhs_ref[c, rows, :]
            out_ref[y, 6, z] = mat_ref[rows, :].astype(jnp.float32)


def strip_kernel(low_ref, own_ref, high_ref, last_ref, left_ref, right_ref):
    lane = lax.broadcasted_iota(jnp.int32, (SUBS, LANES), 1)
    for group, ref in enumerate((low_ref, own_ref, high_ref)):

        def channel(c, ref=ref, group=group):
            for z in range(2):
                left = ref[0, c, z]
                right = pltpu.roll(left, STRIP, 1)
                for r in range(1, SUBS):
                    tile = ref[r, c, z]
                    here = (lane >= STRIP * r) & (lane < STRIP * (r + 1))
                    left = jnp.where(here, pltpu.roll(tile, STRIP * r, 1), left)
                    right = jnp.where(here, pltpu.roll(tile, (STRIP * (r + 1)) % LANES, 1), right)
                left_ref[group * 7 + c, z] = left
                right_ref[group * 7 + c, z] = right

        loop(0, 7, channel)
    for z in range(2):
        left_ref[21, z] = last_ref[z]
        right_ref[21, z] = pltpu.roll(last_ref[z], STRIP, 1)


def iterate(sh, v, out, u, s2, coef, z1, t1, p, node, flux, a, b):
    def fluxes(e, above_row):
        bx = (above_row[1] - e[2]) - (sh.above(e[1]) - e[1])
        by = (sh.above(e[0]) - e[0]) - (sh.east(e[2]) - e[2])
        bz = (sh.east(e[1]) - e[1]) - (above_row[0] - e[0])
        return bx, by, bz

    def curl(row, e, e_next):
        result = []
        for part in range(2):
            here = [e[2 * c + part] for c in range(3)]
            bx, by, bz = fluxes(here, (e_next[part], e_next[4 + part]))
            pbx, pbz = get(flux, row, 2 * part), get(flux, row, 2 * part + 1)
            put(flux, row + 1, 2 * part, bx)
            put(flux, row + 1, 2 * part + 1, bz)
            result.append(
                (
                    (pbz - bz) - (sh.below(by) - by),
                    (sh.below(bx) - bx) - (sh.west(bz) - bz),
                    (sh.west(by) - by) - (pbx - bx),
                )
            )
        return [result[k % 2][k // 2] for k in range(6)]

    def tensor(row, e):
        s = [get(s2, row, c) for c in range(6)]
        return [
            s[0] * e[0] + s[3] * e[1] + s[4] * e[2],
            s[3] * e[0] + s[1] * e[1] + s[5] * e[2],
            s[4] * e[0] + s[5] * e[1] + s[2] * e[2],
        ]

    def operator(row, e, e_next):
        k = curl(row, e, e_next)
        si = tensor(row, e[1::2])
        sr = tensor(row, e[0::2])
        return [k[j] - si[j // 2] if j % 2 == 0 else k[j] + sr[j // 2] for j in range(6)]

    def jacobi(row, e, scale):
        result = []
        for c in range(3):
            alpha, beta = get(coef, row, c), get(coef, row, 3 + c)
            result.append(scale * (alpha * e[2 * c] + beta * e[2 * c + 1]))
            result.append(scale * (alpha * e[2 * c + 1] - beta * e[2 * c]))
        return result

    def nodal(row, q, scale):
        alpha, beta = get(coef, row, 6), get(coef, row, 7)
        return [scale * (alpha * q[0] + beta * q[1]), scale * (alpha * q[1] - beta * q[0])]

    def load(ref, row, n=6):
        return [get(ref, row, c) for c in range(n)]

    def store(ref, row, values, base=0):
        for c, value in enumerate(values):
            put(ref, row, base + c, value)

    store(z1, a, jacobi(a, load(v, a), 0.7))

    def first(y):
        ahead = jacobi(y + 1, load(v, y + 1), 0.7)
        store(z1, y + 1, ahead)
        applied = operator(y, load(z1, y), ahead)
        rest = [r - w for r, w in zip(load(v, y), applied)]
        store(t1, y, rest)
        store(p, y, jacobi(y, rest, 0.6))

    loop(a, b - 1, first)

    def second(y):
        applied = operator(y, load(p, y), load(p, y + 1))
        rest = [r - w for r, w in zip(load(t1, y), applied)]
        source = []
        for part in range(2):
            x, n, d = rest[part], rest[2 + part], rest[4 + part]
            before = get(node, y, 6 + part)
            put(node, y + 1, 6 + part, n)
            source.append(((sh.west(x) - x) + (before - n)) + (sh.below(d) - d))
        store(node, y, source)
        store(node, y, nodal(y, source, 0.8), 2)

    loop(a + 1, b - 2, second)

    def third(y):
        w = [get(node, y, 2 + part) for part in range(2)]
        slopes = []
        for part in range(2):
            ahead = get(node, y + 1, 2 + part)
            slopes.append((sh.east(w[part]) - w[part], ahead - w[part], sh.above(w[part]) - w[part]))
        si = tensor(y, slopes[1])
        sr = tensor(y, slopes[0])
        rest = []
        for part in range(2):
            if part == 0:
                x, n, d = [g - s for g, s in zip(slopes[0], si)]
            else:
                x, n, d = [g + s for g, s in zip(slopes[1], sr)]
            before = get(node, y, 6 + part)
            put(node, y + 1, 6 + part, n)
            applied = ((sh.west(x) - x) + (before - n)) + (sh.below(d) - d)
            rest.append(get(node, y, part) - applied)
        fix = nodal(y, rest, 0.5)
        store(node, y, [w[part] + fix[part] for part in range(2)], 4)

    loop(a + 2, b - 3, third)

    def lift(y):
        w = [get(node, y, 4 + part) for part in range(2)]
        result = []
        for c in range(3):
            for part in range(2):
                k = 2 * c + part
                if c == 0:
                    slope = sh.east(w[part]) - w[part]
                elif c == 1:
                    slope = get(node, y + 1, 4 + part) - w[part]
                else:
                    slope = sh.above(w[part]) - w[part]
                result.append((get(z1, y, k) + get(p, y, k)) + slope)
        store(u, y, result)
        return result

    lift(a + 3)

    def fourth(y):
        ahead = lift(y + 1)
        store(out, y, operator(y, load(u, y), ahead))

    loop(a + 3, b - 4, fourth)


def two_sum(a, b):
    s = a + b
    t = s - a
    return s, (a - (s - t)) + (b - t)


def main_kernel(
    low_ref, own_ref, high_ref, last_ref, left_ref, right_ref, table_ref,
    a0_ref, a1_ref, sums_ref,
    v, c0, c1, u0, u1, mat, pair, s2, coef, z1, t1, p, node, flux,
):
    sh = Shifts()
    lane = lax.broadcasted_iota(jnp.int32, (SUBS, LANES), 1)
    near = lane < LANES // 2

    def halo(strip, z, r):
        east = pltpu.roll(right_ref[strip, z], lax.rem(LANES - STRIP * r, LANES), 1)
        west = pltpu.roll(left_ref[strip, z], lax.rem(2 * LANES - STRIP - STRIP * r, LANES), 1)
        return jnp.where(near, east, west)

    for group, ref in enumerate((low_ref, own_ref, high_ref)):

        def unpack(r, ref=ref, group=group):
            y = group * SUBS + r
            for z in range(2):
                for c in range(6):
                    v[y, c, 2 * z] = ref[r, c, z]
                    v[y, c, 2 * z + 1] = halo(group * 7 + c, z, r)
                mat[y, 2 * z] = ref[r, 6, z]
                mat[y, 2 * z + 1] = halo(group * 7 + 6, z, r)

        loop(0, SUBS, unpack)
    for z in range(2):
        mat[ROWS, 2 * z] = last_ref[z]
        mat[ROWS, 2 * z + 1] = halo(21, z, 0)

    def pairs(y):
        ids = [mat[y, k].astype(jnp.int32) for k in range(4)]
        for c in range(6):
            cell = Field(jnp.take_along_axis(table_ref[c], i, axis=1) for i in ids)
            put(pair, y, c, cell + sh.east(cell))

    loop(0, ROWS + 1, pairs)

    def tensors(y):
        s = [get(pair, y, c) + get(pair, y + 1, c) for c in range(6)]
        for c in range(6):
            put(s2, y, c, s[c])
        for c in range(3):
            inverse = 1.0 / (s[c] * s[c] + 16.0)
            put(coef, y, c, 4.0 * inverse)
            put(coef, y, 3 + c, s[c] * inverse)
        shift = 2.0 * ((s[0] + s[1]) + s[2])
        inverse = 1.0 / (shift * shift + 36.0)
        put(coef, y, 6, 6.0 * inverse)
        put(coef, y, 7, shift * inverse)

    loop(0, ROWS, tensors)

    iterate(sh, v, c0, u0, s2, coef, z1, t1, p, node, flux, 0, ROWS)
    iterate(sh, c0, c1, u1, s2, coef, z1, t1, p, node, flux, REACH, ROWS - REACH)

    def dots(r, sums):
        y = HALO + r
        sums = list(sums)
        for c in range(6):
            for z in range(2):
                a0_ref[r, c, z] = u0[y, c, 2 * z]
                a1_ref[r, c, z] = u1[y, c, 2 * z]
                f, g, h = v[y, c, 2 * z], c0[y, c, 2 * z], c1[y, c, 2 * z]
                for k, term in enumerate((f * f, f * g, g * g, f * h, g * h, h * h)):
                    sums[k] = sums[k] + term
        return tuple(sums)

    zero = jnp.zeros((SUBS, LANES), jnp.float32)
    sums = lax.fori_loop(0, SUBS, dots, (zero,) * 6)
    row = zero
    for k, total in enumerate(sums):
        rest = zero
        for axis, size in ((0, SUBS), (1, LANES)):
            step = size // 2
            while step:
                total, error = two_sum(total, pltpu.roll(total, step, axis))
                rest = rest + pltpu.roll(rest, step, axis) + error
                step //= 2
        row = jnp.where(lane == k, total, row)
        row = jnp.where(lane == 6 + k, rest, row)
    for k in range(16):
        sums_ref[pl.ds(k * SUBS, SUBS), :] = row


def two_product(a, b):
    def split(x):
        t = 4097.0 * x
        high = t - (t - x)
        return high, x - high

    p = a * b
    ah, al = split(a)
    bh, bl = split(b)
    return p, ((ah * bh - p) + ah * bl + al * bh) + al * bl


def quick(s, e):
    t = s + e
    return t, e - (t - s)


def plus(x, y):
    s, e = two_sum(x[0], y[0])
    return quick(s, e + (x[1] + y[1]))


def minus(x, y):
    return plus(x, (-y[0], -y[1]))


def times(x, y):
    p, e = two_product(x[0], y[0])
    return quick(p, e + (x[0] * y[1] + x[1] * y[0]))


def scaled(x, factor):
    p, e = two_product(x[0], jnp.full_like(x[0], factor))
    return quick(p, e + x[1] * factor)


def over(x, y):
    q = x[0] / y[0]
    r = minus(x, times(y, (q, jnp.zeros_like(q))))
    return quick(q, (r[0] + r[1]) / y[0])


def final_kernel(sums_ref, a0_ref, a1_ref, out_ref, hess_ref):
    lane = lax.broadcasted_iota(jnp.int32, (SUBS, LANES), 1)
    sub = lax.broadcasted_iota(jnp.int32, (SUBS, LANES), 0)
    total = sums_ref[pl.ds(0, SUBS), :]
    rest = jnp.zeros_like(total)
    for k in range(1, 16):
        total, error = two_sum(total, sums_ref[pl.ds(k * SUBS, SUBS), :])
        rest = rest + error
    for step in (4, 2, 1):
        total, error = two_sum(total, pltpu.roll(total, step, 0))
        rest = rest + pltpu.roll(rest, step, 0) + error
    rest = rest + pltpu.roll(total, LANES - 6, 1)

    def pick(values, k):
        one = jnp.sum(jnp.where(lane == k, values, 0.0), axis=1, keepdims=True)
        return jnp.broadcast_to(one, (SUBS, LANES))

    bb, bc, cc, bd, cd, dd = [quick(pick(total, k), pick(rest, k)) for k in range(6)]
    eps = (jnp.full((SUBS, LANES), epsilon, jnp.float32), jnp.zeros((SUBS, LANES), jnp.float32))
    beta2 = plus(bb, eps)
    h00 = over(bc, beta2)
    norm1 = minus(minus(cc, times(h00, bc)), times(eps, times(h00, h00)))
    norm1 = (jnp.maximum(norm1[0], 0.0), jnp.where(norm1[0] > 0.0, norm1[1], 0.0))
    tall = plus(norm1, times(eps, beta2))
    x = minus(bd, times(h00, bc))
    y = plus(minus(minus(cd, times(h00, cc)), times(h00, bd)), times(times(h00, h00), bc))
    x_over = over(x, beta2)
    y_over = over(y, tall)
    norm2 = plus(minus(dd, scaled(times(h00, cd), 2.0)), times(times(h00, h00), cc))
    norm2 = minus(norm2, plus(times(x, x_over), times(eps, times(x_over, x_over))))
    norm2 = minus(norm2, plus(times(y, y_over), times(times(eps, beta2), times(y_over, y_over))))
    norm2 = plus(norm2, scaled(times(times(x_over, y_over), times(eps, h00)), 2.0))
    norm2 = over(norm2, tall)

    beta = jnp.sqrt(beta2[0])
    e00 = h00[0]
    e10 = jnp.sqrt(tall[0] / beta2[0])
    e01 = x_over[0] / e10
    e11 = y_over[0]
    e21 = jnp.sqrt(jnp.maximum(norm2[0], 0.0) + epsilon)

    g00 = e00 * e00 + e10 * e10
    g01 = e00 * e01 + e10 * e11
    g11 = e01 * e01 + e11 * e11 + e21 * e21
    l00 = jnp.sqrt(g00)
    l10 = g01 / l00
    l11 = jnp.sqrt(g11 - l10 * l10)
    m0 = beta * e00 / l00
    m1 = (beta * e01 - l10 * m0) / l11
    y1 = m1 / l11
    y0 = (m0 - l10 * y1) / l00
    k0 = (y0 - y1 * e00 / e10) / beta
    k1 = y1 / (e10 * beta)

    table = jnp.where(sub == 0, jnp.where(lane == 0, e00, e01), jnp.where(lane == 0, e10, e11))
    table = jnp.where(sub == 2, jnp.where(lane == 0, 0.0, e21), table)
    hess_ref[...] = table[:3, :2]
    for row in range(SUBS):
        for z in range(2):
            rows = pl.ds(z * 64 + row, SUBS, stride=SUBS)
            for c in range(6):
                out_ref[c, rows, :] = k0 * a0_ref[row, c, z] + k1 * a1_ref[row, c, z]


def tensor_table(sigma_diag, sigma_off):
    along_east = sigma_diag[0]
    along_north = sigma_diag[1]
    along_depth = sigma_diag[2]
    return jnp.stack(
        [
            along_east,
            along_north,
            along_depth,
            sigma_off[0] * jnp.sqrt(along_east * along_north),
            sigma_off[1] * jnp.sqrt(along_east * along_depth),
            sigma_off[2] * jnp.sqrt(along_north * along_depth),
        ]
    )


def call(kernel, outs, scratch=(), n=0):
    vmem = pl.BlockSpec(memory_space=pltpu.VMEM)
    return pl.pallas_call(
        kernel,
        out_shape=[jax.ShapeDtypeStruct(s, jnp.float32) for s in outs],
        in_specs=[vmem] * n,
        out_specs=[vmem] * len(outs),
        scratch_shapes=[pltpu.VMEM(s, jnp.float32) for s in scratch],
        compiler_params=pltpu.CompilerParams(vmem_limit_bytes=VMEM_LIMIT),
    )


def moved(value, axis, step):
    size = lax.axis_size(axis)
    return lax.ppermute(value, axis, [(i, (i + step) % size) for i in range(size)])


def on_device(right_side, materials, sigma_diag, sigma_off):
    table = jnp.pad(0.5 * tensor_table(sigma_diag, sigma_off), ((0, 0), (0, LANES - 8)))
    table = jnp.broadcast_to(table[:, None, :], (6, SUBS, LANES))
    tile = (SUBS, LANES)
    (own,) = call(pack_kernel, [(SUBS, 7, 2) + tile], n=2)(
        right_side.reshape(6, LANES, LANES), materials.reshape(LANES, LANES)
    )
    low = moved(own, "gy", 1)
    high = moved(own, "gy", -1)
    last = moved(own[0, 6], "gy", -2)
    to_left, to_right = call(strip_kernel, [(22, 2) + tile] * 2, n=4)(low, own, high, last)
    from_right = moved(to_left, "gx", -1)
    from_left = moved(to_right, "gx", 1)

    def rows(n, extra=0):
        return (ROWS + extra, n, 4) + tile

    a0, a1, sums = call(
        main_kernel,
        [(SUBS, 6, 2) + tile, (SUBS, 6, 2) + tile, (LANES, LANES)],
        [rows(6)] * 5
        + [(ROWS + 1, 4) + tile, rows(6, 1), rows(6), rows(8)]
        + [rows(6)] * 3
        + [rows(8, 1), rows(4, 1)],
        n=7,
    )(low, own, high, last, from_left, from_right, table)
    gathered = lax.all_to_all(sums, ("gx", "gy"), 0, 0, tiled=True)
    solution_rows, hessenberg = call(final_kernel, [(6, LANES, LANES), (3, 2)], n=3)(gathered, a0, a1)
    return solution_rows.reshape(right_side.shape), hessenberg


def solution(mesh):
    return jax.shard_map(
        on_device,
        mesh=mesh,
        in_specs=(P(None, None, None, "gy", "gx"), P(None, "gy", "gx"), P(), P()),
        out_specs=(P(None, None, None, "gy", "gx"), P()),
        check_vma=False,
    )
```

```python
import jax
import jax.numpy as jnp
from jax import lax
from jax.experimental import pallas as pl
from jax.experimental.pallas import tpu as pltpu
from jax.sharding import PartitionSpec as P

epsilon = 1e-06
LANES = 128
SUBS = 8
REACH = 4
HALO = 2 * REACH
ROWS = SUBS + 2 * HALO
STRIP = 16
JOINED = 14
VMEM_LIMIT = 56 * 2**20


class Field:
    def __init__(self, parts):
        self.parts = tuple(parts)

    def zip(self, other, op):
        if isinstance(other, Field):
            return Field(op(a, b) for a, b in zip(self.parts, other.parts))
        return Field(op(a, other) for a in self.parts)

    def __add__(self, other):
        return self.zip(other, lambda a, b: a + b)

    def __sub__(self, other):
        return self.zip(other, lambda a, b: a - b)

    def __mul__(self, other):
        return self.zip(other, lambda a, b: a * b)

    __rmul__ = __mul__

    def __rtruediv__(self, top):
        return Field(top / a for a in self.parts)


class Shifts:
    def __init__(self):
        lane = lax.broadcasted_iota(jnp.int32, (SUBS, LANES), 1)
        sub = lax.broadcasted_iota(jnp.int32, (SUBS, LANES), 0)
        self.first_lane = lane == 0
        self.last_lane = lane == LANES - 1
        self.first_sub = sub == 0
        self.last_sub = sub == SUBS - 1

    def east(self, field):
        r = [pltpu.roll(t, LANES - 1, 1) for t in field.parts]
        return Field(jnp.where(self.last_lane, r[k ^ 1], r[k]) for k in range(4))

    def west(self, field):
        r = [pltpu.roll(t, 1, 1) for t in field.parts]
        return Field(jnp.where(self.first_lane, r[k ^ 1], r[k]) for k in range(4))

    def above(self, field):
        r = [pltpu.roll(t, SUBS - 1, 0) for t in field.parts]
        low = [jnp.where(self.last_sub, r[2 + k], r[k]) for k in range(2)]
        return Field(low + [jnp.where(self.last_sub, 0.0, r[2 + k]) for k in range(2)])

    def below(self, field):
        r = [pltpu.roll(t, 1, 0) for t in field.parts]
        low = [jnp.where(self.first_sub, 0.0, r[k]) for k in range(2)]
        return Field(low + [jnp.where(self.first_sub, r[k], r[2 + k]) for k in range(2)])


def get(ref, row, c):
    return Field(ref[row, c, k] for k in range(4))


def put(ref, row, c, field):
    for k in range(4):
        ref[row, c, k] = field.parts[k]


def loop(start, stop, body):
    lax.fori_loop(start, stop, lambda i, c: (body(i), c)[1], 0)


def depth_rows(y, z):
    return pl.ds(z * SUBS * SUBS + y, SUBS, stride=SUBS)


def strip_kernel(rhs_ref, mat_ref, diag_ref, off_ref, left_ref, right_ref, own_mat_ref, table_ref):
    lane = lax.broadcasted_iota(jnp.int32, (SUBS, LANES), 1)
    for z in range(2):
        for r in range(SUBS):
            own_mat_ref[r, z] = mat_ref[depth_rows(r, z), :].astype(jnp.float32)
    for c in range(7):
        for z in range(2):
            for r in range(SUBS):
                tile = own_mat_ref[r, z] if c == 6 else rhs_ref[c, depth_rows(r, z), :]
                west = pltpu.roll(tile, STRIP * r, 1) if r else tile
                east = pltpu.roll(tile, STRIP * (r + 1), 1) if r < SUBS - 1 else tile
                if r == 0:
                    left, right = west, east
                else:
                    here = lane >= STRIP * r
                    left, right = jnp.where(here, west, left), jnp.where(here, east, right)
            left_ref[c, z] = left
            right_ref[c, z] = right
    x, n, d = [jnp.broadcast_to(0.5 * diag_ref[c : c + 1, :], (SUBS, SUBS)) for c in range(3)]
    entries = [x, n, d]
    for c, (f, g) in enumerate(((x, n), (x, d), (n, d))):
        entries.append(jnp.broadcast_to(off_ref[c : c + 1, :], (SUBS, SUBS)) * jnp.sqrt(f * g))
    for c in range(6):
        table_ref[c, :, :] = jnp.zeros((SUBS, LANES), jnp.float32)
        table_ref[c, :, :SUBS] = entries[c]


def wavefront(stages):
    edges = sorted({e + lag for _, start, stop, lag in stages for e in (start, stop)})
    for start, stop in zip(edges, edges[1:]):
        active = [st for st in stages if st[1] + st[3] <= start and stop <= st[2] + st[3]]

        def step(s, active=active):
            for body, _, _, lag in reversed(active):
                body(s - lag)

        loop(start, stop, step)


def iterate(sh, v, out, u, s2, coef, z1, t1, p, node, flux, a, b):
    def fluxes(e, above_row):
        bx = (above_row[1] - e[2]) - (sh.above(e[1]) - e[1])
        by = (sh.above(e[0]) - e[0]) - (sh.east(e[2]) - e[2])
        bz = (sh.east(e[1]) - e[1]) - (above_row[0] - e[0])
        return bx, by, bz

    def curl(row, e, e_next):
        result = []
        for part in range(2):
            here = [e[2 * c + part] for c in range(3)]
            bx, by, bz = fluxes(here, (e_next[part], e_next[4 + part]))
            pbx, pbz = get(flux, row, 2 * part), get(flux, row, 2 * part + 1)
            put(flux, row + 1, 2 * part, bx)
            put(flux, row + 1, 2 * part + 1, bz)
            result.append(
                (
                    (pbz - bz) - (sh.below(by) - by),
                    (sh.below(bx) - bx) - (sh.west(bz) - bz),
                    (sh.west(by) - by) - (pbx - bx),
                )
            )
        return [result[k % 2][k // 2] for k in range(6)]

    def tensor(row, e):
        s = [get(s2, row, c) for c in range(6)]
        return [
            s[0] * e[0] + s[3] * e[1] + s[4] * e[2],
            s[3] * e[0] + s[1] * e[1] + s[5] * e[2],
            s[4] * e[0] + s[5] * e[1] + s[2] * e[2],
        ]

    def operator(row, e, e_next):
        k = curl(row, e, e_next)
        si = tensor(row, e[1::2])
        sr = tensor(row, e[0::2])
        return [k[j] - si[j // 2] if j % 2 == 0 else k[j] + sr[j // 2] for j in range(6)]

    def jacobi(row, e, scale):
        result = []
        for c in range(3):
            alpha, beta = get(coef, row, c), get(coef, row, 3 + c)
            result.append(scale * (alpha * e[2 * c] + beta * e[2 * c + 1]))
            result.append(scale * (alpha * e[2 * c + 1] - beta * e[2 * c]))
        return result

    def nodal(row, q, scale):
        alpha, beta = get(coef, row, 6), get(coef, row, 7)
        return [scale * (alpha * q[0] + beta * q[1]), scale * (alpha * q[1] - beta * q[0])]

    def load(ref, row, n=6):
        return [get(ref, row, c) for c in range(n)]

    def store(ref, row, values, base=0):
        for c, value in enumerate(values):
            put(ref, row, base + c, value)

    def zeroth(y):
        store(z1, y, jacobi(y, load(v, y), 0.7))

    def first(y):
        ahead = jacobi(y + 1, load(v, y + 1), 0.7)
        store(z1, y + 1, ahead)
        applied = operator(y, load(z1, y), ahead)
        rest = [r - w for r, w in zip(load(v, y), applied)]
        store(t1, y, rest)
        store(p, y, jacobi(y, rest, 0.6))

    def second(y):
        applied = operator(y, load(p, y), load(p, y + 1))
        rest = [r - w for r, w in zip(load(t1, y), applied)]
        source = []
        for part in range(2):
            x, n, d = rest[part], rest[2 + part], rest[4 + part]
            before = get(node, y, 6 + part)
            put(node, y + 1, 6 + part, n)
            source.append(((sh.west(x) - x) + (before - n)) + (sh.below(d) - d))
        store(node, y, source)
        store(node, y, nodal(y, source, 0.8), 2)

    def third(y):
        w = [get(node, y, 2 + part) for part in range(2)]
        slopes = []
        for part in range(2):
            ahead = get(node, y + 1, 2 + part)
            slopes.append((sh.east(w[part]) - w[part], ahead - w[part], sh.above(w[part]) - w[part]))
        si = tensor(y, slopes[1])
        sr = tensor(y, slopes[0])
        rest = []
        for part in range(2):
            if part == 0:
                x, n, d = [g - s for g, s in zip(slopes[0], si)]
            else:
                x, n, d = [g + s for g, s in zip(slopes[1], sr)]
            before = get(node, y, 6 + part)
            put(node, y + 1, 6 + part, n)
            applied = ((sh.west(x) - x) + (before - n)) + (sh.below(d) - d)
            rest.append(get(node, y, part) - applied)
        fix = nodal(y, rest, 0.5)
        store(node, y, [w[part] + fix[part] for part in range(2)], 4)

    def lift(y):
        w = [get(node, y, 4 + part) for part in range(2)]
        result = []
        for c in range(3):
            for part in range(2):
                k = 2 * c + part
                if c == 0:
                    slope = sh.east(w[part]) - w[part]
                elif c == 1:
                    slope = get(node, y + 1, 4 + part) - w[part]
                else:
                    slope = sh.above(w[part]) - w[part]
                result.append((get(z1, y, k) + get(p, y, k)) + slope)
        store(u, y, result)
        return result

    def fourth(y):
        ahead = lift(y + 1)
        store(out, y, operator(y, load(u, y), ahead))

    return [
        (zeroth, a, a + 1, 0),
        (first, a, b - 1, 1),
        (second, a + 1, b - 2, 3),
        (third, a + 2, b - 3, 5),
        (lift, a + 3, a + 4, 7),
        (fourth, a + 3, b - 4, 8),
    ]


def two_sum(a, b):
    s = a + b
    t = s - a
    return s, (a - (s - t)) + (b - t)


def main_kernel(
    low_ref, own_ref, high_ref, near_low_ref, near_high_ref, last_ref, left_ref, right_ref, own_mat_ref, table_ref,
    a0_ref, a1_ref, sums_ref,
    v, c0, c1, u0, u1, mat, pair, s2, coef, z1, t1, p, node, flux,
):
    sh = Shifts()
    lane = lax.broadcasted_iota(jnp.int32, (SUBS, LANES), 1)
    near = lane < LANES // 2

    def halo(left, right, r):
        east = pltpu.roll(right, lax.rem(LANES - STRIP * r, LANES), 1)
        west = pltpu.roll(left, lax.rem(2 * LANES - STRIP - STRIP * r, LANES), 1)
        return jnp.where(near, east, west)

    def unpack(group, rhs, strips, cells):
        def body(y):
            r = y - group * SUBS
            for z in range(2):
                for c in range(6):
                    v[y, c, 2 * z] = rhs[c, depth_rows(r, z), :]
                    v[y, c, 2 * z + 1] = halo(*strips(c, z), r)
                mat[y, 2 * z] = cells(r, z)
                mat[y, 2 * z + 1] = halo(*strips(6, z), r)

        return (body, group * SUBS, group * SUBS + SUBS, 0)

    def own_strips(c, z):
        return left_ref[c, z], right_ref[c, z]

    def strips_of(ref):
        return lambda c, z: (ref[2 * c + z], ref[JOINED + 2 * c + z])

    def cells_of(ref):
        return lambda r, z: ref[2 * JOINED + 2 * r + z]

    def beyond(y):
        for z in range(2):
            mat[y, 2 * z] = last_ref[4 + z]
            mat[y, 2 * z + 1] = halo(last_ref[z], last_ref[2 + z], 0)

    def pairs(y):
        ids = [mat[y, k].astype(jnp.int32) for k in range(4)]
        for c in range(6):
            cell = Field(jnp.take_along_axis(table_ref[c], i, axis=1) for i in ids)
            put(pair, y, c, cell + sh.east(cell))

    def tensors(y):
        s = [get(pair, y, c) + get(pair, y + 1, c) for c in range(6)]
        for c in range(6):
            put(s2, y, c, s[c])
        for c in range(3):
            inverse = 1.0 / (s[c] * s[c] + 16.0)
            put(coef, y, c, 4.0 * inverse)
            put(coef, y, 3 + c, s[c] * inverse)
        shift = 2.0 * ((s[0] + s[1]) + s[2])
        inverse = 1.0 / (shift * shift + 36.0)
        put(coef, y, 6, 6.0 * inverse)
        put(coef, y, 7, shift * inverse)

    wavefront(
        [
            unpack(0, low_ref, strips_of(near_low_ref), cells_of(near_low_ref)),
            unpack(1, own_ref, own_strips, lambda r, z: own_mat_ref[r, z]),
            unpack(2, high_ref, strips_of(near_high_ref), cells_of(near_high_ref)),
            (beyond, ROWS, ROWS + 1, 0),
            (pairs, 0, ROWS + 1, 1),
            (tensors, 0, ROWS, 3),
        ]
    )
    wavefront(iterate(sh, v, c0, u0, s2, coef, z1, t1, p, node, flux, 0, ROWS))
    wavefront(iterate(sh, c0, c1, u1, s2, coef, z1, t1, p, node, flux, REACH, ROWS - REACH))

    def dots(r, sums):
        y = HALO + r
        sums = list(sums)
        for c in range(6):
            for z in range(2):
                a0_ref[r, c, z] = u0[y, c, 2 * z]
                a1_ref[r, c, z] = u1[y, c, 2 * z]
                f, g, h = v[y, c, 2 * z], c0[y, c, 2 * z], c1[y, c, 2 * z]
                for k, term in enumerate((f * f, f * g, g * g, f * h, g * h, h * h)):
                    sums[k] = sums[k] + term
        return tuple(sums)

    zero = jnp.zeros((SUBS, LANES), jnp.float32)
    sums = lax.fori_loop(0, SUBS, dots, (zero,) * 6)
    row = zero
    for k, total in enumerate(sums):
        rest = zero
        for axis, size in ((0, SUBS), (1, LANES)):
            step = size // 2
            while step:
                total, error = two_sum(total, pltpu.roll(total, step, axis))
                rest = rest + pltpu.roll(rest, step, axis) + error
                step //= 2
        row = jnp.where(lane == k, total, row)
        row = jnp.where(lane == 6 + k, rest, row)
    for k in range(16):
        sums_ref[pl.ds(k * SUBS, SUBS), :] = row


def two_product(a, b):
    def split(x):
        t = 4097.0 * x
        high = t - (t - x)
        return high, x - high

    p = a * b
    ah, al = split(a)
    bh, bl = split(b)
    return p, ((ah * bh - p) + ah * bl + al * bh) + al * bl


def quick(s, e):
    t = s + e
    return t, e - (t - s)


def plus(x, y):
    s, e = two_sum(x[0], y[0])
    return quick(s, e + (x[1] + y[1]))


def minus(x, y):
    return plus(x, (-y[0], -y[1]))


def times(x, y):
    p, e = two_product(x[0], y[0])
    return quick(p, e + (x[0] * y[1] + x[1] * y[0]))


def scaled(x, factor):
    p, e = two_product(x[0], jnp.full_like(x[0], factor))
    return quick(p, e + x[1] * factor)


def over(x, y):
    q = x[0] / y[0]
    r = minus(x, times(y, (q, jnp.zeros_like(q))))
    return quick(q, (r[0] + r[1]) / y[0])


def final_kernel(sums_ref, a0_ref, a1_ref, result_ref, hess_ref, out_ref, done):
    lane = lax.broadcasted_iota(jnp.int32, (SUBS, LANES), 1)
    sub = lax.broadcasted_iota(jnp.int32, (SUBS, LANES), 0)
    total = sums_ref[pl.ds(0, SUBS), :]
    rest = jnp.zeros_like(total)
    for k in range(1, 16):
        total, error = two_sum(total, sums_ref[pl.ds(k * SUBS, SUBS), :])
        rest = rest + error
    for step in (4, 2, 1):
        total, error = two_sum(total, pltpu.roll(total, step, 0))
        rest = rest + pltpu.roll(rest, step, 0) + error
    rest = rest + pltpu.roll(total, LANES - 6, 1)

    def pick(values, k):
        one = jnp.sum(jnp.where(lane == k, values, 0.0), axis=1, keepdims=True)
        return jnp.broadcast_to(one, (SUBS, LANES))

    bb, bc, cc, bd, cd, dd = [quick(pick(total, k), pick(rest, k)) for k in range(6)]
    eps = (jnp.full((SUBS, LANES), epsilon, jnp.float32), jnp.zeros((SUBS, LANES), jnp.float32))
    beta2 = plus(bb, eps)
    h00 = over(bc, beta2)
    norm1 = minus(minus(cc, times(h00, bc)), times(eps, times(h00, h00)))
    norm1 = (jnp.maximum(norm1[0], 0.0), jnp.where(norm1[0] > 0.0, norm1[1], 0.0))
    tall = plus(norm1, times(eps, beta2))
    x = minus(bd, times(h00, bc))
    y = plus(minus(minus(cd, times(h00, cc)), times(h00, bd)), times(times(h00, h00), bc))
    x_over = over(x, beta2)
    y_over = over(y, tall)
    norm2 = plus(minus(dd, scaled(times(h00, cd), 2.0)), times(times(h00, h00), cc))
    norm2 = minus(norm2, plus(times(x, x_over), times(eps, times(x_over, x_over))))
    norm2 = minus(norm2, plus(times(y, y_over), times(times(eps, beta2), times(y_over, y_over))))
    norm2 = plus(norm2, scaled(times(times(x_over, y_over), times(eps, h00)), 2.0))
    norm2 = over(norm2, tall)

    beta = jnp.sqrt(beta2[0])
    e00 = h00[0]
    e10 = jnp.sqrt(tall[0] / beta2[0])
    e01 = x_over[0] / e10
    e11 = y_over[0]
    e21 = jnp.sqrt(jnp.maximum(norm2[0], 0.0) + epsilon)

    g00 = e00 * e00 + e10 * e10
    g01 = e00 * e01 + e10 * e11
    g11 = e01 * e01 + e11 * e11 + e21 * e21
    l00 = jnp.sqrt(g00)
    l10 = g01 / l00
    l11 = jnp.sqrt(g11 - l10 * l10)
    m0 = beta * e00 / l00
    m1 = (beta * e01 - l10 * m0) / l11
    y1 = m1 / l11
    y0 = (m0 - l10 * y1) / l00
    k0 = (y0 - y1 * e00 / e10) / beta
    k1 = y1 / (e10 * beta)

    table = jnp.where(sub == 0, jnp.where(lane == 0, e00, e01), jnp.where(lane == 0, e10, e11))
    table = jnp.where(sub == 2, jnp.where(lane == 0, 0.0, e21), table)
    hess_ref[...] = table[:3, :2]
    copies = []
    for c in range(6):
        for row in range(SUBS):
            for z in range(2):
                out_ref[c, depth_rows(row, z), :] = k0 * a0_ref[row, c, z] + k1 * a1_ref[row, c, z]
        copies.append(pltpu.make_async_copy(out_ref.at[c], result_ref.at[c], done.at[c]))
        copies[-1].start()
    for copy in copies:
        copy.wait()


def call(kernel, outs, scratch=(), n=0):
    vmem = pl.BlockSpec(memory_space=pltpu.VMEM)
    return pl.pallas_call(
        kernel,
        out_shape=[jax.ShapeDtypeStruct(s, jnp.float32) for s in outs],
        in_specs=[vmem] * n,
        out_specs=[vmem] * len(outs),
        scratch_shapes=[pltpu.VMEM(s, jnp.float32) for s in scratch],
        compiler_params=pltpu.CompilerParams(vmem_limit_bytes=VMEM_LIMIT),
    )


def moved(value, axis, step):
    size = lax.axis_size(axis)
    return lax.ppermute(value, axis, [(i, (i + step) % size) for i in range(size)])


def on_device(right_side, materials, sigma_diag, sigma_off):
    tile = (SUBS, LANES)
    rhs = right_side.reshape(6, LANES, LANES)
    low = moved(rhs, "gy", 1)
    high = moved(rhs, "gy", -1)
    to_left, to_right, cells, table = call(
        strip_kernel, [(7, 2) + tile] * 2 + [(SUBS, 2) + tile, (6,) + tile], n=4
    )(rhs, materials.reshape(LANES, LANES), sigma_diag, sigma_off)
    from_right = moved(to_left, "gx", -1)
    from_left = moved(to_right, "gx", 1)
    joined = jnp.concatenate([part.reshape((-1,) + tile) for part in (from_left, from_right, cells)])
    near_low = moved(joined, "gy", 1)
    near_high = moved(joined, "gy", -1)
    first_row = jnp.concatenate(
        [joined[k : k + 2] for k in (JOINED - 2, 2 * JOINED - 2, 2 * JOINED)]
    )
    last = moved(first_row, "gy", -2)

    def rows(n, extra=0):
        return (ROWS + extra, n, 4) + tile

    a0, a1, sums = call(
        main_kernel,
        [(SUBS, 6, 2) + tile, (SUBS, 6, 2) + tile, (LANES, LANES)],
        [rows(6)] * 5
        + [(ROWS + 1, 4) + tile, rows(6, 1), rows(6), rows(8)]
        + [rows(6)] * 3
        + [rows(8, 1), rows(4, 1)],
        n=10,
    )(low, rhs, high, near_low, near_high, last, from_left, from_right, cells, table)
    gathered = lax.all_to_all(sums, ("gx", "gy"), 0, 0, tiled=True)
    vmem = pl.BlockSpec(memory_space=pltpu.VMEM)
    result, hessenberg = pl.pallas_call(
        final_kernel,
        out_shape=[
            jax.ShapeDtypeStruct((6, LANES, LANES), jnp.float32),
            jax.ShapeDtypeStruct((3, 2), jnp.float32),
        ],
        in_specs=[vmem] * 3,
        out_specs=[pl.BlockSpec(memory_space=pl.ANY), vmem],
        scratch_shapes=[pltpu.VMEM((6, LANES, LANES), jnp.float32), pltpu.SemaphoreType.DMA((6,))],
        compiler_params=pltpu.CompilerParams(vmem_limit_bytes=VMEM_LIMIT),
    )(gathered, a0, a1)
    return result.reshape(right_side.shape), hessenberg


def solution(mesh):
    return jax.shard_map(
        on_device,
        mesh=mesh,
        in_specs=(P(None, None, None, "gy", "gx"), P(None, "gy", "gx"), P(), P()),
        out_specs=(P(None, None, None, "gy", "gx"), P()),
        check_vma=False,
    )
```

```python
import jax
import jax.numpy as jnp
from jax import lax
from jax.experimental import pallas as pl
from jax.experimental.pallas import tpu as pltpu
from jax.sharding import PartitionSpec as P

epsilon = 1e-06
LANES = 128
SUBS = 8
REACH = 4
HALO = 2 * REACH
ROWS = SUBS + 2 * HALO
STRIP = 16
PACK = 32
VMEM_LIMIT = 44 * 2**20


class Field:
    def __init__(self, parts):
        self.parts = tuple(parts)

    def zip(self, other, op):
        if isinstance(other, Field):
            return Field(op(a, b) for a, b in zip(self.parts, other.parts))
        return Field(op(a, other) for a in self.parts)

    def __add__(self, other):
        return self.zip(other, lambda a, b: a + b)

    def __sub__(self, other):
        return self.zip(other, lambda a, b: a - b)

    def __mul__(self, other):
        return self.zip(other, lambda a, b: a * b)

    __rmul__ = __mul__

    def __rtruediv__(self, top):
        return Field(top / a for a in self.parts)


class Shifts:
    def __init__(self):
        lane = lax.broadcasted_iota(jnp.int32, (SUBS, LANES), 1)
        sub = lax.broadcasted_iota(jnp.int32, (SUBS, LANES), 0)
        self.first_lane = lane == 0
        self.last_lane = lane == LANES - 1
        self.first_sub = sub == 0
        self.last_sub = sub == SUBS - 1

    def east(self, field):
        r = [pltpu.roll(t, LANES - 1, 1) for t in field.parts]
        return Field(jnp.where(self.last_lane, r[k ^ 1], r[k]) for k in range(4))

    def west(self, field):
        r = [pltpu.roll(t, 1, 1) for t in field.parts]
        return Field(jnp.where(self.first_lane, r[k ^ 1], r[k]) for k in range(4))

    def above(self, field):
        r = [pltpu.roll(t, SUBS - 1, 0) for t in field.parts]
        low = [jnp.where(self.last_sub, r[2 + k], r[k]) for k in range(2)]
        return Field(low + [jnp.where(self.last_sub, 0.0, r[2 + k]) for k in range(2)])

    def below(self, field):
        r = [pltpu.roll(t, 1, 0) for t in field.parts]
        low = [jnp.where(self.first_sub, 0.0, r[k]) for k in range(2)]
        return Field(low + [jnp.where(self.first_sub, r[k], r[2 + k]) for k in range(2)])


def get(ref, row, c):
    return Field(ref[row, c, k] for k in range(4))


def put(ref, row, c, field):
    for k in range(4):
        ref[row, c, k] = field.parts[k]


def loop(start, stop, body):
    lax.fori_loop(start, stop, lambda i, c: (body(i), c)[1], 0)


def depth_rows(y, z):
    return pl.ds(z * SUBS * SUBS + y, SUBS, stride=SUBS)


def strip_kernel(rhs_ref, mat_ref, diag_ref, off_ref, strip_ref, cells_ref, table_ref):
    lane = lax.broadcasted_iota(jnp.int32, (SUBS, LANES), 1)
    half = STRIP // 2

    def packed(tiles, offset):
        result = None
        for r, tile in enumerate(tiles):
            shift = (STRIP * r + offset) % LANES
            moved_tile = pltpu.roll(tile, shift, 1) if shift else tile
            result = moved_tile if r == 0 else jnp.where(lane >= STRIP * r, moved_tile, result)
        return result

    for z in range(2):
        cells = [mat_ref[depth_rows(r, z), :].astype(jnp.float32) for r in range(SUBS)]
        for r in range(SUBS):
            cells_ref[2 * r + z] = cells[r]
        strip_ref[12 + z] = packed(cells, half)
        strip_ref[14 + z] = packed(cells, 0)
        for c in range(6):
            strip_ref[2 * c + z] = packed([rhs_ref[c, depth_rows(r, z), :] for r in range(SUBS)], half)
    x, n, d = [jnp.broadcast_to(0.5 * diag_ref[c : c + 1, :], (SUBS, SUBS)) for c in range(3)]
    entries = [x, n, d]
    for c, (f, g) in enumerate(((x, n), (x, d), (n, d))):
        entries.append(jnp.broadcast_to(off_ref[c : c + 1, :], (SUBS, SUBS)) * jnp.sqrt(f * g))
    for c in range(6):
        table_ref[c, :, :] = jnp.zeros((SUBS, LANES), jnp.float32)
        table_ref[c, :, :SUBS] = entries[c]
    for c in range(6):
        single = table_ref[c]
        table_ref[c] = jnp.take_along_axis(single, lane // SUBS, axis=1) + jnp.take_along_axis(
            single, lane % SUBS, axis=1
        )


def wavefront(stages, events=()):
    edges = {e + lag for _, start, stop, lag in stages for e in (start, stop)}
    edges = sorted(edges | {at for at, _ in events})
    for start, stop in zip(edges, edges[1:]):
        for at, body in events:
            if at == start:
                body()
        active = [st for st in stages if st[1] + st[3] <= start and stop <= st[2] + st[3]]

        def step(s, active=active):
            for body, _, _, lag in reversed(active):
                body(s - lag)

        loop(start, stop, step)


def iterate(sh, v, out, u, keep, s2, coef, z1, t1, p, node, flux, a, b):
    def fluxes(e, above_row):
        bx = (above_row[1] - e[2]) - (sh.above(e[1]) - e[1])
        by = (sh.above(e[0]) - e[0]) - (sh.east(e[2]) - e[2])
        bz = (sh.east(e[1]) - e[1]) - (above_row[0] - e[0])
        return bx, by, bz

    def curl(row, e, e_next):
        result = []
        for part in range(2):
            here = [e[2 * c + part] for c in range(3)]
            bx, by, bz = fluxes(here, (e_next[part], e_next[4 + part]))
            pbx, pbz = get(flux, row, 2 * part), get(flux, row, 2 * part + 1)
            put(flux, row + 1, 2 * part, bx)
            put(flux, row + 1, 2 * part + 1, bz)
            result.append(
                (
                    (pbz - bz) - (sh.below(by) - by),
                    (sh.below(bx) - bx) - (sh.west(bz) - bz),
                    (sh.west(by) - by) - (pbx - bx),
                )
            )
        return [result[k % 2][k // 2] for k in range(6)]

    def tensor(row, e):
        s = [get(s2, row, c) for c in range(6)]
        return [
            s[0] * e[0] + s[3] * e[1] + s[4] * e[2],
            s[3] * e[0] + s[1] * e[1] + s[5] * e[2],
            s[4] * e[0] + s[5] * e[1] + s[2] * e[2],
        ]

    def operator(row, e, e_next):
        k = curl(row, e, e_next)
        si = tensor(row, e[1::2])
        sr = tensor(row, e[0::2])
        return [k[j] - si[j // 2] if j % 2 == 0 else k[j] + sr[j // 2] for j in range(6)]

    def jacobi(row, e, scale):
        result = []
        for c in range(3):
            alpha, beta = get(coef, row, c), get(coef, row, 3 + c)
            result.append(scale * (alpha * e[2 * c] + beta * e[2 * c + 1]))
            result.append(scale * (alpha * e[2 * c + 1] - beta * e[2 * c]))
        return result

    def nodal(row, q, scale):
        alpha, beta = get(coef, row, 6), get(coef, row, 7)
        return [scale * (alpha * q[0] + beta * q[1]), scale * (alpha * q[1] - beta * q[0])]

    def load(ref, row, n=6):
        return [get(ref, row, c) for c in range(n)]

    def store(ref, row, values, base=0):
        for c, value in enumerate(values):
            put(ref, row, base + c, value)

    def zeroth(y):
        store(z1, y, jacobi(y, load(v, y), 0.7))

    def first(y):
        ahead = jacobi(y + 1, load(v, y + 1), 0.7)
        store(z1, y + 1, ahead)
        applied = operator(y, load(z1, y), ahead)
        rest = [r - w for r, w in zip(load(v, y), applied)]
        store(t1, y, rest)
        store(p, y, jacobi(y, rest, 0.6))

    def second(y):
        applied = operator(y, load(p, y), load(p, y + 1))
        rest = [r - w for r, w in zip(load(t1, y), applied)]
        source = []
        for part in range(2):
            x, n, d = rest[part], rest[2 + part], rest[4 + part]
            before = get(node, y, 6 + part)
            put(node, y + 1, 6 + part, n)
            source.append(((sh.west(x) - x) + (before - n)) + (sh.below(d) - d))
        store(node, y, source)
        store(node, y, nodal(y, source, 0.8), 2)

    def third(y):
        w = [get(node, y, 2 + part) for part in range(2)]
        slopes = []
        for part in range(2):
            ahead = get(node, y + 1, 2 + part)
            slopes.append((sh.east(w[part]) - w[part], ahead - w[part], sh.above(w[part]) - w[part]))
        si = tensor(y, slopes[1])
        sr = tensor(y, slopes[0])
        rest = []
        for part in range(2):
            if part == 0:
                x, n, d = [g - s for g, s in zip(slopes[0], si)]
            else:
                x, n, d = [g + s for g, s in zip(slopes[1], sr)]
            before = get(node, y, 6 + part)
            put(node, y + 1, 6 + part, n)
            applied = ((sh.west(x) - x) + (before - n)) + (sh.below(d) - d)
            rest.append(get(node, y, part) - applied)
        fix = nodal(y, rest, 0.5)
        store(node, y, [w[part] + fix[part] for part in range(2)], 4)

    def lift(y):
        w = [get(node, y, 4 + part) for part in range(2)]
        result = []
        for c in range(3):
            for part in range(2):
                k = 2 * c + part
                if c == 0:
                    slope = sh.east(w[part]) - w[part]
                elif c == 1:
                    slope = get(node, y + 1, 4 + part) - w[part]
                else:
                    slope = sh.above(w[part]) - w[part]
                result.append((get(z1, y, k) + get(p, y, k)) + slope)
        store(u, y, result)
        for k in range(6):
            for z in range(2):
                keep[y, k, z] = result[k].parts[2 * z]
        return result

    def fourth(y):
        ahead = lift(y + 1)
        store(out, y, operator(y, load(u, y), ahead))

    return [
        (zeroth, a, a + 1, 0),
        (first, a, b - 1, 1),
        (second, a + 1, b - 2, 3),
        (third, a + 2, b - 3, 5),
        (lift, a + 3, a + 4, 7),
        (fourth, a + 3, b - 4, 8),
    ]


def two_sum(a, b):
    s = a + b
    t = s - a
    return s, (a - (s - t)) + (b - t)


def main_kernel(
    low_ref, own_ref, high_ref, low_pack_ref, own_pack_ref, high_pack_ref, last_ref, table_ref,
    a0_ref, a1_ref, sums_ref,
    v, c0, c1, u, mat, index, pair, s2, coef, z1, t1, p, node, flux,
    keep0, keep1, bulk, packs, last, table, arrived, left,
):
    sh = Shifts()
    lane = lax.broadcasted_iota(jnp.int32, (SUBS, LANES), 1)
    sub = lax.broadcasted_iota(jnp.int32, (SUBS, LANES), 0)
    copies = [
        pltpu.make_async_copy(low_pack_ref, packs.at[0], arrived.at[0]),
        pltpu.make_async_copy(table_ref, table, arrived.at[1]),
        pltpu.make_async_copy(low_ref, bulk.at[0], arrived.at[2]),
        pltpu.make_async_copy(own_pack_ref, packs.at[1], arrived.at[3]),
        pltpu.make_async_copy(own_ref, bulk.at[1], arrived.at[4]),
        pltpu.make_async_copy(high_pack_ref, packs.at[2], arrived.at[5]),
        pltpu.make_async_copy(high_ref, bulk.at[2], arrived.at[6]),
        pltpu.make_async_copy(last_ref, last, arrived.at[7]),
    ]
    for copy in copies:
        copy.start()

    def await_copies(*which):
        def body():
            for k in which:
                copies[k].wait()

        return body

    def spread(strip, r):
        return pltpu.roll(strip, lax.rem(2 * LANES - STRIP // 2 - STRIP * r, LANES), 1)

    def cell_halo(strip, beyond_strip, r):
        ninth = pltpu.roll(beyond_strip, lax.rem(LANES - STRIP * r, LANES), 1)
        return jnp.where(lane == STRIP // 2, ninth, spread(strip, r))

    def unpack(group):
        def body(y):
            r = y - group * SUBS
            for z in range(2):
                for c in range(6):
                    v[y, c, 2 * z] = bulk[group, c, depth_rows(r, z), :]
                    v[y, c, 2 * z + 1] = spread(packs[group, 2 * c + z], r)
                mat[y, 2 * z] = packs[group, 16 + 2 * r + z]
                mat[y, 2 * z + 1] = cell_halo(packs[group, 12 + z], packs[group, 14 + z], r)

        return (body, group * SUBS, group * SUBS + SUBS, 0)

    def beyond(y):
        for z in range(2):
            mat[y, 2 * z] = last[4 + z]
            mat[y, 2 * z + 1] = cell_halo(last[z], last[2 + z], 0)

    def indices(y):
        ids = Field(mat[y, k] for k in range(4))
        both = 8.0 * ids + sh.east(ids)
        for k in range(4):
            index[y, k] = both.parts[k].astype(jnp.int32)

    def pairs(y):
        for k in range(4):
            which = index[y, k]
            for c in range(6):
                pair[y, c, k] = jnp.take_along_axis(table[c], which, axis=1)

    def tensors(y):
        s = [get(pair, y, c) + get(pair, y + 1, c) for c in range(6)]
        for c in range(6):
            put(s2, y, c, s[c])
        for c in range(3):
            inverse = 1.0 / (s[c] * s[c] + 16.0)
            put(coef, y, c, 4.0 * inverse)
            put(coef, y, 3 + c, s[c] * inverse)
        shift = 2.0 * ((s[0] + s[1]) + s[2])
        inverse = 1.0 / (shift * shift + 36.0)
        put(coef, y, 6, 6.0 * inverse)
        put(coef, y, 7, shift * inverse)

    wavefront(
        [
            unpack(0),
            unpack(1),
            unpack(2),
            (beyond, ROWS, ROWS + 1, 0),
            (indices, 0, ROWS + 1, 1),
            (pairs, 0, ROWS + 1, 2),
            (tensors, 0, ROWS, 4),
        ],
        [
            (0, await_copies(0, 1, 2)),
            (SUBS, await_copies(3, 4)),
            (2 * SUBS, await_copies(5, 6)),
            (ROWS, await_copies(7)),
        ],
    )
    own = pl.ds(HALO, SUBS)
    wavefront(iterate(sh, v, c0, u, keep0, s2, coef, z1, t1, p, node, flux, 0, ROWS))
    first_out = pltpu.make_async_copy(keep0.at[own], a0_ref, left.at[0])
    first_out.start()
    wavefront(
        iterate(sh, c0, c1, u, keep1, s2, coef, z1, t1, p, node, flux, REACH, ROWS - REACH)
    )
    second_out = pltpu.make_async_copy(keep1.at[own], a1_ref, left.at[1])
    second_out.start()

    def dots(r, sums):
        y = HALO + r
        sums = list(sums)
        for c in range(6):
            for z in range(2):
                f, g, h = v[y, c, 2 * z], c0[y, c, 2 * z], c1[y, c, 2 * z]
                for k, term in enumerate((f * f, f * g, g * g, f * h, g * h, h * h)):
                    sums[k] = sums[k] + term
        return tuple(sums)

    zero = jnp.zeros((SUBS, LANES), jnp.float32)
    sums = lax.fori_loop(0, SUBS, dots, (zero,) * 6)
    row = zero
    for k, total in enumerate(sums):
        for step in (4, 2, 1):
            total = total + pltpu.roll(total, step, 0)
        row = jnp.where(sub == k, total, row)
    row = jnp.broadcast_to(jnp.sum(row, axis=1, keepdims=True), (SUBS, LANES))
    row = jnp.where(lane == sub, row, 0.0)
    for step in (4, 2, 1):
        row = row + pltpu.roll(row, step, 0)
    for k in range(16):
        sums_ref[pl.ds(k * SUBS, SUBS), :] = row
    first_out.wait()
    second_out.wait()


def two_sum(a, b):
    s = a + b
    t = s - a
    return s, (a - (s - t)) + (b - t)


def two_product(a, b):
    def split(x):
        t = 4097.0 * x
        high = t - (t - x)
        return high, x - high

    p = a * b
    ah, al = split(a)
    bh, bl = split(b)
    return p, ((ah * bh - p) + ah * bl + al * bh) + al * bl


def quick(s, e):
    t = s + e
    return t, e - (t - s)


def plus(x, y):
    s, e = two_sum(x[0], y[0])
    return quick(s, e + (x[1] + y[1]))


def minus(x, y):
    return plus(x, (-y[0], -y[1]))


def times(x, y):
    p, e = two_product(x[0], y[0])
    return quick(p, e + (x[0] * y[1] + x[1] * y[0]))


def scaled(x, factor):
    p, e = two_product(x[0], jnp.full_like(x[0], factor))
    return quick(p, e + x[1] * factor)


def over(x, y):
    q = x[0] / y[0]
    r = minus(x, times(y, (q, jnp.zeros_like(q))))
    return quick(q, (r[0] + r[1]) / y[0])


def final_kernel(sums_ref, a0_ref, a1_ref, result_ref, hess_ref, out, a0, a1, done):
    lane = lax.broadcasted_iota(jnp.int32, (SUBS, LANES), 1)
    sub = lax.broadcasted_iota(jnp.int32, (SUBS, LANES), 0)
    arriving = [
        pltpu.make_async_copy(a0_ref, a0, done.at[6]),
        pltpu.make_async_copy(a1_ref, a1, done.at[7]),
    ]
    for copy in arriving:
        copy.start()
    level = [(sums_ref[pl.ds(k * SUBS, SUBS), :], None) for k in range(16)]
    while len(level) > 1:
        pairs = []
        for (f, f_rest), (g, g_rest) in zip(level[::2], level[1::2]):
            total, error = two_sum(f, g)
            pairs.append((total, error if f_rest is None else error + (f_rest + g_rest)))
        level = pairs
    total, rest = level[0]
    for step in (4, 2, 1):
        total, error = two_sum(total, pltpu.roll(total, step, 0))
        rest = rest + pltpu.roll(rest, step, 0) + error

    def columns(values):
        picked = jnp.sum(jnp.where(lane == sub, values, 0.0), axis=1, keepdims=True)
        return [jnp.broadcast_to(picked[k : k + 1], (SUBS, LANES)) for k in range(6)]

    bb, bc, cc, bd, cd, dd = [quick(f, g) for f, g in zip(columns(total), columns(rest))]
    eps = (jnp.full((SUBS, LANES), epsilon, jnp.float32), jnp.zeros((SUBS, LANES), jnp.float32))
    beta2 = plus(bb, eps)
    h00 = over(bc, beta2)
    norm1 = minus(minus(cc, times(h00, bc)), times(eps, times(h00, h00)))
    norm1 = (jnp.maximum(norm1[0], 0.0), jnp.where(norm1[0] > 0.0, norm1[1], 0.0))
    tall = plus(norm1, times(eps, beta2))
    x = minus(bd, times(h00, bc))
    y = plus(minus(minus(cd, times(h00, cc)), times(h00, bd)), times(times(h00, h00), bc))
    x_over = over(x, beta2)
    y_over = over(y, tall)
    norm2 = plus(minus(dd, scaled(times(h00, cd), 2.0)), times(times(h00, h00), cc))
    norm2 = minus(norm2, plus(times(x, x_over), times(eps, times(x_over, x_over))))
    norm2 = minus(norm2, plus(times(y, y_over), times(times(eps, beta2), times(y_over, y_over))))
    norm2 = plus(norm2, scaled(times(times(x_over, y_over), times(eps, h00)), 2.0))
    norm2 = over(norm2, tall)

    beta = jnp.sqrt(beta2[0])
    e00 = h00[0]
    e10 = jnp.sqrt(tall[0] / beta2[0])
    e01 = x_over[0] / e10
    e11 = y_over[0]
    e21 = jnp.sqrt(jnp.maximum(norm2[0], 0.0) + epsilon)

    g00 = e00 * e00 + e10 * e10
    g01 = e00 * e01 + e10 * e11
    g11 = e01 * e01 + e11 * e11 + e21 * e21
    l00 = jnp.sqrt(g00)
    l10 = g01 / l00
    l11 = jnp.sqrt(g11 - l10 * l10)
    m0 = beta * e00 / l00
    m1 = (beta * e01 - l10 * m0) / l11
    y1 = m1 / l11
    y0 = (m0 - l10 * y1) / l00
    k0 = (y0 - y1 * e00 / e10) / beta
    k1 = y1 / (e10 * beta)

    table = jnp.where(lane == 0, e00, jnp.where(lane == 1, e10, 0.0))
    later = jnp.where(lane == 0, e01, jnp.where(lane == 1, e11, e21))
    hess_ref[...] = jnp.where(sub == 0, table, later)[:2, :3]
    for copy in arriving:
        copy.wait()
    copies = []
    for c in range(6):
        for row in range(SUBS):
            for z in range(2):
                out[c, depth_rows(row, z), :] = k0 * a0[row, c, z] + k1 * a1[row, c, z]
        copies.append(pltpu.make_async_copy(out.at[c], result_ref.at[c], done.at[c]))
        copies[-1].start()
    for copy in copies:
        copy.wait()


VMEM = pl.BlockSpec(memory_space=pltpu.VMEM)
ANY = pl.BlockSpec(memory_space=pl.ANY)


def call(kernel, outs, ins, scratch=(), semaphores=()):
    return pl.pallas_call(
        kernel,
        out_shape=[jax.ShapeDtypeStruct(shape, jnp.float32) for shape, _ in outs],
        in_specs=ins,
        out_specs=[spec for _, spec in outs],
        scratch_shapes=[pltpu.VMEM(shape, dtype) for shape, dtype in scratch]
        + [pltpu.SemaphoreType.DMA((n,)) for n in semaphores],
        compiler_params=pltpu.CompilerParams(vmem_limit_bytes=VMEM_LIMIT),
    )


def moved(value, axis, step):
    size = lax.axis_size(axis)
    return lax.ppermute(value, axis, [(i, (i + step) % size) for i in range(size)])


TILE = (SUBS, LANES)
KEPT = (SUBS, 6, 2) + TILE
BLOCK = (6, LANES, LANES)


def floats(*shapes):
    return [(shape, jnp.float32) for shape in shapes]


def rows(n, extra=0):
    return (ROWS + extra, n, 4) + TILE


def strip_call():
    return call(
        strip_kernel, [((16,) + TILE, VMEM), ((16,) + TILE, VMEM), ((6,) + TILE, VMEM)], [VMEM] * 4
    )


def main_call():
    return call(
        main_kernel,
        [(KEPT, ANY), (KEPT, ANY), ((LANES, LANES), VMEM)],
        [ANY] * 8,
        floats(*[rows(6)] * 4, (ROWS + 1, 4) + TILE)
        + [((ROWS + 1, 4) + TILE, jnp.int32)]
        + floats(rows(6, 1), rows(6), rows(8), *[rows(6)] * 3, rows(8, 1), rows(4, 1))
        + floats((ROWS, 6, 2) + TILE, (ROWS, 6, 2) + TILE)
        + floats((3,) + BLOCK, (3, PACK) + TILE, (6,) + TILE, (6,) + TILE),
        (8, 2),
    )


def final_call():
    return call(
        final_kernel,
        [(BLOCK, ANY), ((2, 3), VMEM)],
        [VMEM, ANY, ANY],
        floats(BLOCK, KEPT, KEPT),
        (8,),
    )


def on_device(right_side, materials, sigma_diag, sigma_off):
    rhs = right_side.reshape(BLOCK)
    strips, cells, table = strip_call()(
        rhs, materials.reshape(LANES, LANES), sigma_diag, sigma_off
    )
    from_right = moved(strips, "gx", -1)
    from_left = moved(strips, "gx", 1)
    bulk, strips = lax.optimization_barrier((rhs, strips))
    low = moved(bulk, "gy", 1)
    high = moved(bulk, "gy", -1)
    lane = lax.broadcasted_iota(jnp.int32, (14,) + TILE, 2)
    mixed = jnp.where(lane % STRIP < STRIP // 2, from_left[:14], from_right[:14])
    pack = jnp.concatenate([mixed, from_right[14:], cells])
    low_pack = moved(pack, "gy", 1)
    high_pack = moved(pack, "gy", -1)
    last = moved(pack[12:18], "gy", -2)
    a0, a1, sums = main_call()(low, rhs, high, low_pack, pack, high_pack, last, table)
    gathered = lax.all_to_all(sums, ("gx", "gy"), 0, 0, tiled=True)
    result, hessenberg = final_call()(gathered, a0, a1)
    return result.reshape(right_side.shape), hessenberg.T


def solution(mesh):
    return jax.shard_map(
        on_device,
        mesh=mesh,
        in_specs=(P(None, None, None, "gy", "gx"), P(None, "gy", "gx"), P(), P()),
        out_specs=(P(None, None, None, "gy", "gx"), P()),
        check_vma=False,
    )
```

```python
import jax
import jax.numpy as jnp
from jax import lax
from jax.experimental import pallas as pl
from jax.experimental.pallas import tpu as pltpu
from jax.sharding import PartitionSpec as P

epsilon = 1e-06
LANES = 128
SUBS = 8
REACH = 4
HALO = 2 * REACH
ROWS = SUBS + 2 * HALO
STRIP = 16
CHUNK = 4
CHUNKS = ROWS // CHUNK
VMEM_LIMIT = 44 * 2**20


class Field:
    def __init__(self, parts):
        self.parts = tuple(parts)

    def zip(self, other, op):
        if isinstance(other, Field):
            return Field(op(a, b) for a, b in zip(self.parts, other.parts))
        return Field(op(a, other) for a in self.parts)

    def __add__(self, other):
        return self.zip(other, lambda a, b: a + b)

    def __sub__(self, other):
        return self.zip(other, lambda a, b: a - b)

    def __mul__(self, other):
        return self.zip(other, lambda a, b: a * b)

    __rmul__ = __mul__

    def __rtruediv__(self, top):
        return Field(top / a for a in self.parts)


class Shifts:
    def __init__(self):
        lane = lax.broadcasted_iota(jnp.int32, (SUBS, LANES), 1)
        sub = lax.broadcasted_iota(jnp.int32, (SUBS, LANES), 0)
        self.first_lane = lane == 0
        self.last_lane = lane == LANES - 1
        self.first_sub = sub == 0
        self.last_sub = sub == SUBS - 1

    def east(self, field):
        r = [pltpu.roll(t, LANES - 1, 1) for t in field.parts]
        return Field(jnp.where(self.last_lane, r[k ^ 1], r[k]) for k in range(4))

    def west(self, field):
        r = [pltpu.roll(t, 1, 1) for t in field.parts]
        return Field(jnp.where(self.first_lane, r[k ^ 1], r[k]) for k in range(4))

    def above(self, field):
        r = [pltpu.roll(t, SUBS - 1, 0) for t in field.parts]
        low = [jnp.where(self.last_sub, r[2 + k], r[k]) for k in range(2)]
        return Field(low + [jnp.where(self.last_sub, 0.0, r[2 + k]) for k in range(2)])

    def below(self, field):
        r = [pltpu.roll(t, 1, 0) for t in field.parts]
        low = [jnp.where(self.first_sub, 0.0, r[k]) for k in range(2)]
        return Field(low + [jnp.where(self.first_sub, r[k], r[2 + k]) for k in range(2)])


def get(ref, row, c):
    return Field(ref[row, c, k] for k in range(4))


def put(ref, row, c, field):
    for k in range(4):
        ref[row, c, k] = field.parts[k]


def loop(start, stop, body):
    lax.fori_loop(start, stop, lambda i, c: (body(i), c)[1], 0)


def depth_rows(y, z):
    return pl.ds(z * SUBS * SUBS + y, SUBS, stride=SUBS)


def packed(tiles, offset):
    lane = lax.broadcasted_iota(jnp.int32, (SUBS, LANES), 1)
    result = None
    for r, tile in enumerate(tiles):
        shift = (STRIP * r + offset) % LANES
        moved_tile = pltpu.roll(tile, shift, 1) if shift else tile
        result = moved_tile if r == 0 else jnp.where(lane >= STRIP * r, moved_tile, result)
    return result


def cell_strip_kernel(low_ref, own_ref, high_ref, last_ref, diag_ref, off_ref, strip_ref, table_ref):
    lane = lax.broadcasted_iota(jnp.int32, (SUBS, LANES), 1)
    for z in range(2):
        for group, ref in enumerate((low_ref, own_ref, high_ref)):
            cells = [ref[depth_rows(r, z), :].astype(jnp.float32) for r in range(SUBS)]
            strip_ref[2 * group + z] = packed(cells, STRIP // 2)
            strip_ref[8 + 2 * group + z] = packed(cells, 0)
        cells = [last_ref[pl.ds(z * SUBS, SUBS), :].astype(jnp.float32)]
        strip_ref[6 + z] = packed(cells, STRIP // 2)
        strip_ref[14 + z] = packed(cells, 0)
    x, n, d = [jnp.broadcast_to(0.5 * diag_ref[c : c + 1, :], (SUBS, SUBS)) for c in range(3)]
    entries = [x, n, d]
    for c, (f, g) in enumerate(((x, n), (x, d), (n, d))):
        entries.append(jnp.broadcast_to(off_ref[c : c + 1, :], (SUBS, SUBS)) * jnp.sqrt(f * g))
    for c in range(6):
        table_ref[c, :, :] = jnp.zeros((SUBS, LANES), jnp.float32)
        table_ref[c, :, :SUBS] = entries[c]
    for c in range(6):
        single = table_ref[c]
        table_ref[c] = jnp.take_along_axis(single, lane // SUBS, axis=1) + jnp.take_along_axis(
            single, lane % SUBS, axis=1
        )


def strip_kernel(low_ref, own_ref, high_ref, strip_ref):
    for group, ref in enumerate((low_ref, own_ref, high_ref)):
        for c in range(6):
            for z in range(2):
                strip_ref[12 * group + 2 * c + z] = packed(
                    [ref[c, depth_rows(r, z), :] for r in range(SUBS)], STRIP // 2
                )


def spread(strip, r):
    return pltpu.roll(strip, lax.rem(2 * LANES - STRIP // 2 - STRIP * r, LANES), 1)


def tensor_kernel(
    low_ref, own_ref, high_ref, last_ref, left_ref, right_ref, table_ref,
    s2_ref, coef_ref,
    mat, index, pair, s2, coef, out_sem,
):
    sh = Shifts()
    lane = lax.broadcasted_iota(jnp.int32, (SUBS, LANES), 1)
    west = lane % STRIP < STRIP // 2

    def cell_halo(k, r):
        strip = jnp.where(west, left_ref[k], right_ref[k])
        ninth = pltpu.roll(right_ref[8 + k], lax.rem(LANES - STRIP * r, LANES), 1)
        return jnp.where(lane == STRIP // 2, ninth, spread(strip, r))

    def unpack(group, ref):
        def body(y):
            r = y - group * SUBS
            for z in range(2):
                mat[y, 2 * z] = ref[depth_rows(r, z), :].astype(jnp.float32)
                mat[y, 2 * z + 1] = cell_halo(2 * group + z, r)

        return (body, group * SUBS, group * SUBS + SUBS, 0)

    def beyond(y):
        for z in range(2):
            mat[y, 2 * z] = last_ref[pl.ds(z * SUBS, SUBS), :].astype(jnp.float32)
            mat[y, 2 * z + 1] = cell_halo(6 + z, 0)

    def indices(y):
        ids = Field(mat[y, k] for k in range(4))
        both = 8.0 * ids + sh.east(ids)
        for k in range(4):
            index[y, k] = both.parts[k].astype(jnp.int32)

    def pairs(y):
        for k in range(4):
            which = index[y, k]
            for c in range(6):
                pair[y, c, k] = jnp.take_along_axis(table_ref[c], which, axis=1)

    def tensors(y):
        s = [get(pair, y, c) + get(pair, y + 1, c) for c in range(6)]
        for c in range(6):
            put(s2, y, c, s[c])
        for c in range(3):
            inverse = 1.0 / (s[c] * s[c] + 16.0)
            put(coef, y, c, 4.0 * inverse)
            put(coef, y, 3 + c, s[c] * inverse)
        shift = 2.0 * ((s[0] + s[1]) + s[2])
        inverse = 1.0 / (shift * shift + 36.0)
        put(coef, y, 6, 6.0 * inverse)
        put(coef, y, 7, shift * inverse)

    copies = chunk_copies(s2, s2_ref, coef, coef_ref, out_sem)

    def send(k):
        def body():
            copies[2 * k].start()
            copies[2 * k + 1].start()

        return body

    wavefront(
        [
            unpack(0, low_ref),
            unpack(1, own_ref),
            unpack(2, high_ref),
            (beyond, ROWS, ROWS + 1, 0),
            (indices, 0, ROWS + 1, 1),
            (pairs, 0, ROWS + 1, 2),
            (tensors, 0, ROWS, 4),
        ],
        [(CHUNK * (k + 1) + 4, send(k)) for k in range(CHUNKS - 1)],
    )
    send(CHUNKS - 1)()
    for copy in copies:
        copy.wait()


def chunk_copies(s2_from, s2_to, coef_from, coef_to, semaphores):
    copies = []
    for k in range(CHUNKS):
        part = pl.ds(CHUNK * k, CHUNK)
        for j, (f, t) in enumerate(((s2_from, s2_to), (coef_from, coef_to))):
            copies.append(pltpu.make_async_copy(f.at[part], t.at[part], semaphores.at[2 * k + j]))
    return copies


def wavefront(stages, events=()):
    edges = {e + lag for _, start, stop, lag in stages for e in (start, stop)}
    edges = sorted(edges | {at for at, _ in events})
    for start, stop in zip(edges, edges[1:]):
        for at, body in events:
            if at == start:
                body()
        active = [st for st in stages if st[1] + st[3] <= start and stop <= st[2] + st[3]]

        def step(s, active=active):
            for body, _, _, lag in reversed(active):
                body(s - lag)

        loop(start, stop, step)


def iterate(sh, v, out, u, keep, s2, coef, z1, t1, p, node, flux, a, b, wait=0):
    def fluxes(e, above_row):
        bx = (above_row[1] - e[2]) - (sh.above(e[1]) - e[1])
        by = (sh.above(e[0]) - e[0]) - (sh.east(e[2]) - e[2])
        bz = (sh.east(e[1]) - e[1]) - (above_row[0] - e[0])
        return bx, by, bz

    def curl(row, e, e_next):
        result = []
        for part in range(2):
            here = [e[2 * c + part] for c in range(3)]
            bx, by, bz = fluxes(here, (e_next[part], e_next[4 + part]))
            pbx, pbz = get(flux, row, 2 * part), get(flux, row, 2 * part + 1)
            put(flux, row + 1, 2 * part, bx)
            put(flux, row + 1, 2 * part + 1, bz)
            result.append(
                (
                    (pbz - bz) - (sh.below(by) - by),
                    (sh.below(bx) - bx) - (sh.west(bz) - bz),
                    (sh.west(by) - by) - (pbx - bx),
                )
            )
        return [result[k % 2][k // 2] for k in range(6)]

    def tensor(row, e):
        s = [get(s2, row, c) for c in range(6)]
        return [
            s[0] * e[0] + s[3] * e[1] + s[4] * e[2],
            s[3] * e[0] + s[1] * e[1] + s[5] * e[2],
            s[4] * e[0] + s[5] * e[1] + s[2] * e[2],
        ]

    def operator(row, e, e_next):
        k = curl(row, e, e_next)
        si = tensor(row, e[1::2])
        sr = tensor(row, e[0::2])
        return [k[j] - si[j // 2] if j % 2 == 0 else k[j] + sr[j // 2] for j in range(6)]

    def jacobi(row, e, scale):
        result = []
        for c in range(3):
            alpha, beta = get(coef, row, c), get(coef, row, 3 + c)
            result.append(scale * (alpha * e[2 * c] + beta * e[2 * c + 1]))
            result.append(scale * (alpha * e[2 * c + 1] - beta * e[2 * c]))
        return result

    def nodal(row, q, scale):
        alpha, beta = get(coef, row, 6), get(coef, row, 7)
        return [scale * (alpha * q[0] + beta * q[1]), scale * (alpha * q[1] - beta * q[0])]

    def load(ref, row, n=6):
        return [get(ref, row, c) for c in range(n)]

    def store(ref, row, values, base=0):
        for c, value in enumerate(values):
            put(ref, row, base + c, value)

    def zeroth(y):
        store(z1, y, jacobi(y, load(v, y), 0.7))

    def first(y):
        ahead = jacobi(y + 1, load(v, y + 1), 0.7)
        store(z1, y + 1, ahead)
        applied = operator(y, load(z1, y), ahead)
        rest = [r - w for r, w in zip(load(v, y), applied)]
        store(t1, y, rest)
        store(p, y, jacobi(y, rest, 0.6))

    def second(y):
        applied = operator(y, load(p, y), load(p, y + 1))
        rest = [r - w for r, w in zip(load(t1, y), applied)]
        source = []
        for part in range(2):
            x, n, d = rest[part], rest[2 + part], rest[4 + part]
            before = get(node, y, 6 + part)
            put(node, y + 1, 6 + part, n)
            source.append(((sh.west(x) - x) + (before - n)) + (sh.below(d) - d))
        store(node, y, source)
        store(node, y, nodal(y, source, 0.8), 2)

    def third(y):
        w = [get(node, y, 2 + part) for part in range(2)]
        slopes = []
        for part in range(2):
            ahead = get(node, y + 1, 2 + part)
            slopes.append((sh.east(w[part]) - w[part], ahead - w[part], sh.above(w[part]) - w[part]))
        si = tensor(y, slopes[1])
        sr = tensor(y, slopes[0])
        rest = []
        for part in range(2):
            if part == 0:
                x, n, d = [g - s for g, s in zip(slopes[0], si)]
            else:
                x, n, d = [g + s for g, s in zip(slopes[1], sr)]
            before = get(node, y, 6 + part)
            put(node, y + 1, 6 + part, n)
            applied = ((sh.west(x) - x) + (before - n)) + (sh.below(d) - d)
            rest.append(get(node, y, part) - applied)
        fix = nodal(y, rest, 0.5)
        store(node, y, [w[part] + fix[part] for part in range(2)], 4)

    def lift(y):
        w = [get(node, y, 4 + part) for part in range(2)]
        result = []
        for c in range(3):
            for part in range(2):
                k = 2 * c + part
                if c == 0:
                    slope = sh.east(w[part]) - w[part]
                elif c == 1:
                    slope = get(node, y + 1, 4 + part) - w[part]
                else:
                    slope = sh.above(w[part]) - w[part]
                result.append((get(z1, y, k) + get(p, y, k)) + slope)
        store(u, y, result)
        for k in range(6):
            for z in range(2):
                keep[y, k, z] = result[k].parts[2 * z]
        return result

    def fourth(y):
        ahead = lift(y + 1)
        store(out, y, operator(y, load(u, y), ahead))

    return [
        (zeroth, a, a + 1, wait),
        (first, a, b - 1, wait + 1),
        (second, a + 1, b - 2, wait + 3),
        (third, a + 2, b - 3, wait + 5),
        (lift, a + 3, a + 4, wait + 7),
        (fourth, a + 3, b - 4, wait + 8),
    ]


def main_kernel(
    low_ref, own_ref, high_ref, left_ref, right_ref, s2_ref, coef_ref,
    a0_ref, a1_ref, sums_ref,
    v, c0, c1, u, s2, coef, z1, t1, p, node, flux,
    keep0, keep1, bulk, left_strip, right_strip, arrived, tensors_in, out_sem,
):
    sh = Shifts()
    lane = lax.broadcasted_iota(jnp.int32, (SUBS, LANES), 1)
    sub = lax.broadcasted_iota(jnp.int32, (SUBS, LANES), 0)
    west = lane % STRIP < STRIP // 2
    copies = [
        pltpu.make_async_copy(left_ref, left_strip, arrived.at[0]),
        pltpu.make_async_copy(right_ref, right_strip, arrived.at[1]),
    ]
    for group, ref in enumerate((low_ref, own_ref, high_ref)):
        copies.append(pltpu.make_async_copy(ref, bulk.at[group], arrived.at[2 + group]))
    tensor_copies = chunk_copies(s2_ref, s2, coef_ref, coef, tensors_in)
    for copy in copies[:3] + tensor_copies[:4] + copies[3:] + tensor_copies[4:]:
        copy.start()

    def awaited(*waiting):
        def body():
            for copy in waiting:
                copy.wait()

        return body

    def unpack(group):
        def body(y):
            r = y - group * SUBS
            for z in range(2):
                for c in range(6):
                    k = 12 * group + 2 * c + z
                    v[y, c, 2 * z] = bulk[group, c, depth_rows(r, z), :]
                    v[y, c, 2 * z + 1] = spread(jnp.where(west, left_strip[k], right_strip[k]), r)

        return (body, group * SUBS, group * SUBS + SUBS, 0)

    own = pl.ds(HALO, SUBS)
    wavefront(
        [unpack(0), unpack(1), unpack(2)]
        + iterate(sh, v, c0, u, keep0, s2, coef, z1, t1, p, node, flux, 0, ROWS, 1),
        [(0, awaited(*copies[:3]))]
        + [(CHUNK * k + 1, awaited(*tensor_copies[2 * k : 2 * k + 2])) for k in range(CHUNKS)]
        + [(SUBS, awaited(copies[3])), (2 * SUBS, awaited(copies[4]))],
    )
    first_out = pltpu.make_async_copy(keep0.at[own], a0_ref, out_sem.at[0])
    first_out.start()
    wavefront(
        iterate(sh, c0, c1, u, keep1, s2, coef, z1, t1, p, node, flux, REACH, ROWS - REACH)
    )
    second_out = pltpu.make_async_copy(keep1.at[own], a1_ref, out_sem.at[1])
    second_out.start()

    def dots(r, sums):
        y = HALO + r
        sums = list(sums)
        for c in range(6):
            for z in range(2):
                f, g, h = v[y, c, 2 * z], c0[y, c, 2 * z], c1[y, c, 2 * z]
                for k, term in enumerate((f * f, f * g, g * g, f * h, g * h, h * h)):
                    sums[k] = sums[k] + term
        return tuple(sums)

    zero = jnp.zeros((SUBS, LANES), jnp.float32)
    sums = lax.fori_loop(0, SUBS, dots, (zero,) * 6)
    row = zero
    for k, total in enumerate(sums):
        for step in (4, 2, 1):
            total = total + pltpu.roll(total, step, 0)
        row = jnp.where(sub == k, total, row)
    row = jnp.broadcast_to(jnp.sum(row, axis=1, keepdims=True), (SUBS, LANES))
    row = jnp.where(lane == sub, row, 0.0)
    for step in (4, 2, 1):
        row = row + pltpu.roll(row, step, 0)
    for k in range(16):
        sums_ref[pl.ds(k * SUBS, SUBS), :] = row
    first_out.wait()
    second_out.wait()


def two_sum(a, b):
    s = a + b
    t = s - a
    return s, (a - (s - t)) + (b - t)


def two_product(a, b):
    def split(x):
        t = 4097.0 * x
        high = t - (t - x)
        return high, x - high

    p = a * b
    ah, al = split(a)
    bh, bl = split(b)
    return p, ((ah * bh - p) + ah * bl + al * bh) + al * bl


def quick(s, e):
    t = s + e
    return t, e - (t - s)


def plus(x, y):
    s, e = two_sum(x[0], y[0])
    return quick(s, e + (x[1] + y[1]))


def minus(x, y):
    return plus(x, (-y[0], -y[1]))


def times(x, y):
    p, e = two_product(x[0], y[0])
    return quick(p, e + (x[0] * y[1] + x[1] * y[0]))


def scaled(x, factor):
    p, e = two_product(x[0], jnp.full_like(x[0], factor))
    return quick(p, e + x[1] * factor)


def over(x, y):
    q = x[0] / y[0]
    r = minus(x, times(y, (q, jnp.zeros_like(q))))
    return quick(q, (r[0] + r[1]) / y[0])


def final_kernel(sums_ref, a0_ref, a1_ref, result_ref, hess_ref, out, a0, a1, done):
    lane = lax.broadcasted_iota(jnp.int32, (SUBS, LANES), 1)
    sub = lax.broadcasted_iota(jnp.int32, (SUBS, LANES), 0)
    arriving = [
        pltpu.make_async_copy(a0_ref, a0, done.at[6]),
        pltpu.make_async_copy(a1_ref, a1, done.at[7]),
    ]
    for copy in arriving:
        copy.start()
    level = [(sums_ref[pl.ds(k * SUBS, SUBS), :], None) for k in range(16)]
    while len(level) > 1:
        pairs = []
        for (f, f_rest), (g, g_rest) in zip(level[::2], level[1::2]):
            total, error = two_sum(f, g)
            pairs.append((total, error if f_rest is None else error + (f_rest + g_rest)))
        level = pairs
    total, rest = level[0]
    for step in (4, 2, 1):
        total, error = two_sum(total, pltpu.roll(total, step, 0))
        rest = rest + pltpu.roll(rest, step, 0) + error

    def columns(values):
        picked = jnp.sum(jnp.where(lane == sub, values, 0.0), axis=1, keepdims=True)
        return [jnp.broadcast_to(picked[k : k + 1], (SUBS, LANES)) for k in range(6)]

    bb, bc, cc, bd, cd, dd = [quick(f, g) for f, g in zip(columns(total), columns(rest))]
    eps = (jnp.full((SUBS, LANES), epsilon, jnp.float32), jnp.zeros((SUBS, LANES), jnp.float32))
    beta2 = plus(bb, eps)
    h00 = over(bc, beta2)
    norm1 = minus(minus(cc, times(h00, bc)), times(eps, times(h00, h00)))
    norm1 = (jnp.maximum(norm1[0], 0.0), jnp.where(norm1[0] > 0.0, norm1[1], 0.0))
    tall = plus(norm1, times(eps, beta2))
    x = minus(bd, times(h00, bc))
    y = plus(minus(minus(cd, times(h00, cc)), times(h00, bd)), times(times(h00, h00), bc))
    x_over = over(x, beta2)
    y_over = over(y, tall)
    norm2 = plus(minus(dd, scaled(times(h00, cd), 2.0)), times(times(h00, h00), cc))
    norm2 = minus(norm2, plus(times(x, x_over), times(eps, times(x_over, x_over))))
    norm2 = minus(norm2, plus(times(y, y_over), times(times(eps, beta2), times(y_over, y_over))))
    norm2 = plus(norm2, scaled(times(times(x_over, y_over), times(eps, h00)), 2.0))
    norm2 = over(norm2, tall)

    beta = jnp.sqrt(beta2[0])
    e00 = h00[0]
    e10 = jnp.sqrt(tall[0] / beta2[0])
    e01 = x_over[0] / e10
    e11 = y_over[0]
    e21 = jnp.sqrt(jnp.maximum(norm2[0], 0.0) + epsilon)

    g00 = e00 * e00 + e10 * e10
    g01 = e00 * e01 + e10 * e11
    g11 = e01 * e01 + e11 * e11 + e21 * e21
    l00 = jnp.sqrt(g00)
    l10 = g01 / l00
    l11 = jnp.sqrt(g11 - l10 * l10)
    m0 = beta * e00 / l00
    m1 = (beta * e01 - l10 * m0) / l11
    y1 = m1 / l11
    y0 = (m0 - l10 * y1) / l00
    k0 = (y0 - y1 * e00 / e10) / beta
    k1 = y1 / (e10 * beta)

    table = jnp.where(lane == 0, e00, jnp.where(lane == 1, e10, 0.0))
    later = jnp.where(lane == 0, e01, jnp.where(lane == 1, e11, e21))
    hess_ref[...] = jnp.where(sub == 0, table, later)[:2, :3]
    for copy in arriving:
        copy.wait()
    copies = []
    for c in range(6):
        for row in range(SUBS):
            for z in range(2):
                out[c, depth_rows(row, z), :] = k0 * a0[row, c, z] + k1 * a1[row, c, z]
        copies.append(pltpu.make_async_copy(out.at[c], result_ref.at[c], done.at[c]))
        copies[-1].start()
    for copy in copies:
        copy.wait()


VMEM = pl.BlockSpec(memory_space=pltpu.VMEM)
ANY = pl.BlockSpec(memory_space=pl.ANY)


def call(kernel, outs, ins, scratch=(), semaphores=()):
    return pl.pallas_call(
        kernel,
        out_shape=[jax.ShapeDtypeStruct(shape, jnp.float32) for shape, _ in outs],
        in_specs=ins,
        out_specs=[spec for _, spec in outs],
        scratch_shapes=[pltpu.VMEM(shape, dtype) for shape, dtype in scratch]
        + [pltpu.SemaphoreType.DMA((n,)) for n in semaphores],
        compiler_params=pltpu.CompilerParams(vmem_limit_bytes=VMEM_LIMIT),
    )


def moved(value, axis, step):
    size = lax.axis_size(axis)
    return lax.ppermute(value, axis, [(i, (i + step) % size) for i in range(size)])


TILE = (SUBS, LANES)
KEPT = (SUBS, 6, 2) + TILE
BLOCK = (6, LANES, LANES)


def floats(*shapes):
    return [(shape, jnp.float32) for shape in shapes]


def rows(n, extra=0):
    return (ROWS + extra, n, 4) + TILE


def cell_strip_call():
    return call(cell_strip_kernel, [((16,) + TILE, VMEM), ((6,) + TILE, VMEM)], [VMEM] * 6)


def strip_call():
    return call(strip_kernel, [((36,) + TILE, VMEM)], [VMEM] * 3)


def tensor_call():
    return call(
        tensor_kernel,
        [(rows(6), ANY), (rows(8), ANY)],
        [VMEM] * 7,
        floats((ROWS + 1, 4) + TILE)
        + [((ROWS + 1, 4) + TILE, jnp.int32)]
        + floats(rows(6, 1), rows(6), rows(8)),
        (2 * CHUNKS,),
    )


def main_call():
    return call(
        main_kernel,
        [(KEPT, ANY), (KEPT, ANY), ((LANES, LANES), VMEM)],
        [ANY] * 7,
        floats(*[rows(6)] * 5, rows(8), *[rows(6)] * 3, rows(8, 1), rows(4, 1))
        + floats((ROWS, 6, 2) + TILE, (ROWS, 6, 2) + TILE)
        + floats((3,) + BLOCK, (36,) + TILE, (36,) + TILE),
        (5, 2 * CHUNKS, 2),
    )


def final_call():
    return call(
        final_kernel,
        [(BLOCK, ANY), ((2, 3), VMEM)],
        [VMEM, ANY, ANY],
        floats(BLOCK, KEPT, KEPT),
        (8,),
    )


def on_device(right_side, materials, sigma_diag, sigma_off):
    rhs = right_side.reshape(BLOCK)
    cells = materials.reshape(LANES, LANES)
    low_cells = moved(cells, "gy", 1)
    high_cells = moved(cells, "gy", -1)
    first_row = materials[:, 0, :]
    bulk, first_row = lax.optimization_barrier((rhs, first_row))
    last = moved(first_row, "gy", -2)
    low = moved(bulk, "gy", 1)
    high = moved(bulk, "gy", -1)
    cell_strips, table = cell_strip_call()(
        low_cells, cells, high_cells, last, sigma_diag, sigma_off
    )
    s2, coef = tensor_call()(
        low_cells, cells, high_cells, last,
        moved(cell_strips, "gx", 1), moved(cell_strips, "gx", -1), table,
    )
    low, high, s2, coef = lax.optimization_barrier((low, high, s2, coef))
    (strips,) = strip_call()(low, rhs, high)
    a0, a1, sums = main_call()(
        low, rhs, high, moved(strips, "gx", 1), moved(strips, "gx", -1), s2, coef
    )
    gathered = lax.all_to_all(sums, ("gx", "gy"), 0, 0, tiled=True)
    result, hessenberg = final_call()(gathered, a0, a1)
    return result.reshape(right_side.shape), hessenberg.T


def solution(mesh):
    return jax.shard_map(
        on_device,
        mesh=mesh,
        in_specs=(P(None, None, None, "gy", "gx"), P(None, "gy", "gx"), P(), P()),
        out_specs=(P(None, None, None, "gy", "gx"), P()),
        check_vma=False,
    )
```

```python
import jax
import jax.numpy as jnp
from jax import lax
from jax.experimental import pallas as pl
from jax.experimental.pallas import tpu as pltpu
from jax.sharding import PartitionSpec as P

epsilon = 1e-06
LANES = 128
SUBS = 8
REACH = 4
HALO = 2 * REACH
ROWS = SUBS + 2 * HALO
STRIP = 16
PACK = 32
VMEM_LIMIT = 44 * 2**20


class Field:
    def __init__(self, parts):
        self.parts = tuple(parts)

    def zip(self, other, op):
        if isinstance(other, Field):
            return Field(op(a, b) for a, b in zip(self.parts, other.parts))
        return Field(op(a, other) for a in self.parts)

    def __add__(self, other):
        return self.zip(other, lambda a, b: a + b)

    def __sub__(self, other):
        return self.zip(other, lambda a, b: a - b)

    def __mul__(self, other):
        return self.zip(other, lambda a, b: a * b)

    __rmul__ = __mul__

    def __rtruediv__(self, top):
        return Field(top / a for a in self.parts)


class Shifts:
    def __init__(self):
        lane = lax.broadcasted_iota(jnp.int32, (SUBS, LANES), 1)
        sub = lax.broadcasted_iota(jnp.int32, (SUBS, LANES), 0)
        self.first_lane = lane == 0
        self.last_lane = lane == LANES - 1
        self.first_sub = sub == 0
        self.last_sub = sub == SUBS - 1

    def east(self, field):
        r = [pltpu.roll(t, LANES - 1, 1) for t in field.parts]
        return Field(jnp.where(self.last_lane, r[k ^ 1], r[k]) for k in range(4))

    def west(self, field):
        r = [pltpu.roll(t, 1, 1) for t in field.parts]
        return Field(jnp.where(self.first_lane, r[k ^ 1], r[k]) for k in range(4))

    def above(self, field):
        r = [pltpu.roll(t, SUBS - 1, 0) for t in field.parts]
        low = [jnp.where(self.last_sub, r[2 + k], r[k]) for k in range(2)]
        return Field(low + [jnp.where(self.last_sub, 0.0, r[2 + k]) for k in range(2)])

    def below(self, field):
        r = [pltpu.roll(t, 1, 0) for t in field.parts]
        low = [jnp.where(self.first_sub, 0.0, r[k]) for k in range(2)]
        return Field(low + [jnp.where(self.first_sub, r[k], r[2 + k]) for k in range(2)])


def get(ref, row, c):
    return Field(ref[row, c, k] for k in range(4))


def put(ref, row, c, field):
    for k in range(4):
        ref[row, c, k] = field.parts[k]


def loop(start, stop, body):
    lax.fori_loop(start, stop, lambda i, c: (body(i), c)[1], 0)


def depth_rows(y, z):
    return pl.ds(z * SUBS * SUBS + y, SUBS, stride=SUBS)


def strip_kernel(
    rhs_in, mat_in, diag_in, off_in, strip_ref, cells_ref, table_ref,
    rhs_ref, mat_ref, diag_ref, off_ref, arrived,
):
    pairs = ((mat_in, mat_ref), (rhs_in, rhs_ref), (diag_in, diag_ref), (off_in, off_ref))
    copies = [pltpu.make_async_copy(f, t, arrived.at[k]) for k, (f, t) in enumerate(pairs)]
    for copy in copies:
        copy.start()
    for copy in copies:
        copy.wait()
    lane = lax.broadcasted_iota(jnp.int32, (SUBS, LANES), 1)
    half = STRIP // 2

    def packed(tiles, offset):
        result = None
        for r, tile in enumerate(tiles):
            shift = (STRIP * r + offset) % LANES
            moved_tile = pltpu.roll(tile, shift, 1) if shift else tile
            result = moved_tile if r == 0 else jnp.where(lane >= STRIP * r, moved_tile, result)
        return result

    for z in range(2):
        cells = [mat_ref[depth_rows(r, z), :].astype(jnp.float32) for r in range(SUBS)]
        for r in range(SUBS):
            cells_ref[2 * r + z] = cells[r]
        strip_ref[12 + z] = packed(cells, half)
        strip_ref[14 + z] = packed(cells, 0)
        for c in range(6):
            strip_ref[2 * c + z] = packed([rhs_ref[c, depth_rows(r, z), :] for r in range(SUBS)], half)
    x, n, d = [jnp.broadcast_to(0.5 * diag_ref[c : c + 1, :], (SUBS, SUBS)) for c in range(3)]
    entries = [x, n, d]
    for c, (f, g) in enumerate(((x, n), (x, d), (n, d))):
        entries.append(jnp.broadcast_to(off_ref[c : c + 1, :], (SUBS, SUBS)) * jnp.sqrt(f * g))
    for c in range(6):
        table_ref[c, :, :] = jnp.zeros((SUBS, LANES), jnp.float32)
        table_ref[c, :, :SUBS] = entries[c]
    for c in range(6):
        single = table_ref[c]
        table_ref[c] = jnp.take_along_axis(single, lane // SUBS, axis=1) + jnp.take_along_axis(
            single, lane % SUBS, axis=1
        )


def wavefront(stages, events=()):
    edges = {e + lag for _, start, stop, lag in stages for e in (start, stop)}
    edges = sorted(edges | {at for at, _ in events})
    for start, stop in zip(edges, edges[1:]):
        for at, body in events:
            if at == start:
                body()
        active = [st for st in stages if st[1] + st[3] <= start and stop <= st[2] + st[3]]

        def step(s, active=active):
            for body, _, _, lag in reversed(active):
                body(s - lag)

        loop(start, stop, step)


def iterate(sh, v, out, u, keep, s2, coef, z1, t1, p, node, flux, a, b):
    def fluxes(e, above_row):
        bx = (above_row[1] - e[2]) - (sh.above(e[1]) - e[1])
        by = (sh.above(e[0]) - e[0]) - (sh.east(e[2]) - e[2])
        bz = (sh.east(e[1]) - e[1]) - (above_row[0] - e[0])
        return bx, by, bz

    def curl(row, e, e_next):
        result = []
        for part in range(2):
            here = [e[2 * c + part] for c in range(3)]
            bx, by, bz = fluxes(here, (e_next[part], e_next[4 + part]))
            pbx, pbz = get(flux, row, 2 * part), get(flux, row, 2 * part + 1)
            put(flux, row + 1, 2 * part, bx)
            put(flux, row + 1, 2 * part + 1, bz)
            result.append(
                (
                    (pbz - bz) - (sh.below(by) - by),
                    (sh.below(bx) - bx) - (sh.west(bz) - bz),
                    (sh.west(by) - by) - (pbx - bx),
                )
            )
        return [result[k % 2][k // 2] for k in range(6)]

    def tensor(row, e):
        s = [get(s2, row, c) for c in range(6)]
        return [
            s[0] * e[0] + s[3] * e[1] + s[4] * e[2],
            s[3] * e[0] + s[1] * e[1] + s[5] * e[2],
            s[4] * e[0] + s[5] * e[1] + s[2] * e[2],
        ]

    def operator(row, e, e_next):
        k = curl(row, e, e_next)
        si = tensor(row, e[1::2])
        sr = tensor(row, e[0::2])
        return [k[j] - si[j // 2] if j % 2 == 0 else k[j] + sr[j // 2] for j in range(6)]

    def jacobi(row, e, scale):
        result = []
        for c in range(3):
            alpha, beta = get(coef, row, c), get(coef, row, 3 + c)
            result.append(scale * (alpha * e[2 * c] + beta * e[2 * c + 1]))
            result.append(scale * (alpha * e[2 * c + 1] - beta * e[2 * c]))
        return result

    def nodal(row, q, scale):
        alpha, beta = get(coef, row, 6), get(coef, row, 7)
        return [scale * (alpha * q[0] + beta * q[1]), scale * (alpha * q[1] - beta * q[0])]

    def load(ref, row, n=6):
        return [get(ref, row, c) for c in range(n)]

    def store(ref, row, values, base=0):
        for c, value in enumerate(values):
            put(ref, row, base + c, value)

    def zeroth(y):
        store(z1, y, jacobi(y, load(v, y), 0.7))

    def first(y):
        ahead = jacobi(y + 1, load(v, y + 1), 0.7)
        store(z1, y + 1, ahead)
        applied = operator(y, load(z1, y), ahead)
        rest = [r - w for r, w in zip(load(v, y), applied)]
        store(t1, y, rest)
        store(p, y, jacobi(y, rest, 0.6))

    def second(y):
        applied = operator(y, load(p, y), load(p, y + 1))
        rest = [r - w for r, w in zip(load(t1, y), applied)]
        source = []
        for part in range(2):
            x, n, d = rest[part], rest[2 + part], rest[4 + part]
            before = get(node, y, 6 + part)
            put(node, y + 1, 6 + part, n)
            source.append(((sh.west(x) - x) + (before - n)) + (sh.below(d) - d))
        store(node, y, source)
        store(node, y, nodal(y, source, 0.8), 2)

    def third(y):
        w = [get(node, y, 2 + part) for part in range(2)]
        slopes = []
        for part in range(2):
            ahead = get(node, y + 1, 2 + part)
            slopes.append((sh.east(w[part]) - w[part], ahead - w[part], sh.above(w[part]) - w[part]))
        si = tensor(y, slopes[1])
        sr = tensor(y, slopes[0])
        rest = []
        for part in range(2):
            if part == 0:
                x, n, d = [g - s for g, s in zip(slopes[0], si)]
            else:
                x, n, d = [g + s for g, s in zip(slopes[1], sr)]
            before = get(node, y, 6 + part)
            put(node, y + 1, 6 + part, n)
            applied = ((sh.west(x) - x) + (before - n)) + (sh.below(d) - d)
            rest.append(get(node, y, part) - applied)
        fix = nodal(y, rest, 0.5)
        store(node, y, [w[part] + fix[part] for part in range(2)], 4)

    def lift(y):
        w = [get(node, y, 4 + part) for part in range(2)]
        result = []
        for c in range(3):
            for part in range(2):
                k = 2 * c + part
                if c == 0:
                    slope = sh.east(w[part]) - w[part]
                elif c == 1:
                    slope = get(node, y + 1, 4 + part) - w[part]
                else:
                    slope = sh.above(w[part]) - w[part]
                result.append((get(z1, y, k) + get(p, y, k)) + slope)
        store(u, y, result)
        for k in range(6):
            for z in range(2):
                keep[y, k, z] = result[k].parts[2 * z]
        return result

    def fourth(y):
        ahead = lift(y + 1)
        store(out, y, operator(y, load(u, y), ahead))

    return [
        (zeroth, a, a + 1, 0),
        (first, a, b - 1, 1),
        (second, a + 1, b - 2, 3),
        (third, a + 2, b - 3, 5),
        (lift, a + 3, a + 4, 7),
        (fourth, a + 3, b - 4, 8),
    ]


def two_sum(a, b):
    s = a + b
    t = s - a
    return s, (a - (s - t)) + (b - t)


def main_kernel(
    odd_ref, own_ref, first_ref, second_ref, own_pack_ref, first_pack_ref, second_pack_ref, last_ref, table_ref,
    a0_ref, a1_ref, sums_ref,
    v, c0, c1, u, mat, index, pair, s2, coef, z1, t1, p, node, flux,
    keep0, keep1, bulk, packs, last, table, arrived, left,
):
    sh = Shifts()
    lane = lax.broadcasted_iota(jnp.int32, (SUBS, LANES), 1)
    sub = lax.broadcasted_iota(jnp.int32, (SUBS, LANES), 0)
    odd = odd_ref[0]
    first, second = 2 - 2 * odd, 2 * odd
    for ref, slot in ((second_pack_ref, second), (first_pack_ref, first), (own_pack_ref, 1)):
        pltpu.make_async_copy(ref, packs.at[slot], arrived.at[slot]).start()
    for ref, slot in ((second_ref, second), (first_ref, first), (own_ref, 1)):
        pltpu.make_async_copy(ref, bulk.at[slot], arrived.at[3 + slot]).start()
    last_copy = pltpu.make_async_copy(last_ref, last, arrived.at[6])
    table_copy = pltpu.make_async_copy(table_ref, table, arrived.at[7])
    last_copy.start()
    table_copy.start()

    def await_group(slot):
        def body():
            pltpu.make_async_copy(own_pack_ref, packs.at[slot], arrived.at[slot]).wait()
            pltpu.make_async_copy(own_ref, bulk.at[slot], arrived.at[3 + slot]).wait()

        return body

    def spread(strip, r):
        return pltpu.roll(strip, lax.rem(2 * LANES - STRIP // 2 - STRIP * r, LANES), 1)

    def cell_halo(strip, beyond_strip, r):
        ninth = pltpu.roll(beyond_strip, lax.rem(LANES - STRIP * r, LANES), 1)
        return jnp.where(lane == STRIP // 2, ninth, spread(strip, r))

    def unpack(group):
        def body(y):
            r = y - group * SUBS
            for z in range(2):
                for c in range(6):
                    v[y, c, 2 * z] = bulk[group, c, depth_rows(r, z), :]
                    v[y, c, 2 * z + 1] = spread(packs[group, 2 * c + z], r)
                mat[y, 2 * z] = packs[group, 16 + 2 * r + z]
                mat[y, 2 * z + 1] = cell_halo(packs[group, 12 + z], packs[group, 14 + z], r)

        return (body, group * SUBS, group * SUBS + SUBS, 0)

    def beyond(y):
        for z in range(2):
            mat[y, 2 * z] = last[4 + z]
            mat[y, 2 * z + 1] = cell_halo(last[z], last[2 + z], 0)

    def indices(y):
        ids = Field(mat[y, k] for k in range(4))
        both = 8.0 * ids + sh.east(ids)
        for k in range(4):
            index[y, k] = both.parts[k].astype(jnp.int32)

    def pairs(y):
        for k in range(4):
            which = index[y, k]
            for c in range(6):
                pair[y, c, k] = jnp.take_along_axis(table[c], which, axis=1)

    def tensors(y):
        s = [get(pair, y, c) + get(pair, y + 1, c) for c in range(6)]
        for c in range(6):
            put(s2, y, c, s[c])
        for c in range(3):
            inverse = 1.0 / (s[c] * s[c] + 16.0)
            put(coef, y, c, 4.0 * inverse)
            put(coef, y, 3 + c, s[c] * inverse)
        shift = 2.0 * ((s[0] + s[1]) + s[2])
        inverse = 1.0 / (shift * shift + 36.0)
        put(coef, y, 6, 6.0 * inverse)
        put(coef, y, 7, shift * inverse)

    wavefront(
        [
            unpack(0),
            unpack(1),
            unpack(2),
            (beyond, ROWS, ROWS + 1, 0),
            (indices, 0, ROWS + 1, 1),
            (pairs, 0, ROWS + 1, 2),
            (tensors, 0, ROWS, 4),
        ],
        [
            (0, await_group(0)),
            (1, table_copy.wait),
            (SUBS, await_group(1)),
            (2 * SUBS, await_group(2)),
            (ROWS, last_copy.wait),
        ],
    )
    own = pl.ds(HALO, SUBS)
    wavefront(iterate(sh, v, c0, u, keep0, s2, coef, z1, t1, p, node, flux, 0, ROWS))
    first_out = pltpu.make_async_copy(keep0.at[own], a0_ref, left.at[0])
    first_out.start()
    wavefront(
        iterate(sh, c0, c1, u, keep1, s2, coef, z1, t1, p, node, flux, REACH, ROWS - REACH)
    )
    second_out = pltpu.make_async_copy(keep1.at[own], a1_ref, left.at[1])
    second_out.start()

    def dots(r, sums):
        y = HALO + r
        sums = list(sums)
        for c in range(6):
            for z in range(2):
                f, g, h = v[y, c, 2 * z], c0[y, c, 2 * z], c1[y, c, 2 * z]
                for k, term in enumerate((f * f, f * g, g * g, f * h, g * h, h * h)):
                    sums[k] = sums[k] + term
        return tuple(sums)

    zero = jnp.zeros((SUBS, LANES), jnp.float32)
    sums = lax.fori_loop(0, SUBS, dots, (zero,) * 6)
    row = zero
    for k, total in enumerate(sums):
        for step in (4, 2, 1):
            total = total + pltpu.roll(total, step, 0)
        row = jnp.where(sub == k, total, row)
    row = jnp.broadcast_to(jnp.sum(row, axis=1, keepdims=True), (SUBS, LANES))
    row = jnp.where(lane == sub, row, 0.0)
    for step in (4, 2, 1):
        row = row + pltpu.roll(row, step, 0)
    for k in range(16):
        sums_ref[pl.ds(k * SUBS, SUBS), :] = row
    first_out.wait()
    second_out.wait()


def two_sum(a, b):
    s = a + b
    t = s - a
    return s, (a - (s - t)) + (b - t)


def two_product(a, b):
    def split(x):
        t = 4097.0 * x
        high = t - (t - x)
        return high, x - high

    p = a * b
    ah, al = split(a)
    bh, bl = split(b)
    return p, ((ah * bh - p) + ah * bl + al * bh) + al * bl


def quick(s, e):
    t = s + e
    return t, e - (t - s)


def plus(x, y):
    s, e = two_sum(x[0], y[0])
    return quick(s, e + (x[1] + y[1]))


def minus(x, y):
    return plus(x, (-y[0], -y[1]))


def times(x, y):
    p, e = two_product(x[0], y[0])
    return quick(p, e + (x[0] * y[1] + x[1] * y[0]))


def scaled(x, factor):
    p, e = two_product(x[0], jnp.full_like(x[0], factor))
    return quick(p, e + x[1] * factor)


def over(x, y):
    q = x[0] / y[0]
    r = minus(x, times(y, (q, jnp.zeros_like(q))))
    return quick(q, (r[0] + r[1]) / y[0])


def final_kernel(sums_ref, a0_ref, a1_ref, result_ref, hess_ref, out, a0, a1, done):
    lane = lax.broadcasted_iota(jnp.int32, (SUBS, LANES), 1)
    sub = lax.broadcasted_iota(jnp.int32, (SUBS, LANES), 0)
    arriving = [
        pltpu.make_async_copy(a0_ref, a0, done.at[6]),
        pltpu.make_async_copy(a1_ref, a1, done.at[7]),
    ]
    for copy in arriving:
        copy.start()
    level = [(sums_ref[pl.ds(k * SUBS, SUBS), :], None) for k in range(16)]
    while len(level) > 1:
        pairs = []
        for (f, f_rest), (g, g_rest) in zip(level[::2], level[1::2]):
            total, error = two_sum(f, g)
            pairs.append((total, error if f_rest is None else error + (f_rest + g_rest)))
        level = pairs
    total, rest = level[0]
    for step in (4, 2, 1):
        total, error = two_sum(total, pltpu.roll(total, step, 0))
        rest = rest + pltpu.roll(rest, step, 0) + error

    def columns(values):
        picked = jnp.sum(jnp.where(lane == sub, values, 0.0), axis=1, keepdims=True)
        return [jnp.broadcast_to(picked[k : k + 1], (SUBS, LANES)) for k in range(6)]

    bb, bc, cc, bd, cd, dd = [quick(f, g) for f, g in zip(columns(total), columns(rest))]
    eps = (jnp.full((SUBS, LANES), epsilon, jnp.float32), jnp.zeros((SUBS, LANES), jnp.float32))
    beta2 = plus(bb, eps)
    h00 = over(bc, beta2)
    norm1 = minus(minus(cc, times(h00, bc)), times(eps, times(h00, h00)))
    norm1 = (jnp.maximum(norm1[0], 0.0), jnp.where(norm1[0] > 0.0, norm1[1], 0.0))
    tall = plus(norm1, times(eps, beta2))
    x = minus(bd, times(h00, bc))
    y = plus(minus(minus(cd, times(h00, cc)), times(h00, bd)), times(times(h00, h00), bc))
    x_over = over(x, beta2)
    y_over = over(y, tall)
    norm2 = plus(minus(dd, scaled(times(h00, cd), 2.0)), times(times(h00, h00), cc))
    norm2 = minus(norm2, plus(times(x, x_over), times(eps, times(x_over, x_over))))
    norm2 = minus(norm2, plus(times(y, y_over), times(times(eps, beta2), times(y_over, y_over))))
    norm2 = plus(norm2, scaled(times(times(x_over, y_over), times(eps, h00)), 2.0))
    norm2 = over(norm2, tall)

    beta = jnp.sqrt(beta2[0])
    e00 = h00[0]
    e10 = jnp.sqrt(tall[0] / beta2[0])
    e01 = x_over[0] / e10
    e11 = y_over[0]
    e21 = jnp.sqrt(jnp.maximum(norm2[0], 0.0) + epsilon)

    g00 = e00 * e00 + e10 * e10
    g01 = e00 * e01 + e10 * e11
    g11 = e01 * e01 + e11 * e11 + e21 * e21
    l00 = jnp.sqrt(g00)
    l10 = g01 / l00
    l11 = jnp.sqrt(g11 - l10 * l10)
    m0 = beta * e00 / l00
    m1 = (beta * e01 - l10 * m0) / l11
    y1 = m1 / l11
    y0 = (m0 - l10 * y1) / l00
    k0 = (y0 - y1 * e00 / e10) / beta
    k1 = y1 / (e10 * beta)

    table = jnp.where(lane == 0, e00, jnp.where(lane == 1, e10, 0.0))
    later = jnp.where(lane == 0, e01, jnp.where(lane == 1, e11, e21))
    hess_ref[...] = jnp.where(sub == 0, table, later)[:2, :3]
    for copy in arriving:
        copy.wait()
    copies = []
    for c in range(6):
        for row in range(SUBS):
            for z in range(2):
                out[c, depth_rows(row, z), :] = k0 * a0[row, c, z] + k1 * a1[row, c, z]
        copies.append(pltpu.make_async_copy(out.at[c], result_ref.at[c], done.at[c]))
        copies[-1].start()
    for copy in copies:
        copy.wait()


VMEM = pl.BlockSpec(memory_space=pltpu.VMEM)
ANY = pl.BlockSpec(memory_space=pl.ANY)
SMEM = pl.BlockSpec(memory_space=pltpu.SMEM)


def call(kernel, outs, ins, scratch=(), semaphores=(), limit=VMEM_LIMIT):
    return pl.pallas_call(
        kernel,
        out_shape=[jax.ShapeDtypeStruct(shape, jnp.float32) for shape, _ in outs],
        in_specs=ins,
        out_specs=[spec for _, spec in outs],
        scratch_shapes=[pltpu.VMEM(shape, dtype) for shape, dtype in scratch]
        + [pltpu.SemaphoreType.DMA((n,)) for n in semaphores],
        compiler_params=pltpu.CompilerParams(vmem_limit_bytes=limit),
    )


def moved(value, axis, step):
    size = lax.axis_size(axis)
    return lax.ppermute(value, axis, [(i, (i + step) % size) for i in range(size)])


TILE = (SUBS, LANES)
KEPT = (SUBS, 6, 2) + TILE
BLOCK = (6, LANES, LANES)


def floats(*shapes):
    return [(shape, jnp.float32) for shape in shapes]


def rows(n, extra=0):
    return (ROWS + extra, n, 4) + TILE


def strip_call():
    return call(
        strip_kernel,
        [((16,) + TILE, VMEM), ((16,) + TILE, VMEM), ((6,) + TILE, VMEM)],
        [ANY] * 4,
        floats(BLOCK) + [((LANES, LANES), jnp.int32)] + floats((3, SUBS), (3, SUBS)),
        (4,),
        60 * 2**20,
    )


def main_call():
    return call(
        main_kernel,
        [(KEPT, ANY), (KEPT, ANY), ((LANES, LANES), VMEM)],
        [SMEM] + [ANY] * 8,
        floats(*[rows(6)] * 4, (ROWS + 1, 4) + TILE)
        + [((ROWS + 1, 4) + TILE, jnp.int32)]
        + floats(rows(6, 1), rows(6), rows(8), *[rows(6)] * 3, rows(8, 1), rows(4, 1))
        + floats((ROWS, 6, 2) + TILE, (ROWS, 6, 2) + TILE)
        + floats((3,) + BLOCK, (3, PACK) + TILE, (6,) + TILE, (6,) + TILE),
        (8, 2),
    )


def final_call():
    return call(
        final_kernel,
        [(BLOCK, ANY), ((2, 3), VMEM)],
        [VMEM, ANY, ANY],
        floats(BLOCK, KEPT, KEPT),
        (8,),
    )


def swapped(value, axis):
    size = lax.axis_size(axis)
    pairs = [(i, i ^ 1) for i in range(size)]
    others = [((i + 1) % size, (j + 1) % size) for i, j in pairs]
    second = lax.ppermute(value, axis, others)
    return lax.ppermute(value, axis, pairs), second


def on_device(right_side, materials, sigma_diag, sigma_off):
    rhs = right_side.reshape(BLOCK)
    bulk = swapped(rhs, "gy")
    strips, cells, table = strip_call()(
        rhs, materials.reshape(LANES, LANES), sigma_diag, sigma_off
    )
    first, second = swapped(strips, "gx")
    odd = lax.axis_index("gx") % 2 == 1
    lane = lax.broadcasted_iota(jnp.int32, (14,) + TILE, 2)
    mixed = jnp.where((lane % STRIP < STRIP // 2) == odd, first[:14], second[:14])
    pack = jnp.concatenate([mixed, jnp.where(odd, second[14:], first[14:]), cells])
    packs = swapped(pack, "gy")
    last = moved(pack[12:18], "gy", -2)
    a0, a1, sums = main_call()(
        lax.axis_index("gy").reshape(1) % 2, rhs, *bulk, pack, *packs, last, table
    )
    gathered = lax.all_to_all(sums, ("gx", "gy"), 0, 0, tiled=True)
    result, hessenberg = final_call()(gathered, a0, a1)
    return result.reshape(right_side.shape), hessenberg.T


def solution(mesh):
    return jax.shard_map(
        on_device,
        mesh=mesh,
        in_specs=(P(None, None, None, "gy", "gx"), P(None, "gy", "gx"), P(), P()),
        out_specs=(P(None, None, None, "gy", "gx"), P()),
        check_vma=False,
    )
```

```python
import jax
import jax.numpy as jnp
from jax import lax
from jax.experimental import pallas as pl
from jax.experimental.pallas import tpu as pltpu
from jax.sharding import PartitionSpec as P

epsilon = 1e-06
LANES = 128
SUBS = 8
REACH = 4
HALO = 2 * REACH
ROWS = SUBS + 2 * HALO
HALF = LANES // 2
STRIP = 16
PACK = 32
VMEM_LIMIT = 44 * 2**20


class Field:
    def __init__(self, parts):
        self.parts = tuple(parts)

    def zip(self, other, op):
        if isinstance(other, Field):
            return Field(op(a, b) for a, b in zip(self.parts, other.parts))
        return Field(op(a, other) for a in self.parts)

    def __add__(self, other):
        return self.zip(other, lambda a, b: a + b)

    def __sub__(self, other):
        return self.zip(other, lambda a, b: a - b)

    def __mul__(self, other):
        return self.zip(other, lambda a, b: a * b)

    __rmul__ = __mul__

    def __rtruediv__(self, top):
        return Field(top / a for a in self.parts)


class Shifts:
    def __init__(self):
        lane = lax.broadcasted_iota(jnp.int32, (SUBS, LANES), 1)
        sub = lax.broadcasted_iota(jnp.int32, (SUBS, LANES), 0)
        low = lane < HALF
        self.first, self.last = sub == 0, sub == SUBS - 1
        self.first_low, self.first_high = self.first & low, self.first & ~low
        self.last_low, self.last_high = self.last & low, self.last & ~low

    def east(self, field):
        return Field(pltpu.roll(t, LANES - 1, 1) for t in field.parts)

    def west(self, field):
        return Field(pltpu.roll(t, 1, 1) for t in field.parts)

    def above(self, field):
        r = [pltpu.roll(t, SUBS - 1, 0) for t in field.parts]
        other = pltpu.roll(r[2], HALF, 1)
        outer = jnp.where(self.last_low, other, jnp.where(self.last_high, 0.0, r[2]))
        return Field([jnp.where(self.last, r[1], r[0]), jnp.where(self.last, 0.0, r[1]), outer])

    def below(self, field):
        r = [pltpu.roll(t, 1, 0) for t in field.parts]
        other = pltpu.roll(r[2], HALF, 1)
        outer = jnp.where(self.first_high, other, jnp.where(self.first_low, 0.0, r[2]))
        return Field([jnp.where(self.first, 0.0, r[0]), jnp.where(self.first, r[0], r[1]), outer])


def outer_columns(own, halo):
    lane = lax.broadcasted_iota(jnp.int32, (SUBS, LANES), 1)
    pieces = []
    for z in range(2):
        start = jnp.where(lane >= LANES - HALO, halo[z], own[z])
        end = jnp.where(lane < HALO, halo[z], own[z])
        pieces.append(pltpu.roll(start, HALO + HALF * z, 1))
        pieces.append(pltpu.roll(end, 5 * HALO + HALF * z, 1))
    low = jnp.where(lane < 3 * HALO, pieces[0], pieces[1])
    high = jnp.where(lane < HALF + 3 * HALO, pieces[2], pieces[3])
    return jnp.where(lane < HALF, low, high)


def get(ref, row, c):
    return Field(ref[row, c, k] for k in range(3))


def put(ref, row, c, field):
    for k in range(3):
        ref[row, c, k] = field.parts[k]


def loop(start, stop, body):
    lax.fori_loop(start, stop, lambda i, c: (body(i), c)[1], 0)


def depth_rows(y, z):
    return pl.ds(z * SUBS * SUBS + y, SUBS, stride=SUBS)


def strip_kernel(
    rhs_in, mat_in, diag_in, off_in, strip_ref, table_ref, rhs_ref, mat_ref, diag_ref, off_ref, arrived
):
    lane = lax.broadcasted_iota(jnp.int32, (SUBS, LANES), 1)
    half = STRIP // 2
    pairs = [(diag_in, diag_ref), (off_in, off_ref), (mat_in, mat_ref)]
    pairs += [(rhs_in.at[c], rhs_ref.at[c]) for c in range(6)]
    copies = [pltpu.make_async_copy(f, t, arrived.at[k]) for k, (f, t) in enumerate(pairs)]
    for copy in copies:
        copy.start()

    def packed(tiles, offset):
        result = None
        for r, tile in enumerate(tiles):
            shift = (STRIP * r + offset) % LANES
            moved_tile = pltpu.roll(tile, shift, 1) if shift else tile
            result = moved_tile if r == 0 else jnp.where(lane >= STRIP * r, moved_tile, result)
        return result

    copies[0].wait()
    copies[1].wait()
    copies[2].wait()
    for z in range(2):
        cells = [mat_ref[depth_rows(r, z), :].astype(jnp.float32) for r in range(SUBS)]
        strip_ref[12 + z] = packed(cells, half)
        strip_ref[14 + z] = packed(cells, 0)
    for c in range(6):
        copies[3 + c].wait()
        for z in range(2):
            strip_ref[2 * c + z] = packed([rhs_ref[c, depth_rows(r, z), :] for r in range(SUBS)], half)
    x, n, d = [jnp.broadcast_to(0.5 * diag_ref[c : c + 1, :], (SUBS, SUBS)) for c in range(3)]
    entries = [x, n, d]
    for c, (f, g) in enumerate(((x, n), (x, d), (n, d))):
        entries.append(jnp.broadcast_to(off_ref[c : c + 1, :], (SUBS, SUBS)) * jnp.sqrt(f * g))
    for c in range(6):
        table_ref[c, :, :] = jnp.zeros((SUBS, LANES), jnp.float32)
        table_ref[c, :, :SUBS] = entries[c]
    for c in range(6):
        single = table_ref[c]
        table_ref[c] = jnp.take_along_axis(single, lane // SUBS, axis=1) + jnp.take_along_axis(
            single, lane % SUBS, axis=1
        )


def wavefront(stages, events=()):
    edges = {e + lag for _, start, stop, lag in stages for e in (start, stop)}
    edges = sorted(edges | {at for at, _ in events})
    for start, stop in zip(edges, edges[1:]):
        for at, body in events:
            if at == start:
                body()
        active = [st for st in stages if st[1] + st[3] <= start and stop <= st[2] + st[3]]

        def step(s, active=active):
            for body, _, _, lag in reversed(active):
                body(s - lag)

        loop(start, stop, step)


def iterate(sh, v, out, u, keep, s2, coef, z1, t1, p, node, flux, a, b, wait=0):
    def fluxes(e, above_row):
        bx = (above_row[1] - e[2]) - (sh.above(e[1]) - e[1])
        by = (sh.above(e[0]) - e[0]) - (sh.east(e[2]) - e[2])
        bz = (sh.east(e[1]) - e[1]) - (above_row[0] - e[0])
        return bx, by, bz

    def curl(row, e, e_next):
        result = []
        for part in range(2):
            here = [e[2 * c + part] for c in range(3)]
            bx, by, bz = fluxes(here, (e_next[part], e_next[4 + part]))
            pbx, pbz = get(flux, row, 2 * part), get(flux, row, 2 * part + 1)
            put(flux, row + 1, 2 * part, bx)
            put(flux, row + 1, 2 * part + 1, bz)
            result.append(
                (
                    (pbz - bz) - (sh.below(by) - by),
                    (sh.below(bx) - bx) - (sh.west(bz) - bz),
                    (sh.west(by) - by) - (pbx - bx),
                )
            )
        return [result[k % 2][k // 2] for k in range(6)]

    def tensor(row, e):
        s = [get(s2, row, c) for c in range(6)]
        return [
            s[0] * e[0] + s[3] * e[1] + s[4] * e[2],
            s[3] * e[0] + s[1] * e[1] + s[5] * e[2],
            s[4] * e[0] + s[5] * e[1] + s[2] * e[2],
        ]

    def operator(row, e, e_next):
        k = curl(row, e, e_next)
        si = tensor(row, e[1::2])
        sr = tensor(row, e[0::2])
        return [k[j] - si[j // 2] if j % 2 == 0 else k[j] + sr[j // 2] for j in range(6)]

    def jacobi(row, e, scale):
        result = []
        for c in range(3):
            alpha, beta = get(coef, row, c), get(coef, row, 3 + c)
            result.append(scale * (alpha * e[2 * c] + beta * e[2 * c + 1]))
            result.append(scale * (alpha * e[2 * c + 1] - beta * e[2 * c]))
        return result

    def nodal(row, q, scale):
        alpha, beta = get(coef, row, 6), get(coef, row, 7)
        return [scale * (alpha * q[0] + beta * q[1]), scale * (alpha * q[1] - beta * q[0])]

    def load(ref, row, n=6):
        return [get(ref, row, c) for c in range(n)]

    def store(ref, row, values, base=0):
        for c, value in enumerate(values):
            put(ref, row, base + c, value)

    def zeroth(y):
        store(z1, y, jacobi(y, load(v, y), 0.7))

    def first(y):
        ahead = jacobi(y + 1, load(v, y + 1), 0.7)
        store(z1, y + 1, ahead)
        applied = operator(y, load(z1, y), ahead)
        rest = [r - w for r, w in zip(load(v, y), applied)]
        store(t1, y, rest)
        store(p, y, jacobi(y, rest, 0.6))

    def second(y):
        applied = operator(y, load(p, y), load(p, y + 1))
        rest = [r - w for r, w in zip(load(t1, y), applied)]
        source = []
        for part in range(2):
            x, n, d = rest[part], rest[2 + part], rest[4 + part]
            before = get(node, y, 6 + part)
            put(node, y + 1, 6 + part, n)
            source.append(((sh.west(x) - x) + (before - n)) + (sh.below(d) - d))
        store(node, y, source)
        store(node, y, nodal(y, source, 0.8), 2)

    def third(y):
        w = [get(node, y, 2 + part) for part in range(2)]
        slopes = []
        for part in range(2):
            ahead = get(node, y + 1, 2 + part)
            slopes.append((sh.east(w[part]) - w[part], ahead - w[part], sh.above(w[part]) - w[part]))
        si = tensor(y, slopes[1])
        sr = tensor(y, slopes[0])
        rest = []
        for part in range(2):
            if part == 0:
                x, n, d = [g - s for g, s in zip(slopes[0], si)]
            else:
                x, n, d = [g + s for g, s in zip(slopes[1], sr)]
            before = get(node, y, 6 + part)
            put(node, y + 1, 6 + part, n)
            applied = ((sh.west(x) - x) + (before - n)) + (sh.below(d) - d)
            rest.append(get(node, y, part) - applied)
        fix = nodal(y, rest, 0.5)
        store(node, y, [w[part] + fix[part] for part in range(2)], 4)

    def lift(y):
        w = [get(node, y, 4 + part) for part in range(2)]
        result = []
        for c in range(3):
            for part in range(2):
                k = 2 * c + part
                if c == 0:
                    slope = sh.east(w[part]) - w[part]
                elif c == 1:
                    slope = get(node, y + 1, 4 + part) - w[part]
                else:
                    slope = sh.above(w[part]) - w[part]
                result.append((get(z1, y, k) + get(p, y, k)) + slope)
        store(u, y, result)
        return result

    def fourth(y):
        ahead = lift(y + 1)
        store(out, y, operator(y, load(u, y), ahead))

    def merge(y):
        lane = lax.broadcasted_iota(jnp.int32, (SUBS, LANES), 1)
        for c in range(6):
            outer = u[y, c, 2]
            for z in range(2):
                start = pltpu.roll(outer, (LANES - HALO - HALF * z) % LANES, 1)
                end = pltpu.roll(outer, (11 * HALO - HALF * z) % LANES, 1)
                inner = jnp.where(lane < HALO, start, u[y, c, z])
                keep[y - HALO, c, z] = jnp.where(lane >= LANES - HALO, end, inner)

    return [
        (zeroth, a, a + 1, wait),
        (first, a, b - 1, wait + 1),
        (second, a + 1, b - 2, wait + 3),
        (third, a + 2, b - 3, wait + 5),
        (lift, a + 3, a + 4, wait + 7),
        (fourth, a + 3, b - 4, wait + 8),
        (merge, HALO, HALO + SUBS, wait + 9),
    ]


def main_kernel(
    odd_ref, own_ref, first_ref, second_ref, own_pack_ref, first_pack_ref, second_pack_ref, last_ref, table_ref,
    a0_ref, a1_ref, sums_ref,
    v, c0, c1, u, mat, index, pair, s2, coef, z1, t1, p, node, flux,
    keep0, keep1, bulk, packs, last, table, arrived, left,
):
    sh = Shifts()
    lane = lax.broadcasted_iota(jnp.int32, (SUBS, LANES), 1)
    sub = lax.broadcasted_iota(jnp.int32, (SUBS, LANES), 0)
    odd = odd_ref[0]
    first, second = 2 - 2 * odd, 2 * odd
    for ref, slot in ((second_pack_ref, second), (first_pack_ref, first), (own_pack_ref, 1)):
        pltpu.make_async_copy(ref, packs.at[slot], arrived.at[slot]).start()
    for ref, slot in ((second_ref, second), (first_ref, first), (own_ref, 1)):
        pltpu.make_async_copy(ref, bulk.at[slot], arrived.at[3 + slot]).start()
    last_copy = pltpu.make_async_copy(last_ref, last, arrived.at[6])
    table_copy = pltpu.make_async_copy(table_ref, table, arrived.at[7])
    last_copy.start()
    table_copy.start()

    def await_group(slot):
        def body():
            pltpu.make_async_copy(own_pack_ref, packs.at[slot], arrived.at[slot]).wait()
            pltpu.make_async_copy(own_ref, bulk.at[slot], arrived.at[3 + slot]).wait()

        return body

    def spread(strip, r):
        return pltpu.roll(strip, lax.rem(2 * LANES - STRIP // 2 - STRIP * r, LANES), 1)

    def cell_halo(strip, beyond_strip, r):
        ninth = pltpu.roll(beyond_strip, lax.rem(LANES - STRIP * r, LANES), 1)
        return jnp.where(lane == STRIP // 2, ninth, spread(strip, r))

    def strip(group, k):
        return packs[group, pl.ds(SUBS * k, SUBS), :]

    def strip(group, k):
        return packs[group, pl.ds(SUBS * k, SUBS), :]

    def unpack(group):
        def body(y):
            r = y - group * SUBS
            for c in range(6):
                inner = [bulk[group, c, depth_rows(r, z), :] for z in range(2)]
                outer = outer_columns(inner, [spread(strip(group, 2 * c + z), r) for z in range(2)])
                put(v, y, c, Field(inner + [outer]))
            for z in range(2):
                mat[y, 2 * z] = packs[group, depth_rows(r, 2 + z), :]
                mat[y, 2 * z + 1] = cell_halo(strip(group, 12 + z), strip(group, 14 + z), r)

        return (body, group * SUBS, group * SUBS + SUBS, 0)

    def beyond(y):
        for z in range(2):
            mat[y, 2 * z] = last[4 + z]
            mat[y, 2 * z + 1] = cell_halo(last[z], last[2 + z], 0)

    def indices(y):
        ids = [mat[y, k] for k in range(4)]
        r = [pltpu.roll(t, LANES - 1, 1) for t in ids]
        both = [8.0 * ids[k] + jnp.where(lane == LANES - 1, r[k ^ 1], r[k]) for k in range(4)]
        inner = both[0::2]
        for k, part in enumerate(inner + [outer_columns(inner, both[1::2])]):
            index[y, k] = part.astype(jnp.int32)

    def pairs(y):
        for k in range(3):
            which = index[y, k]
            for c in range(6):
                pair[y, c, k] = jnp.take_along_axis(table[c], which, axis=1)

    def tensors(y):
        s = [get(pair, y, c) + get(pair, y + 1, c) for c in range(6)]
        for c in range(6):
            put(s2, y, c, s[c])
        for c in range(3):
            inverse = 1.0 / (s[c] * s[c] + 16.0)
            put(coef, y, c, 4.0 * inverse)
            put(coef, y, 3 + c, s[c] * inverse)
        shift = 2.0 * ((s[0] + s[1]) + s[2])
        inverse = 1.0 / (shift * shift + 36.0)
        put(coef, y, 6, 6.0 * inverse)
        put(coef, y, 7, shift * inverse)

    wavefront(
        [
            unpack(0),
            unpack(1),
            unpack(2),
            (beyond, ROWS, ROWS + 1, 0),
            (indices, 0, ROWS + 1, 1),
            (pairs, 0, ROWS + 1, 2),
            (tensors, 0, ROWS, 4),
        ]
        + iterate(sh, v, c0, u, keep0, s2, coef, z1, t1, p, node, flux, 0, ROWS, 5),
        [
            (0, await_group(0)),
            (2, table_copy.wait),
            (SUBS, await_group(1)),
            (2 * SUBS, await_group(2)),
            (ROWS, last_copy.wait),
        ],
    )
    first_out = pltpu.make_async_copy(keep0, a0_ref, left.at[0])
    first_out.start()
    wavefront(
        iterate(sh, c0, c1, u, keep1, s2, coef, z1, t1, p, node, flux, REACH, ROWS - REACH)
    )
    second_out = pltpu.make_async_copy(keep1, a1_ref, left.at[1])
    second_out.start()

    def dots(r, sums):
        y = HALO + r
        sums = list(sums)
        for c in range(6):
            for part in range(3):
                base = 6 if part == 2 else 0
                f, g, h = v[y, c, part], c0[y, c, part], c1[y, c, part]
                for k, term in enumerate((f * f, f * g, g * g, f * h, g * h, h * h)):
                    sums[base + k] = sums[base + k] + term
        return tuple(sums)

    zero = jnp.zeros((SUBS, LANES), jnp.float32)
    sums = lax.fori_loop(0, SUBS, dots, (zero,) * 12)
    inner = (lane >= HALO) & (lane < LANES - HALO)
    place = lane % HALF
    outer = ((place >= HALO) & (place < 2 * HALO)) | ((place >= 4 * HALO) & (place < 5 * HALO))
    row = zero
    for k in range(6):
        total = jnp.where(inner, sums[k], 0.0) + jnp.where(outer, sums[6 + k], 0.0)
        for step in (4, 2, 1):
            total = total + pltpu.roll(total, step, 0)
        row = jnp.where(sub == k, total, row)
    row = jnp.broadcast_to(jnp.sum(row, axis=1, keepdims=True), (SUBS, LANES))
    row = jnp.where(lane == sub, row, 0.0)
    for step in (4, 2, 1):
        row = row + pltpu.roll(row, step, 0)
    for k in range(16):
        sums_ref[pl.ds(k * SUBS, SUBS), :] = row
    first_out.wait()
    second_out.wait()


def two_sum(a, b):
    s = a + b
    t = s - a
    return s, (a - (s - t)) + (b - t)


def two_product(a, b):
    def split(x):
        t = 4097.0 * x
        high = t - (t - x)
        return high, x - high

    p = a * b
    ah, al = split(a)
    bh, bl = split(b)
    return p, ((ah * bh - p) + ah * bl + al * bh) + al * bl


def quick(s, e):
    t = s + e
    return t, e - (t - s)


def plus(x, y):
    s, e = two_sum(x[0], y[0])
    return quick(s, e + (x[1] + y[1]))


def minus(x, y):
    return plus(x, (-y[0], -y[1]))


def times(x, y):
    p, e = two_product(x[0], y[0])
    return quick(p, e + (x[0] * y[1] + x[1] * y[0]))


def scaled(x, factor):
    p, e = two_product(x[0], jnp.full_like(x[0], factor))
    return quick(p, e + x[1] * factor)


def over(x, y):
    q = x[0] / y[0]
    r = minus(x, times(y, (q, jnp.zeros_like(q))))
    return quick(q, (r[0] + r[1]) / y[0])


def final_kernel(sums_ref, a0_ref, a1_ref, result_ref, hess_ref, out, a0, a1, done):
    lane = lax.broadcasted_iota(jnp.int32, (SUBS, LANES), 1)
    sub = lax.broadcasted_iota(jnp.int32, (SUBS, LANES), 0)
    arriving = [
        pltpu.make_async_copy(a0_ref, a0, done.at[6]),
        pltpu.make_async_copy(a1_ref, a1, done.at[7]),
    ]
    for copy in arriving:
        copy.start()
    level = [(sums_ref[pl.ds(k * SUBS, SUBS), :], None) for k in range(16)]
    while len(level) > 1:
        pairs = []
        for (f, f_rest), (g, g_rest) in zip(level[::2], level[1::2]):
            total, error = two_sum(f, g)
            pairs.append((total, error if f_rest is None else error + (f_rest + g_rest)))
        level = pairs
    total, rest = level[0]
    for step in (4, 2, 1):
        total, error = two_sum(total, pltpu.roll(total, step, 0))
        rest = rest + pltpu.roll(rest, step, 0) + error

    def columns(values):
        picked = jnp.sum(jnp.where(lane == sub, values, 0.0), axis=1, keepdims=True)
        return [jnp.broadcast_to(picked[k : k + 1], (SUBS, LANES)) for k in range(6)]

    bb, bc, cc, bd, cd, dd = [quick(f, g) for f, g in zip(columns(total), columns(rest))]
    eps = (jnp.full((SUBS, LANES), epsilon, jnp.float32), jnp.zeros((SUBS, LANES), jnp.float32))
    beta2 = plus(bb, eps)
    h00 = over(bc, beta2)
    norm1 = minus(minus(cc, times(h00, bc)), times(eps, times(h00, h00)))
    norm1 = (jnp.maximum(norm1[0], 0.0), jnp.where(norm1[0] > 0.0, norm1[1], 0.0))
    tall = plus(norm1, times(eps, beta2))
    x = minus(bd, times(h00, bc))
    y = plus(minus(minus(cd, times(h00, cc)), times(h00, bd)), times(times(h00, h00), bc))
    x_over = over(x, beta2)
    y_over = over(y, tall)
    norm2 = plus(minus(dd, scaled(times(h00, cd), 2.0)), times(times(h00, h00), cc))
    norm2 = minus(norm2, plus(times(x, x_over), times(eps, times(x_over, x_over))))
    norm2 = minus(norm2, plus(times(y, y_over), times(times(eps, beta2), times(y_over, y_over))))
    norm2 = plus(norm2, scaled(times(times(x_over, y_over), times(eps, h00)), 2.0))
    norm2 = over(norm2, tall)

    beta = jnp.sqrt(beta2[0])
    e00 = h00[0]
    e10 = jnp.sqrt(tall[0] / beta2[0])
    e01 = x_over[0] / e10
    e11 = y_over[0]
    e21 = jnp.sqrt(jnp.maximum(norm2[0], 0.0) + epsilon)

    g00 = e00 * e00 + e10 * e10
    g01 = e00 * e01 + e10 * e11
    g11 = e01 * e01 + e11 * e11 + e21 * e21
    l00 = jnp.sqrt(g00)
    l10 = g01 / l00
    l11 = jnp.sqrt(g11 - l10 * l10)
    m0 = beta * e00 / l00
    m1 = (beta * e01 - l10 * m0) / l11
    y1 = m1 / l11
    y0 = (m0 - l10 * y1) / l00
    k0 = (y0 - y1 * e00 / e10) / beta
    k1 = y1 / (e10 * beta)

    table = jnp.where(lane == 0, e00, jnp.where(lane == 1, e10, 0.0))
    later = jnp.where(lane == 0, e01, jnp.where(lane == 1, e11, e21))
    hess_ref[...] = jnp.where(sub == 0, table, later)[:2, :3]
    for copy in arriving:
        copy.wait()
    copies = []
    for c in range(6):
        for row in range(SUBS):
            for z in range(2):
                out[c, depth_rows(row, z), :] = k0 * a0[row, c, z] + k1 * a1[row, c, z]
        copies.append(pltpu.make_async_copy(out.at[c], result_ref.at[c], done.at[c]))
        copies[-1].start()
    for copy in copies:
        copy.wait()


VMEM = pl.BlockSpec(memory_space=pltpu.VMEM)
ANY = pl.BlockSpec(memory_space=pl.ANY)
SMEM = pl.BlockSpec(memory_space=pltpu.SMEM)
HBM = pl.BlockSpec(memory_space=pltpu.HBM)


def call(kernel, outs, ins, scratch=(), semaphores=(), limit=VMEM_LIMIT):
    return pl.pallas_call(
        kernel,
        out_shape=[jax.ShapeDtypeStruct(shape, jnp.float32) for shape, _ in outs],
        in_specs=ins,
        out_specs=[spec for _, spec in outs],
        scratch_shapes=[pltpu.VMEM(shape, dtype) for shape, dtype in scratch]
        + [pltpu.SemaphoreType.DMA((n,)) for n in semaphores],
        compiler_params=pltpu.CompilerParams(vmem_limit_bytes=limit),
    )


def moved(value, axis, step):
    size = lax.axis_size(axis)
    return lax.ppermute(value, axis, [(i, (i + step) % size) for i in range(size)])


TILE = (SUBS, LANES)
KEPT = (SUBS, 6, 2) + TILE
BLOCK = (6, LANES, LANES)


def floats(*shapes):
    return [(shape, jnp.float32) for shape in shapes]


def rows(n, extra=0):
    return (ROWS + extra, n, 3) + TILE


def strip_call():
    return call(
        strip_kernel,
        [((16,) + TILE, VMEM), ((6,) + TILE, VMEM)],
        [HBM] * 4,
        floats(BLOCK) + [((LANES, LANES), jnp.int32)] + floats((3, SUBS), (3, SUBS)),
        (9,),
        60 * 2**20,
    )


def main_call():
    return call(
        main_kernel,
        [(KEPT, ANY), (KEPT, ANY), ((LANES, LANES), VMEM)],
        [SMEM, HBM] + [ANY] * 7,
        floats(*[rows(6)] * 4, (ROWS + 1, 4) + TILE)
        + [((ROWS + 1, 3) + TILE, jnp.int32)]
        + floats(rows(6, 1), rows(6), rows(8), *[rows(6)] * 3, rows(8, 1), rows(4, 1))
        + floats(KEPT, KEPT)
        + floats((3,) + BLOCK, (3, SUBS * PACK, LANES), (6,) + TILE, (6,) + TILE),
        (8, 2),
    )


def final_call():
    return call(
        final_kernel,
        [(BLOCK, ANY), ((2, 3), VMEM)],
        [VMEM, ANY, ANY],
        floats(BLOCK, KEPT, KEPT),
        (8,),
    )


def swapped(value, axis):
    size = lax.axis_size(axis)
    pairs = [(i, i ^ 1) for i in range(size)]
    others = [((i + 1) % size, (j + 1) % size) for i, j in pairs]
    second = lax.ppermute(value, axis, others)
    return lax.ppermute(value, axis, pairs), second


def on_device(right_side, materials, sigma_diag, sigma_off):
    rhs = right_side.reshape(BLOCK)
    bulk = swapped(rhs, "gy")
    strips, table = strip_call()(rhs, materials.reshape(LANES, LANES), sigma_diag, sigma_off)
    first_row = materials[:, 0, :].astype(jnp.float32).reshape((2,) + TILE)
    first, second = swapped(strips, "gx")
    odd = lax.axis_index("gx") % 2 == 1
    lane = lax.broadcasted_iota(jnp.int32, (14,) + TILE, 2)
    mixed = jnp.where((lane % STRIP < STRIP // 2) == odd, first[:14], second[:14])
    beyond = jnp.where(odd, second[14:], first[14:])
    last = moved(jnp.concatenate([mixed[12:], beyond, first_row]), "gy", -2)
    pack = jnp.concatenate([mixed, beyond, materials.astype(jnp.float32)])
    pack = pack.reshape(SUBS * PACK, LANES)
    packs = swapped(pack, "gy")
    a0, a1, sums = main_call()(
        lax.axis_index("gy").reshape(1) % 2, rhs, *bulk, pack, *packs, last, table
    )
    gathered = lax.all_to_all(sums, ("gx", "gy"), 0, 0, tiled=True)
    result, hessenberg = final_call()(gathered, a0, a1)
    return result.reshape(right_side.shape), hessenberg.T


def solution(mesh):
    return jax.shard_map(
        on_device,
        mesh=mesh,
        in_specs=(P(None, None, None, "gy", "gx"), P(None, "gy", "gx"), P(), P()),
        out_specs=(P(None, None, None, "gy", "gx"), P()),
        check_vma=False,
    )
```

```python
import jax
import jax.numpy as jnp
from jax import lax
from jax.experimental import pallas as pl
from jax.experimental.pallas import tpu as pltpu
from jax.sharding import PartitionSpec as P

epsilon = 1e-06
LANES = 128
SUBS = 8
REACH = 4
HALO = 2 * REACH
ROWS = SUBS + 2 * HALO
STRIP = 16
PACK = 32
VMEM_LIMIT = 44 * 2**20


class Field:
    def __init__(self, parts):
        self.parts = tuple(parts)

    def zip(self, other, op):
        if isinstance(other, Field):
            return Field(op(a, b) for a, b in zip(self.parts, other.parts))
        return Field(op(a, other) for a in self.parts)

    def __add__(self, other):
        return self.zip(other, lambda a, b: a + b)

    def __sub__(self, other):
        return self.zip(other, lambda a, b: a - b)

    def __mul__(self, other):
        return self.zip(other, lambda a, b: a * b)

    __rmul__ = __mul__

    def __rtruediv__(self, top):
        return Field(top / a for a in self.parts)


class Shifts:
    def __init__(self):
        lane = lax.broadcasted_iota(jnp.int32, (SUBS, LANES), 1)
        sub = lax.broadcasted_iota(jnp.int32, (SUBS, LANES), 0)
        self.first_lane = lane == 0
        self.last_lane = lane == LANES - 1
        self.first_sub = sub == 0
        self.last_sub = sub == SUBS - 1

    def east(self, field):
        r = [pltpu.roll(t, LANES - 1, 1) for t in field.parts]
        return Field(jnp.where(self.last_lane, r[k ^ 1], r[k]) for k in range(4))

    def west(self, field):
        r = [pltpu.roll(t, 1, 1) for t in field.parts]
        return Field(jnp.where(self.first_lane, r[k ^ 1], r[k]) for k in range(4))

    def above(self, field):
        r = [pltpu.roll(t, SUBS - 1, 0) for t in field.parts]
        low = [jnp.where(self.last_sub, r[2 + k], r[k]) for k in range(2)]
        return Field(low + [jnp.where(self.last_sub, 0.0, r[2 + k]) for k in range(2)])

    def below(self, field):
        r = [pltpu.roll(t, 1, 0) for t in field.parts]
        low = [jnp.where(self.first_sub, 0.0, r[k]) for k in range(2)]
        return Field(low + [jnp.where(self.first_sub, r[k], r[2 + k]) for k in range(2)])


def get(ref, row, c):
    return Field(ref[row, c, k] for k in range(4))


def put(ref, row, c, field):
    for k in range(4):
        ref[row, c, k] = field.parts[k]


def loop(start, stop, body):
    lax.fori_loop(start, stop, lambda i, c: (body(i), c)[1], 0)


def depth_rows(y, z):
    return pl.ds(z * SUBS * SUBS + y, SUBS, stride=SUBS)


def strip_kernel(
    rhs_in, mat_in, diag_in, off_in, strip_ref, cells_ref, table_ref, own_ref,
    rhs_ref, mat_ref, diag_ref, off_ref, arrived,
):
    pairs = ((mat_in, mat_ref), (rhs_in, rhs_ref), (diag_in, diag_ref), (off_in, off_ref))
    copies = [pltpu.make_async_copy(f, t, arrived.at[k]) for k, (f, t) in enumerate(pairs)]
    for copy in copies:
        copy.start()
    for copy in copies:
        copy.wait()
    own_copy = pltpu.make_async_copy(rhs_ref, own_ref, arrived.at[4])
    own_copy.start()
    lane = lax.broadcasted_iota(jnp.int32, (SUBS, LANES), 1)
    half = STRIP // 2

    def packed(tiles, offset):
        result = None
        for r, tile in enumerate(tiles):
            shift = (STRIP * r + offset) % LANES
            moved_tile = pltpu.roll(tile, shift, 1) if shift else tile
            result = moved_tile if r == 0 else jnp.where(lane >= STRIP * r, moved_tile, result)
        return result

    for z in range(2):
        cells = [mat_ref[depth_rows(r, z), :].astype(jnp.float32) for r in range(SUBS)]
        for r in range(SUBS):
            cells_ref[2 * r + z] = cells[r]
        strip_ref[12 + z] = packed(cells, half)
        strip_ref[14 + z] = packed(cells, 0)
        for c in range(6):
            strip_ref[2 * c + z] = packed([rhs_ref[c, depth_rows(r, z), :] for r in range(SUBS)], half)
    x, n, d = [jnp.broadcast_to(0.5 * diag_ref[c : c + 1, :], (SUBS, SUBS)) for c in range(3)]
    entries = [x, n, d]
    for c, (f, g) in enumerate(((x, n), (x, d), (n, d))):
        entries.append(jnp.broadcast_to(off_ref[c : c + 1, :], (SUBS, SUBS)) * jnp.sqrt(f * g))
    for c in range(6):
        table_ref[c, :, :] = jnp.zeros((SUBS, LANES), jnp.float32)
        table_ref[c, :, :SUBS] = entries[c]
    for c in range(6):
        single = table_ref[c]
        table_ref[c] = jnp.take_along_axis(single, lane // SUBS, axis=1) + jnp.take_along_axis(
            single, lane % SUBS, axis=1
        )
    own_copy.wait()


def wavefront(stages, events=()):
    edges = {e + lag for _, start, stop, lag in stages for e in (start, stop)}
    edges = sorted(edges | {at for at, _ in events})
    for start, stop in zip(edges, edges[1:]):
        for at, body in events:
            if at == start:
                body()
        active = [st for st in stages if st[1] + st[3] <= start and stop <= st[2] + st[3]]

        def step(s, active=active):
            for body, _, _, lag in reversed(active):
                body(s - lag)

        loop(start, stop, step)


def iterate(sh, v, out, u, keep, s2, coef, z1, t1, p, node, flux, a, b):
    def fluxes(e, above_row):
        bx = (above_row[1] - e[2]) - (sh.above(e[1]) - e[1])
        by = (sh.above(e[0]) - e[0]) - (sh.east(e[2]) - e[2])
        bz = (sh.east(e[1]) - e[1]) - (above_row[0] - e[0])
        return bx, by, bz

    def curl(row, e, e_next):
        result = []
        for part in range(2):
            here = [e[2 * c + part] for c in range(3)]
            bx, by, bz = fluxes(here, (e_next[part], e_next[4 + part]))
            pbx, pbz = get(flux, row, 2 * part), get(flux, row, 2 * part + 1)
            put(flux, row + 1, 2 * part, bx)
            put(flux, row + 1, 2 * part + 1, bz)
            result.append(
                (
                    (pbz - bz) - (sh.below(by) - by),
                    (sh.below(bx) - bx) - (sh.west(bz) - bz),
                    (sh.west(by) - by) - (pbx - bx),
                )
            )
        return [result[k % 2][k // 2] for k in range(6)]

    def tensor(row, e):
        s = [get(s2, row, c) for c in range(6)]
        return [
            s[0] * e[0] + s[3] * e[1] + s[4] * e[2],
            s[3] * e[0] + s[1] * e[1] + s[5] * e[2],
            s[4] * e[0] + s[5] * e[1] + s[2] * e[2],
        ]

    def operator(row, e, e_next):
        k = curl(row, e, e_next)
        si = tensor(row, e[1::2])
        sr = tensor(row, e[0::2])
        return [k[j] - si[j // 2] if j % 2 == 0 else k[j] + sr[j // 2] for j in range(6)]

    def jacobi(row, e, scale):
        result = []
        for c in range(3):
            alpha, beta = get(coef, row, c), get(coef, row, 3 + c)
            result.append(scale * (alpha * e[2 * c] + beta * e[2 * c + 1]))
            result.append(scale * (alpha * e[2 * c + 1] - beta * e[2 * c]))
        return result

    def nodal(row, q, scale):
        alpha, beta = get(coef, row, 6), get(coef, row, 7)
        return [scale * (alpha * q[0] + beta * q[1]), scale * (alpha * q[1] - beta * q[0])]

    def load(ref, row, n=6):
        return [get(ref, row, c) for c in range(n)]

    def store(ref, row, values, base=0):
        for c, value in enumerate(values):
            put(ref, row, base + c, value)

    def zeroth(y):
        store(z1, y, jacobi(y, load(v, y), 0.7))

    def first(y):
        ahead = jacobi(y + 1, load(v, y + 1), 0.7)
        store(z1, y + 1, ahead)
        applied = operator(y, load(z1, y), ahead)
        rest = [r - w for r, w in zip(load(v, y), applied)]
        store(t1, y, rest)
        store(p, y, jacobi(y, rest, 0.6))

    def second(y):
        applied = operator(y, load(p, y), load(p, y + 1))
        rest = [r - w for r, w in zip(load(t1, y), applied)]
        source = []
        for part in range(2):
            x, n, d = rest[part], rest[2 + part], rest[4 + part]
            before = get(node, y, 6 + part)
            put(node, y + 1, 6 + part, n)
            source.append(((sh.west(x) - x) + (before - n)) + (sh.below(d) - d))
        store(node, y, source)
        store(node, y, nodal(y, source, 0.8), 2)

    def third(y):
        w = [get(node, y, 2 + part) for part in range(2)]
        slopes = []
        for part in range(2):
            ahead = get(node, y + 1, 2 + part)
            slopes.append((sh.east(w[part]) - w[part], ahead - w[part], sh.above(w[part]) - w[part]))
        si = tensor(y, slopes[1])
        sr = tensor(y, slopes[0])
        rest = []
        for part in range(2):
            if part == 0:
                x, n, d = [g - s for g, s in zip(slopes[0], si)]
            else:
                x, n, d = [g + s for g, s in zip(slopes[1], sr)]
            before = get(node, y, 6 + part)
            put(node, y + 1, 6 + part, n)
            applied = ((sh.west(x) - x) + (before - n)) + (sh.below(d) - d)
            rest.append(get(node, y, part) - applied)
        fix = nodal(y, rest, 0.5)
        store(node, y, [w[part] + fix[part] for part in range(2)], 4)

    def lift(y):
        w = [get(node, y, 4 + part) for part in range(2)]
        result = []
        for c in range(3):
            for part in range(2):
                k = 2 * c + part
                if c == 0:
                    slope = sh.east(w[part]) - w[part]
                elif c == 1:
                    slope = get(node, y + 1, 4 + part) - w[part]
                else:
                    slope = sh.above(w[part]) - w[part]
                result.append((get(z1, y, k) + get(p, y, k)) + slope)
        store(u, y, result)
        for k in range(6):
            for z in range(2):
                keep[y, k, z] = result[k].parts[2 * z]
        return result

    def fourth(y):
        ahead = lift(y + 1)
        store(out, y, operator(y, load(u, y), ahead))

    return [
        (zeroth, a, a + 1, 0),
        (first, a, b - 1, 1),
        (second, a + 1, b - 2, 3),
        (third, a + 2, b - 3, 5),
        (lift, a + 3, a + 4, 7),
        (fourth, a + 3, b - 4, 8),
    ]


def two_sum(a, b):
    s = a + b
    t = s - a
    return s, (a - (s - t)) + (b - t)


def main_kernel(
    odd_ref, own_ref, first_ref, second_ref, own_pack_ref, first_pack_ref, second_pack_ref, last_ref, table_ref,
    a0_ref, a1_ref, sums_ref,
    v, c0, c1, u, mat, index, pair, s2, coef, z1, t1, p, node, flux,
    keep0, keep1, bulk, packs, last, table, arrived, left,
):
    sh = Shifts()
    lane = lax.broadcasted_iota(jnp.int32, (SUBS, LANES), 1)
    sub = lax.broadcasted_iota(jnp.int32, (SUBS, LANES), 0)
    odd = odd_ref[0]
    first, second = 2 - 2 * odd, 2 * odd
    for ref, slot in ((second_pack_ref, second), (first_pack_ref, first), (own_pack_ref, 1)):
        pltpu.make_async_copy(ref, packs.at[slot], arrived.at[slot]).start()
    for ref, slot in ((second_ref, second), (first_ref, first), (own_ref, 1)):
        pltpu.make_async_copy(ref, bulk.at[slot], arrived.at[3 + slot]).start()
    last_copy = pltpu.make_async_copy(last_ref, last, arrived.at[6])
    table_copy = pltpu.make_async_copy(table_ref, table, arrived.at[7])
    last_copy.start()
    table_copy.start()

    def await_group(slot):
        def body():
            pltpu.make_async_copy(own_pack_ref, packs.at[slot], arrived.at[slot]).wait()
            pltpu.make_async_copy(own_ref, bulk.at[slot], arrived.at[3 + slot]).wait()

        return body

    def spread(strip, r):
        return pltpu.roll(strip, lax.rem(2 * LANES - STRIP // 2 - STRIP * r, LANES), 1)

    def cell_halo(strip, beyond_strip, r):
        ninth = pltpu.roll(beyond_strip, lax.rem(LANES - STRIP * r, LANES), 1)
        return jnp.where(lane == STRIP // 2, ninth, spread(strip, r))

    def unpack(group):
        def body(y):
            r = y - group * SUBS
            for z in range(2):
                for c in range(6):
                    v[y, c, 2 * z] = bulk[group, c, depth_rows(r, z), :]
                    v[y, c, 2 * z + 1] = spread(packs[group, 2 * c + z], r)
                mat[y, 2 * z] = packs[group, 16 + 2 * r + z]
                mat[y, 2 * z + 1] = cell_halo(packs[group, 12 + z], packs[group, 14 + z], r)

        return (body, group * SUBS, group * SUBS + SUBS, 0)

    def beyond(y):
        for z in range(2):
            mat[y, 2 * z] = last[4 + z]
            mat[y, 2 * z + 1] = cell_halo(last[z], last[2 + z], 0)

    def indices(y):
        ids = Field(mat[y, k] for k in range(4))
        both = 8.0 * ids + sh.east(ids)
        for k in range(4):
            index[y, k] = both.parts[k].astype(jnp.int32)

    def pairs(y):
        for k in range(4):
            which = index[y, k]
            for c in range(6):
                pair[y, c, k] = jnp.take_along_axis(table[c], which, axis=1)

    def tensors(y):
        s = [get(pair, y, c) + get(pair, y + 1, c) for c in range(6)]
        for c in range(6):
            put(s2, y, c, s[c])
        for c in range(3):
            inverse = 1.0 / (s[c] * s[c] + 16.0)
            put(coef, y, c, 4.0 * inverse)
            put(coef, y, 3 + c, s[c] * inverse)
        shift = 2.0 * ((s[0] + s[1]) + s[2])
        inverse = 1.0 / (shift * shift + 36.0)
        put(coef, y, 6, 6.0 * inverse)
        put(coef, y, 7, shift * inverse)

    wavefront(
        [
            unpack(0),
            unpack(1),
            unpack(2),
            (beyond, ROWS, ROWS + 1, 0),
            (indices, 0, ROWS + 1, 1),
            (pairs, 0, ROWS + 1, 2),
            (tensors, 0, ROWS, 4),
        ],
        [
            (0, await_group(0)),
            (1, table_copy.wait),
            (SUBS, await_group(1)),
            (2 * SUBS, await_group(2)),
            (ROWS, last_copy.wait),
        ],
    )
    own = pl.ds(HALO, SUBS)
    wavefront(iterate(sh, v, c0, u, keep0, s2, coef, z1, t1, p, node, flux, 0, ROWS))
    first_out = pltpu.make_async_copy(keep0.at[own], a0_ref, left.at[0])
    first_out.start()
    wavefront(
        iterate(sh, c0, c1, u, keep1, s2, coef, z1, t1, p, node, flux, REACH, ROWS - REACH)
    )
    second_out = pltpu.make_async_copy(keep1.at[own], a1_ref, left.at[1])
    second_out.start()

    def dots(r, sums):
        y = HALO + r
        sums = list(sums)
        for c in range(6):
            for z in range(2):
                f, g, h = v[y, c, 2 * z], c0[y, c, 2 * z], c1[y, c, 2 * z]
                for k, term in enumerate((f * f, f * g, g * g, f * h, g * h, h * h)):
                    sums[k] = sums[k] + term
        return tuple(sums)

    zero = jnp.zeros((SUBS, LANES), jnp.float32)
    sums = lax.fori_loop(0, SUBS, dots, (zero,) * 6)
    row = zero
    for k, total in enumerate(sums):
        for step in (4, 2, 1):
            total = total + pltpu.roll(total, step, 0)
        row = jnp.where(sub == k, total, row)
    row = jnp.broadcast_to(jnp.sum(row, axis=1, keepdims=True), (SUBS, LANES))
    row = jnp.where(lane == sub, row, 0.0)
    for step in (4, 2, 1):
        row = row + pltpu.roll(row, step, 0)
    for k in range(16):
        sums_ref[pl.ds(k * SUBS, SUBS), :] = row
    first_out.wait()
    second_out.wait()


def two_sum(a, b):
    s = a + b
    t = s - a
    return s, (a - (s - t)) + (b - t)


def two_product(a, b):
    def split(x):
        t = 4097.0 * x
        high = t - (t - x)
        return high, x - high

    p = a * b
    ah, al = split(a)
    bh, bl = split(b)
    return p, ((ah * bh - p) + ah * bl + al * bh) + al * bl


def quick(s, e):
    t = s + e
    return t, e - (t - s)


def plus(x, y):
    s, e = two_sum(x[0], y[0])
    return quick(s, e + (x[1] + y[1]))


def minus(x, y):
    return plus(x, (-y[0], -y[1]))


def times(x, y):
    p, e = two_product(x[0], y[0])
    return quick(p, e + (x[0] * y[1] + x[1] * y[0]))


def scaled(x, factor):
    p, e = two_product(x[0], jnp.full_like(x[0], factor))
    return quick(p, e + x[1] * factor)


def over(x, y):
    q = x[0] / y[0]
    r = minus(x, times(y, (q, jnp.zeros_like(q))))
    return quick(q, (r[0] + r[1]) / y[0])


def final_kernel(sums_ref, a0_ref, a1_ref, result_ref, hess_ref, out, a0, a1, done):
    lane = lax.broadcasted_iota(jnp.int32, (SUBS, LANES), 1)
    sub = lax.broadcasted_iota(jnp.int32, (SUBS, LANES), 0)
    arriving = [
        pltpu.make_async_copy(a0_ref, a0, done.at[6]),
        pltpu.make_async_copy(a1_ref, a1, done.at[7]),
    ]
    for copy in arriving:
        copy.start()
    level = [(sums_ref[pl.ds(k * SUBS, SUBS), :], None) for k in range(16)]
    while len(level) > 1:
        pairs = []
        for (f, f_rest), (g, g_rest) in zip(level[::2], level[1::2]):
            total, error = two_sum(f, g)
            pairs.append((total, error if f_rest is None else error + (f_rest + g_rest)))
        level = pairs
    total, rest = level[0]
    for step in (4, 2, 1):
        total, error = two_sum(total, pltpu.roll(total, step, 0))
        rest = rest + pltpu.roll(rest, step, 0) + error

    def columns(values):
        picked = jnp.sum(jnp.where(lane == sub, values, 0.0), axis=1, keepdims=True)
        return [jnp.broadcast_to(picked[k : k + 1], (SUBS, LANES)) for k in range(6)]

    bb, bc, cc, bd, cd, dd = [quick(f, g) for f, g in zip(columns(total), columns(rest))]
    eps = (jnp.full((SUBS, LANES), epsilon, jnp.float32), jnp.zeros((SUBS, LANES), jnp.float32))
    beta2 = plus(bb, eps)
    h00 = over(bc, beta2)
    norm1 = minus(minus(cc, times(h00, bc)), times(eps, times(h00, h00)))
    norm1 = (jnp.maximum(norm1[0], 0.0), jnp.where(norm1[0] > 0.0, norm1[1], 0.0))
    tall = plus(norm1, times(eps, beta2))
    x = minus(bd, times(h00, bc))
    y = plus(minus(minus(cd, times(h00, cc)), times(h00, bd)), times(times(h00, h00), bc))
    x_over = over(x, beta2)
    y_over = over(y, tall)
    norm2 = plus(minus(dd, scaled(times(h00, cd), 2.0)), times(times(h00, h00), cc))
    norm2 = minus(norm2, plus(times(x, x_over), times(eps, times(x_over, x_over))))
    norm2 = minus(norm2, plus(times(y, y_over), times(times(eps, beta2), times(y_over, y_over))))
    norm2 = plus(norm2, scaled(times(times(x_over, y_over), times(eps, h00)), 2.0))
    norm2 = over(norm2, tall)

    beta = jnp.sqrt(beta2[0])
    e00 = h00[0]
    e10 = jnp.sqrt(tall[0] / beta2[0])
    e01 = x_over[0] / e10
    e11 = y_over[0]
    e21 = jnp.sqrt(jnp.maximum(norm2[0], 0.0) + epsilon)

    g00 = e00 * e00 + e10 * e10
    g01 = e00 * e01 + e10 * e11
    g11 = e01 * e01 + e11 * e11 + e21 * e21
    l00 = jnp.sqrt(g00)
    l10 = g01 / l00
    l11 = jnp.sqrt(g11 - l10 * l10)
    m0 = beta * e00 / l00
    m1 = (beta * e01 - l10 * m0) / l11
    y1 = m1 / l11
    y0 = (m0 - l10 * y1) / l00
    k0 = (y0 - y1 * e00 / e10) / beta
    k1 = y1 / (e10 * beta)

    table = jnp.where(lane == 0, e00, jnp.where(lane == 1, e10, 0.0))
    later = jnp.where(lane == 0, e01, jnp.where(lane == 1, e11, e21))
    hess_ref[...] = jnp.where(sub == 0, table, later)[:2, :3]
    for copy in arriving:
        copy.wait()
    copies = []
    for c in range(6):
        for row in range(SUBS):
            for z in range(2):
                out[c, depth_rows(row, z), :] = k0 * a0[row, c, z] + k1 * a1[row, c, z]
        copies.append(pltpu.make_async_copy(out.at[c], result_ref.at[c], done.at[c]))
        copies[-1].start()
    for copy in copies:
        copy.wait()


VMEM = pl.BlockSpec(memory_space=pltpu.VMEM)
ANY = pl.BlockSpec(memory_space=pl.ANY)
SMEM = pl.BlockSpec(memory_space=pltpu.SMEM)


def call(kernel, outs, ins, scratch=(), semaphores=(), limit=VMEM_LIMIT):
    return pl.pallas_call(
        kernel,
        out_shape=[jax.ShapeDtypeStruct(shape, jnp.float32) for shape, _ in outs],
        in_specs=ins,
        out_specs=[spec for _, spec in outs],
        scratch_shapes=[pltpu.VMEM(shape, dtype) for shape, dtype in scratch]
        + [pltpu.SemaphoreType.DMA((n,)) for n in semaphores],
        compiler_params=pltpu.CompilerParams(vmem_limit_bytes=limit),
    )


def moved(value, axis, step):
    size = lax.axis_size(axis)
    return lax.ppermute(value, axis, [(i, (i + step) % size) for i in range(size)])


TILE = (SUBS, LANES)
KEPT = (SUBS, 6, 2) + TILE
BLOCK = (6, LANES, LANES)


def floats(*shapes):
    return [(shape, jnp.float32) for shape in shapes]


def rows(n, extra=0):
    return (ROWS + extra, n, 4) + TILE


def strip_call():
    return call(
        strip_kernel,
        [((16,) + TILE, VMEM), ((16,) + TILE, VMEM), ((6,) + TILE, VMEM), (BLOCK, ANY)],
        [ANY] * 4,
        floats(BLOCK) + [((LANES, LANES), jnp.int32)] + floats((3, SUBS), (3, SUBS)),
        (5,),
        60 * 2**20,
    )


def main_call():
    return call(
        main_kernel,
        [(KEPT, ANY), (KEPT, ANY), ((LANES, LANES), VMEM)],
        [SMEM] + [ANY] * 8,
        floats(*[rows(6)] * 4, (ROWS + 1, 4) + TILE)
        + [((ROWS + 1, 4) + TILE, jnp.int32)]
        + floats(rows(6, 1), rows(6), rows(8), *[rows(6)] * 3, rows(8, 1), rows(4, 1))
        + floats((ROWS, 6, 2) + TILE, (ROWS, 6, 2) + TILE)
        + floats((3,) + BLOCK, (3, PACK) + TILE, (6,) + TILE, (6,) + TILE),
        (8, 2),
    )


def final_call():
    return call(
        final_kernel,
        [(BLOCK, ANY), ((2, 3), VMEM)],
        [VMEM, ANY, ANY],
        floats(BLOCK, KEPT, KEPT),
        (8,),
    )


def swapped(value, axis):
    size = lax.axis_size(axis)
    pairs = [(i, i ^ 1) for i in range(size)]
    others = [((i + 1) % size, (j + 1) % size) for i, j in pairs]
    second = lax.ppermute(value, axis, others)
    return lax.ppermute(value, axis, pairs), second


def on_device(right_side, materials, sigma_diag, sigma_off):
    rhs = right_side.reshape(BLOCK)
    bulk = swapped(rhs, "gy")
    strips, cells, table, own = strip_call()(
        rhs, materials.reshape(LANES, LANES), sigma_diag, sigma_off
    )
    first, second = swapped(strips, "gx")
    odd = lax.axis_index("gx") % 2 == 1
    lane = lax.broadcasted_iota(jnp.int32, (14,) + TILE, 2)
    mixed = jnp.where((lane % STRIP < STRIP // 2) == odd, first[:14], second[:14])
    pack = jnp.concatenate([mixed, jnp.where(odd, second[14:], first[14:]), cells])
    packs = swapped(pack, "gy")
    last = moved(pack[12:18], "gy", -2)
    a0, a1, sums = main_call()(
        lax.axis_index("gy").reshape(1) % 2, own, *bulk, pack, *packs, last, table
    )
    gathered = lax.all_to_all(sums, ("gx", "gy"), 0, 0, tiled=True)
    result, hessenberg = final_call()(gathered, a0, a1)
    return result.reshape(right_side.shape), hessenberg.T


def solution(mesh):
    return jax.shard_map(
        on_device,
        mesh=mesh,
        in_specs=(P(None, None, None, "gy", "gx"), P(None, "gy", "gx"), P(), P()),
        out_specs=(P(None, None, None, "gy", "gx"), P()),
        check_vma=False,
    )
```

```python
import jax
import jax.numpy as jnp
from jax import lax
from jax.experimental import pallas as pl
from jax.experimental.pallas import tpu as pltpu
from jax.sharding import PartitionSpec as P

epsilon = 1e-06
LANES = 128
SUBS = 8
REACH = 4
HALO = 2 * REACH
ROWS = SUBS + 2 * HALO
STRIP = 16
PACK = 32
VMEM_LIMIT = 44 * 2**20


class Field:
    def __init__(self, parts):
        self.parts = tuple(parts)

    def zip(self, other, op):
        if isinstance(other, Field):
            return Field(op(a, b) for a, b in zip(self.parts, other.parts))
        return Field(op(a, other) for a in self.parts)

    def __add__(self, other):
        return self.zip(other, lambda a, b: a + b)

    def __sub__(self, other):
        return self.zip(other, lambda a, b: a - b)

    def __mul__(self, other):
        return self.zip(other, lambda a, b: a * b)

    __rmul__ = __mul__

    def __rtruediv__(self, top):
        return Field(top / a for a in self.parts)


class Shifts:
    def __init__(self):
        lane = lax.broadcasted_iota(jnp.int32, (SUBS, LANES), 1)
        sub = lax.broadcasted_iota(jnp.int32, (SUBS, LANES), 0)
        self.first_lane = lane == 0
        self.last_lane = lane == LANES - 1
        self.first_sub = sub == 0
        self.last_sub = sub == SUBS - 1

    def east(self, field):
        r = [pltpu.roll(t, LANES - 1, 1) for t in field.parts]
        return Field(jnp.where(self.last_lane, r[k ^ 1], r[k]) for k in range(4))

    def west(self, field):
        r = [pltpu.roll(t, 1, 1) for t in field.parts]
        return Field(jnp.where(self.first_lane, r[k ^ 1], r[k]) for k in range(4))

    def above(self, field):
        r = [pltpu.roll(t, SUBS - 1, 0) for t in field.parts]
        low = [jnp.where(self.last_sub, r[2 + k], r[k]) for k in range(2)]
        return Field(low + [jnp.where(self.last_sub, 0.0, r[2 + k]) for k in range(2)])

    def below(self, field):
        r = [pltpu.roll(t, 1, 0) for t in field.parts]
        low = [jnp.where(self.first_sub, 0.0, r[k]) for k in range(2)]
        return Field(low + [jnp.where(self.first_sub, r[k], r[2 + k]) for k in range(2)])


def get(ref, row, c):
    return Field(ref[row, c, k] for k in range(4))


def put(ref, row, c, field):
    for k in range(4):
        ref[row, c, k] = field.parts[k]


def loop(start, stop, body):
    lax.fori_loop(start, stop, lambda i, c: (body(i), c)[1], 0)


def depth_rows(y, z):
    return pl.ds(z * SUBS * SUBS + y, SUBS, stride=SUBS)


def strip_kernel(
    rhs_in, mat_in, diag_in, off_in, strip_ref, cells_ref, table_ref, own_ref,
    rhs_ref, mat_ref, diag_ref, off_ref, arrived,
):
    pairs = ((mat_in, mat_ref), (rhs_in, rhs_ref), (diag_in, diag_ref), (off_in, off_ref))
    copies = [pltpu.make_async_copy(f, t, arrived.at[k]) for k, (f, t) in enumerate(pairs)]
    for copy in copies:
        copy.start()
    for copy in copies:
        copy.wait()
    own_copy = pltpu.make_async_copy(rhs_ref, own_ref, arrived.at[4])
    own_copy.start()
    lane = lax.broadcasted_iota(jnp.int32, (SUBS, LANES), 1)
    half = STRIP // 2

    def packed(tiles, offset):
        result = None
        for r, tile in enumerate(tiles):
            shift = (STRIP * r + offset) % LANES
            moved_tile = pltpu.roll(tile, shift, 1) if shift else tile
            result = moved_tile if r == 0 else jnp.where(lane >= STRIP * r, moved_tile, result)
        return result

    for z in range(2):
        cells = [mat_ref[depth_rows(r, z), :].astype(jnp.float32) for r in range(SUBS)]
        for r in range(SUBS):
            cells_ref[2 * r + z] = cells[r]
        strip_ref[12 + z] = packed(cells, half)
        strip_ref[14 + z] = packed(cells, 0)
        for c in range(6):
            strip_ref[2 * c + z] = packed([rhs_ref[c, depth_rows(r, z), :] for r in range(SUBS)], half)
    x, n, d = [jnp.broadcast_to(0.5 * diag_ref[c : c + 1, :], (SUBS, SUBS)) for c in range(3)]
    entries = [x, n, d]
    for c, (f, g) in enumerate(((x, n), (x, d), (n, d))):
        entries.append(jnp.broadcast_to(off_ref[c : c + 1, :], (SUBS, SUBS)) * jnp.sqrt(f * g))
    for c in range(6):
        table_ref[c, :, :] = jnp.zeros((SUBS, LANES), jnp.float32)
        table_ref[c, :, :SUBS] = entries[c]
    for c in range(6):
        single = table_ref[c]
        table_ref[c] = jnp.take_along_axis(single, lane // SUBS, axis=1) + jnp.take_along_axis(
            single, lane % SUBS, axis=1
        )
    own_copy.wait()


def wavefront(stages, events=()):
    edges = {e + lag for _, start, stop, lag in stages for e in (start, stop)}
    edges = sorted(edges | {at for at, _ in events})
    for start, stop in zip(edges, edges[1:]):
        for at, body in events:
            if at == start:
                body()
        active = [st for st in stages if st[1] + st[3] <= start and stop <= st[2] + st[3]]

        def step(s, active=active):
            for body, _, _, lag in reversed(active):
                body(s - lag)

        loop(start, stop, step)


def iterate(sh, v, out, u, keep, s2, coef, z1, t1, p, node, flux, a, b):
    def fluxes(e, above_row):
        bx = (above_row[1] - e[2]) - (sh.above(e[1]) - e[1])
        by = (sh.above(e[0]) - e[0]) - (sh.east(e[2]) - e[2])
        bz = (sh.east(e[1]) - e[1]) - (above_row[0] - e[0])
        return bx, by, bz

    def curl(row, e, e_next):
        result = []
        for part in range(2):
            here = [e[2 * c + part] for c in range(3)]
            bx, by, bz = fluxes(here, (e_next[part], e_next[4 + part]))
            pbx, pbz = get(flux, row, 2 * part), get(flux, row, 2 * part + 1)
            put(flux, row + 1, 2 * part, bx)
            put(flux, row + 1, 2 * part + 1, bz)
            result.append(
                (
                    (pbz - bz) - (sh.below(by) - by),
                    (sh.below(bx) - bx) - (sh.west(bz) - bz),
                    (sh.west(by) - by) - (pbx - bx),
                )
            )
        return [result[k % 2][k // 2] for k in range(6)]

    def tensor(row, e):
        s = [get(s2, row, c) for c in range(6)]
        return [
            s[0] * e[0] + s[3] * e[1] + s[4] * e[2],
            s[3] * e[0] + s[1] * e[1] + s[5] * e[2],
            s[4] * e[0] + s[5] * e[1] + s[2] * e[2],
        ]

    def operator(row, e, e_next):
        k = curl(row, e, e_next)
        si = tensor(row, e[1::2])
        sr = tensor(row, e[0::2])
        return [k[j] - si[j // 2] if j % 2 == 0 else k[j] + sr[j // 2] for j in range(6)]

    def jacobi(row, e, scale):
        result = []
        for c in range(3):
            alpha, beta = get(coef, row, c), get(coef, row, 3 + c)
            result.append(scale * (alpha * e[2 * c] + beta * e[2 * c + 1]))
            result.append(scale * (alpha * e[2 * c + 1] - beta * e[2 * c]))
        return result

    def nodal(row, q, scale):
        alpha, beta = get(coef, row, 6), get(coef, row, 7)
        return [scale * (alpha * q[0] + beta * q[1]), scale * (alpha * q[1] - beta * q[0])]

    def load(ref, row, n=6):
        return [get(ref, row, c) for c in range(n)]

    def store(ref, row, values, base=0):
        for c, value in enumerate(values):
            put(ref, row, base + c, value)

    def zeroth(y):
        store(z1, y, jacobi(y, load(v, y), 0.7))

    def first(y):
        ahead = jacobi(y + 1, load(v, y + 1), 0.7)
        store(z1, y + 1, ahead)
        applied = operator(y, load(z1, y), ahead)
        rest = [r - w for r, w in zip(load(v, y), applied)]
        store(t1, y, rest)
        store(p, y, jacobi(y, rest, 0.6))

    def second(y):
        applied = operator(y, load(p, y), load(p, y + 1))
        rest = [r - w for r, w in zip(load(t1, y), applied)]
        source = []
        for part in range(2):
            x, n, d = rest[part], rest[2 + part], rest[4 + part]
            before = get(node, y, 6 + part)
            put(node, y + 1, 6 + part, n)
            source.append(((sh.west(x) - x) + (before - n)) + (sh.below(d) - d))
        store(node, y, source)
        store(node, y, nodal(y, source, 0.8), 2)

    def third(y):
        w = [get(node, y, 2 + part) for part in range(2)]
        slopes = []
        for part in range(2):
            ahead = get(node, y + 1, 2 + part)
            slopes.append((sh.east(w[part]) - w[part], ahead - w[part], sh.above(w[part]) - w[part]))
        si = tensor(y, slopes[1])
        sr = tensor(y, slopes[0])
        rest = []
        for part in range(2):
            if part == 0:
                x, n, d = [g - s for g, s in zip(slopes[0], si)]
            else:
                x, n, d = [g + s for g, s in zip(slopes[1], sr)]
            before = get(node, y, 6 + part)
            put(node, y + 1, 6 + part, n)
            applied = ((sh.west(x) - x) + (before - n)) + (sh.below(d) - d)
            rest.append(get(node, y, part) - applied)
        fix = nodal(y, rest, 0.5)
        store(node, y, [w[part] + fix[part] for part in range(2)], 4)

    def lift(y):
        w = [get(node, y, 4 + part) for part in range(2)]
        result = []
        for c in range(3):
            for part in range(2):
                k = 2 * c + part
                if c == 0:
                    slope = sh.east(w[part]) - w[part]
                elif c == 1:
                    slope = get(node, y + 1, 4 + part) - w[part]
                else:
                    slope = sh.above(w[part]) - w[part]
                result.append((get(z1, y, k) + get(p, y, k)) + slope)
        store(u, y, result)
        for k in range(6):
            for z in range(2):
                keep[y, k, z] = result[k].parts[2 * z]
        return result

    def fourth(y):
        ahead = lift(y + 1)
        store(out, y, operator(y, load(u, y), ahead))

    return [
        (zeroth, a, a + 1, 0),
        (first, a, b - 1, 1),
        (second, a + 1, b - 2, 3),
        (third, a + 2, b - 3, 5),
        (lift, a + 3, a + 4, 7),
        (fourth, a + 3, b - 4, 8),
    ]


def two_sum(a, b):
    s = a + b
    t = s - a
    return s, (a - (s - t)) + (b - t)


def main_kernel(
    odd_ref, own_ref, first_ref, second_ref, own_pack_ref, first_pack_ref, second_pack_ref, last_ref, table_ref,
    a0_ref, a1_ref, sums_ref,
    v, c0, c1, u, mat, index, pair, s2, coef, z1, t1, p, node, flux,
    keep0, keep1, bulk, packs, last, table, arrived, left,
):
    sh = Shifts()
    lane = lax.broadcasted_iota(jnp.int32, (SUBS, LANES), 1)
    sub = lax.broadcasted_iota(jnp.int32, (SUBS, LANES), 0)
    odd = odd_ref[0]
    first, second = 2 - 2 * odd, 2 * odd
    for ref, slot in ((second_pack_ref, second), (first_pack_ref, first), (own_pack_ref, 1)):
        pltpu.make_async_copy(ref, packs.at[slot], arrived.at[slot]).start()
    for ref, slot in ((second_ref, second), (first_ref, first), (own_ref, 1)):
        pltpu.make_async_copy(ref, bulk.at[slot], arrived.at[3 + slot]).start()
    last_copy = pltpu.make_async_copy(last_ref, last, arrived.at[6])
    table_copy = pltpu.make_async_copy(table_ref, table, arrived.at[7])
    last_copy.start()
    table_copy.start()

    def await_group(slot):
        def body():
            pltpu.make_async_copy(own_pack_ref, packs.at[slot], arrived.at[slot]).wait()
            pltpu.make_async_copy(own_ref, bulk.at[slot], arrived.at[3 + slot]).wait()

        return body

    def spread(strip, r):
        return pltpu.roll(strip, lax.rem(2 * LANES - STRIP // 2 - STRIP * r, LANES), 1)

    def cell_halo(strip, beyond_strip, r):
        ninth = pltpu.roll(beyond_strip, lax.rem(LANES - STRIP * r, LANES), 1)
        return jnp.where(lane == STRIP // 2, ninth, spread(strip, r))

    def unpack(group):
        def body(y):
            r = y - group * SUBS
            for z in range(2):
                for c in range(6):
                    v[y, c, 2 * z] = bulk[group, c, depth_rows(r, z), :]
                    v[y, c, 2 * z + 1] = spread(packs[group, 2 * c + z], r)
                mat[y, 2 * z] = packs[group, 16 + 2 * r + z]
                mat[y, 2 * z + 1] = cell_halo(packs[group, 12 + z], packs[group, 14 + z], r)

        return (body, group * SUBS, group * SUBS + SUBS, 0)

    def beyond(y):
        for z in range(2):
            mat[y, 2 * z] = last[4 + z]
            mat[y, 2 * z + 1] = jnp.where(lane < LANES // 2, last[2 + z], last[z])

    def indices(y):
        ids = Field(mat[y, k] for k in range(4))
        both = 8.0 * ids + sh.east(ids)
        for k in range(4):
            index[y, k] = both.parts[k].astype(jnp.int32)

    def pairs(y):
        for k in range(4):
            which = index[y, k]
            for c in range(6):
                pair[y, c, k] = jnp.take_along_axis(table[c], which, axis=1)

    def tensors(y):
        s = [get(pair, y, c) + get(pair, y + 1, c) for c in range(6)]
        for c in range(6):
            put(s2, y, c, s[c])
        for c in range(3):
            inverse = 1.0 / (s[c] * s[c] + 16.0)
            put(coef, y, c, 4.0 * inverse)
            put(coef, y, 3 + c, s[c] * inverse)
        shift = 2.0 * ((s[0] + s[1]) + s[2])
        inverse = 1.0 / (shift * shift + 36.0)
        put(coef, y, 6, 6.0 * inverse)
        put(coef, y, 7, shift * inverse)

    wavefront(
        [
            unpack(0),
            unpack(1),
            unpack(2),
            (beyond, ROWS, ROWS + 1, 0),
            (indices, 0, ROWS + 1, 1),
            (pairs, 0, ROWS + 1, 2),
            (tensors, 0, ROWS, 4),
        ],
        [
            (0, await_group(0)),
            (1, table_copy.wait),
            (SUBS, await_group(1)),
            (2 * SUBS, await_group(2)),
            (ROWS, last_copy.wait),
        ],
    )
    own = pl.ds(HALO, SUBS)
    wavefront(iterate(sh, v, c0, u, keep0, s2, coef, z1, t1, p, node, flux, 0, ROWS))
    first_out = pltpu.make_async_copy(keep0.at[own], a0_ref, left.at[0])
    first_out.start()
    wavefront(
        iterate(sh, c0, c1, u, keep1, s2, coef, z1, t1, p, node, flux, REACH, ROWS - REACH)
    )
    second_out = pltpu.make_async_copy(keep1.at[own], a1_ref, left.at[1])
    second_out.start()

    def dots(r, sums):
        y = HALO + r
        sums = list(sums)
        for c in range(6):
            for z in range(2):
                f, g, h = v[y, c, 2 * z], c0[y, c, 2 * z], c1[y, c, 2 * z]
                for k, term in enumerate((f * f, f * g, g * g, f * h, g * h, h * h)):
                    sums[k] = sums[k] + term
        return tuple(sums)

    zero = jnp.zeros((SUBS, LANES), jnp.float32)
    sums = lax.fori_loop(0, SUBS, dots, (zero,) * 6)
    row = zero
    for k, total in enumerate(sums):
        for step in (4, 2, 1):
            total = total + pltpu.roll(total, step, 0)
        row = jnp.where(sub == k, total, row)
    row = jnp.broadcast_to(jnp.sum(row, axis=1, keepdims=True), (SUBS, LANES))
    row = jnp.where(lane == sub, row, 0.0)
    for step in (4, 2, 1):
        row = row + pltpu.roll(row, step, 0)
    for k in range(16):
        sums_ref[pl.ds(k * SUBS, SUBS), :] = row
    first_out.wait()
    second_out.wait()


def two_sum(a, b):
    s = a + b
    t = s - a
    return s, (a - (s - t)) + (b - t)


def two_product(a, b):
    def split(x):
        t = 4097.0 * x
        high = t - (t - x)
        return high, x - high

    p = a * b
    ah, al = split(a)
    bh, bl = split(b)
    return p, ((ah * bh - p) + ah * bl + al * bh) + al * bl


def quick(s, e):
    t = s + e
    return t, e - (t - s)


def plus(x, y):
    s, e = two_sum(x[0], y[0])
    return quick(s, e + (x[1] + y[1]))


def minus(x, y):
    return plus(x, (-y[0], -y[1]))


def times(x, y):
    p, e = two_product(x[0], y[0])
    return quick(p, e + (x[0] * y[1] + x[1] * y[0]))


def scaled(x, factor):
    p, e = two_product(x[0], jnp.full_like(x[0], factor))
    return quick(p, e + x[1] * factor)


def over(x, y):
    q = x[0] / y[0]
    r = minus(x, times(y, (q, jnp.zeros_like(q))))
    return quick(q, (r[0] + r[1]) / y[0])


def final_kernel(sums_ref, a0_ref, a1_ref, result_ref, hess_ref, out, a0, a1, done):
    lane = lax.broadcasted_iota(jnp.int32, (SUBS, LANES), 1)
    sub = lax.broadcasted_iota(jnp.int32, (SUBS, LANES), 0)
    arriving = [
        pltpu.make_async_copy(a0_ref, a0, done.at[6]),
        pltpu.make_async_copy(a1_ref, a1, done.at[7]),
    ]
    for copy in arriving:
        copy.start()
    level = [(sums_ref[pl.ds(k * SUBS, SUBS), :], None) for k in range(16)]
    while len(level) > 1:
        pairs = []
        for (f, f_rest), (g, g_rest) in zip(level[::2], level[1::2]):
            total, error = two_sum(f, g)
            pairs.append((total, error if f_rest is None else error + (f_rest + g_rest)))
        level = pairs
    total, rest = level[0]
    for step in (4, 2, 1):
        total, error = two_sum(total, pltpu.roll(total, step, 0))
        rest = rest + pltpu.roll(rest, step, 0) + error

    def columns(values):
        picked = jnp.sum(jnp.where(lane == sub, values, 0.0), axis=1, keepdims=True)
        return [jnp.broadcast_to(picked[k : k + 1], (SUBS, LANES)) for k in range(6)]

    bb, bc, cc, bd, cd, dd = [quick(f, g) for f, g in zip(columns(total), columns(rest))]
    eps = (jnp.full((SUBS, LANES), epsilon, jnp.float32), jnp.zeros((SUBS, LANES), jnp.float32))
    beta2 = plus(bb, eps)
    h00 = over(bc, beta2)
    norm1 = minus(minus(cc, times(h00, bc)), times(eps, times(h00, h00)))
    norm1 = (jnp.maximum(norm1[0], 0.0), jnp.where(norm1[0] > 0.0, norm1[1], 0.0))
    tall = plus(norm1, times(eps, beta2))
    x = minus(bd, times(h00, bc))
    y = plus(minus(minus(cd, times(h00, cc)), times(h00, bd)), times(times(h00, h00), bc))
    x_over = over(x, beta2)
    y_over = over(y, tall)
    norm2 = plus(minus(dd, scaled(times(h00, cd), 2.0)), times(times(h00, h00), cc))
    norm2 = minus(norm2, plus(times(x, x_over), times(eps, times(x_over, x_over))))
    norm2 = minus(norm2, plus(times(y, y_over), times(times(eps, beta2), times(y_over, y_over))))
    norm2 = plus(norm2, scaled(times(times(x_over, y_over), times(eps, h00)), 2.0))
    norm2 = over(norm2, tall)

    beta = jnp.sqrt(beta2[0])
    e00 = h00[0]
    e10 = jnp.sqrt(tall[0] / beta2[0])
    e01 = x_over[0] / e10
    e11 = y_over[0]
    e21 = jnp.sqrt(jnp.maximum(norm2[0], 0.0) + epsilon)

    g00 = e00 * e00 + e10 * e10
    g01 = e00 * e01 + e10 * e11
    g11 = e01 * e01 + e11 * e11 + e21 * e21
    l00 = jnp.sqrt(g00)
    l10 = g01 / l00
    l11 = jnp.sqrt(g11 - l10 * l10)
    m0 = beta * e00 / l00
    m1 = (beta * e01 - l10 * m0) / l11
    y1 = m1 / l11
    y0 = (m0 - l10 * y1) / l00
    k0 = (y0 - y1 * e00 / e10) / beta
    k1 = y1 / (e10 * beta)

    table = jnp.where(lane == 0, e00, jnp.where(lane == 1, e10, 0.0))
    later = jnp.where(lane == 0, e01, jnp.where(lane == 1, e11, e21))
    hess_ref[...] = jnp.where(sub == 0, table, later)[:2, :3]
    for copy in arriving:
        copy.wait()
    copies = []
    for c in range(6):
        for row in range(SUBS):
            for z in range(2):
                out[c, depth_rows(row, z), :] = k0 * a0[row, c, z] + k1 * a1[row, c, z]
        copies.append(pltpu.make_async_copy(out.at[c], result_ref.at[c], done.at[c]))
        copies[-1].start()
    for copy in copies:
        copy.wait()


VMEM = pl.BlockSpec(memory_space=pltpu.VMEM)
ANY = pl.BlockSpec(memory_space=pl.ANY)
SMEM = pl.BlockSpec(memory_space=pltpu.SMEM)


def call(kernel, outs, ins, scratch=(), semaphores=(), limit=VMEM_LIMIT):
    return pl.pallas_call(
        kernel,
        out_shape=[jax.ShapeDtypeStruct(shape, jnp.float32) for shape, _ in outs],
        in_specs=ins,
        out_specs=[spec for _, spec in outs],
        scratch_shapes=[pltpu.VMEM(shape, dtype) for shape, dtype in scratch]
        + [pltpu.SemaphoreType.DMA((n,)) for n in semaphores],
        compiler_params=pltpu.CompilerParams(vmem_limit_bytes=limit),
    )


def moved(value, axis, step):
    size = lax.axis_size(axis)
    return lax.ppermute(value, axis, [(i, (i + step) % size) for i in range(size)])


TILE = (SUBS, LANES)
KEPT = (SUBS, 6, 2) + TILE
BLOCK = (6, LANES, LANES)


def floats(*shapes):
    return [(shape, jnp.float32) for shape in shapes]


def rows(n, extra=0):
    return (ROWS + extra, n, 4) + TILE


def strip_call():
    return call(
        strip_kernel,
        [((16,) + TILE, VMEM), ((16,) + TILE, VMEM), ((6,) + TILE, VMEM), (BLOCK, ANY)],
        [ANY] * 4,
        floats(BLOCK) + [((LANES, LANES), jnp.int32)] + floats((3, SUBS), (3, SUBS)),
        (5,),
        60 * 2**20,
    )


def main_call():
    return call(
        main_kernel,
        [(KEPT, ANY), (KEPT, ANY), ((LANES, LANES), VMEM)],
        [SMEM] + [ANY] * 8,
        floats(*[rows(6)] * 4, (ROWS + 1, 4) + TILE)
        + [((ROWS + 1, 4) + TILE, jnp.int32)]
        + floats(rows(6, 1), rows(6), rows(8), *[rows(6)] * 3, rows(8, 1), rows(4, 1))
        + floats((ROWS, 6, 2) + TILE, (ROWS, 6, 2) + TILE)
        + floats((3,) + BLOCK, (3, PACK) + TILE, (6,) + TILE, (6,) + TILE),
        (8, 2),
    )


def final_call():
    return call(
        final_kernel,
        [(BLOCK, ANY), ((2, 3), VMEM)],
        [VMEM, ANY, ANY],
        floats(BLOCK, KEPT, KEPT),
        (8,),
    )


def swapped(value, axis):
    size = lax.axis_size(axis)
    pairs = [(i, i ^ 1) for i in range(size)]
    others = [((i + 1) % size, (j + 1) % size) for i, j in pairs]
    second = lax.ppermute(value, axis, others)
    return lax.ppermute(value, axis, pairs), second


def on_device(right_side, materials, sigma_diag, sigma_off):
    rhs = right_side.reshape(BLOCK)
    bulk = swapped(rhs, "gy")
    strips, cells, table, own = strip_call()(
        rhs, materials.reshape(LANES, LANES), sigma_diag, sigma_off
    )
    row = moved(materials[:, 0, :].astype(jnp.float32).reshape((2,) + TILE), "gy", -2)
    first, second = swapped(strips, "gx")
    odd = lax.axis_index("gx") % 2 == 1
    lane = lax.broadcasted_iota(jnp.int32, (14,) + TILE, 2)
    mixed = jnp.where((lane % STRIP < STRIP // 2) == odd, first[:14], second[:14])
    pack = jnp.concatenate([mixed, jnp.where(odd, second[14:], first[14:]), cells])
    packs = swapped(pack, "gy")
    side_first, side_second = swapped(row, "gx")
    left, right = jnp.where(odd, side_first, side_second), jnp.where(odd, side_second, side_first)
    last = jnp.concatenate([left, right, row])
    a0, a1, sums = main_call()(
        lax.axis_index("gy").reshape(1) % 2, own, *bulk, pack, *packs, last, table
    )
    gathered = lax.all_to_all(sums, ("gx", "gy"), 0, 0, tiled=True)
    result, hessenberg = final_call()(gathered, a0, a1)
    return result.reshape(right_side.shape), hessenberg.T


def solution(mesh):
    return jax.shard_map(
        on_device,
        mesh=mesh,
        in_specs=(P(None, None, None, "gy", "gx"), P(None, "gy", "gx"), P(), P()),
        out_specs=(P(None, None, None, "gy", "gx"), P()),
        check_vma=False,
    )
```

```python
import jax
import jax.numpy as jnp
from jax import lax
from jax.experimental import pallas as pl
from jax.experimental.pallas import tpu as pltpu
from jax.sharding import PartitionSpec as P

epsilon = 1e-06
LANES = 128
SUBS = 8
REACH = 4
HALO = 2 * REACH
ROWS = SUBS + 2 * HALO
STRIP = 16
PACK = 32
VMEM_LIMIT = 44 * 2**20


class Field:
    def __init__(self, parts):
        self.parts = tuple(parts)

    def zip(self, other, op):
        if isinstance(other, Field):
            return Field(op(a, b) for a, b in zip(self.parts, other.parts))
        return Field(op(a, other) for a in self.parts)

    def __add__(self, other):
        return self.zip(other, lambda a, b: a + b)

    def __sub__(self, other):
        return self.zip(other, lambda a, b: a - b)

    def __mul__(self, other):
        return self.zip(other, lambda a, b: a * b)

    __rmul__ = __mul__

    def __rtruediv__(self, top):
        return Field(top / a for a in self.parts)


class Shifts:
    def __init__(self):
        lane = lax.broadcasted_iota(jnp.int32, (SUBS, LANES), 1)
        sub = lax.broadcasted_iota(jnp.int32, (SUBS, LANES), 0)
        self.first_lane = lane == 0
        self.last_lane = lane == LANES - 1
        self.first_sub = sub == 0
        self.last_sub = sub == SUBS - 1

    def east(self, field):
        r = [pltpu.roll(t, LANES - 1, 1) for t in field.parts]
        return Field(jnp.where(self.last_lane, r[k ^ 1], r[k]) for k in range(4))

    def west(self, field):
        r = [pltpu.roll(t, 1, 1) for t in field.parts]
        return Field(jnp.where(self.first_lane, r[k ^ 1], r[k]) for k in range(4))

    def above(self, field):
        r = [pltpu.roll(t, SUBS - 1, 0) for t in field.parts]
        low = [jnp.where(self.last_sub, r[2 + k], r[k]) for k in range(2)]
        return Field(low + [jnp.where(self.last_sub, 0.0, r[2 + k]) for k in range(2)])

    def below(self, field):
        r = [pltpu.roll(t, 1, 0) for t in field.parts]
        low = [jnp.where(self.first_sub, 0.0, r[k]) for k in range(2)]
        return Field(low + [jnp.where(self.first_sub, r[k], r[2 + k]) for k in range(2)])


def get(ref, row, c):
    return Field(ref[row, c, k] for k in range(4))


def put(ref, row, c, field):
    for k in range(4):
        ref[row, c, k] = field.parts[k]


def loop(start, stop, body):
    lax.fori_loop(start, stop, lambda i, c: (body(i), c)[1], 0)


def depth_rows(y, z):
    return pl.ds(z * SUBS * SUBS + y, SUBS, stride=SUBS)


def strip_kernel(
    rhs_in, mat_in, diag_in, off_in, strip_ref, table_ref, own_ref,
    rhs_ref, mat_ref, diag_ref, off_ref, arrived,
):
    pairs = ((mat_in, mat_ref), (rhs_in, rhs_ref), (diag_in, diag_ref), (off_in, off_ref))
    copies = [pltpu.make_async_copy(f, t, arrived.at[k]) for k, (f, t) in enumerate(pairs)]
    for copy in copies:
        copy.start()
    for copy in copies:
        copy.wait()
    own_copy = pltpu.make_async_copy(rhs_ref, own_ref, arrived.at[4])
    own_copy.start()
    lane = lax.broadcasted_iota(jnp.int32, (SUBS, LANES), 1)
    half = STRIP // 2

    def packed(tiles, offset):
        result = None
        for r, tile in enumerate(tiles):
            shift = (STRIP * r + offset) % LANES
            moved_tile = pltpu.roll(tile, shift, 1) if shift else tile
            result = moved_tile if r == 0 else jnp.where(lane >= STRIP * r, moved_tile, result)
        return result

    for z in range(2):
        cells = [mat_ref[depth_rows(r, z), :].astype(jnp.float32) for r in range(SUBS)]
        strip_ref[12 + z] = packed(cells, half)
        strip_ref[14 + z] = packed(cells, 0)
        for c in range(6):
            strip_ref[2 * c + z] = packed([rhs_ref[c, depth_rows(r, z), :] for r in range(SUBS)], half)
    x, n, d = [jnp.broadcast_to(0.5 * diag_ref[c : c + 1, :], (SUBS, SUBS)) for c in range(3)]
    entries = [x, n, d]
    for c, (f, g) in enumerate(((x, n), (x, d), (n, d))):
        entries.append(jnp.broadcast_to(off_ref[c : c + 1, :], (SUBS, SUBS)) * jnp.sqrt(f * g))
    for c in range(6):
        table_ref[c, :, :] = jnp.zeros((SUBS, LANES), jnp.float32)
        table_ref[c, :, :SUBS] = entries[c]
    for c in range(6):
        single = table_ref[c]
        table_ref[c] = jnp.take_along_axis(single, lane // SUBS, axis=1) + jnp.take_along_axis(
            single, lane % SUBS, axis=1
        )
    own_copy.wait()


def wavefront(stages, events=()):
    edges = {e + lag for _, start, stop, lag in stages for e in (start, stop)}
    edges = sorted(edges | {at for at, _ in events})
    for start, stop in zip(edges, edges[1:]):
        for at, body in events:
            if at == start:
                body()
        active = [st for st in stages if st[1] + st[3] <= start and stop <= st[2] + st[3]]

        def step(s, active=active):
            for body, _, _, lag in reversed(active):
                body(s - lag)

        loop(start, stop, step)


def iterate(sh, v, out, u, keep, s2, coef, z1, t1, p, node, flux, a, b):
    def fluxes(e, above_row):
        bx = (above_row[1] - e[2]) - (sh.above(e[1]) - e[1])
        by = (sh.above(e[0]) - e[0]) - (sh.east(e[2]) - e[2])
        bz = (sh.east(e[1]) - e[1]) - (above_row[0] - e[0])
        return bx, by, bz

    def curl(row, e, e_next):
        result = []
        for part in range(2):
            here = [e[2 * c + part] for c in range(3)]
            bx, by, bz = fluxes(here, (e_next[part], e_next[4 + part]))
            pbx, pbz = get(flux, row, 2 * part), get(flux, row, 2 * part + 1)
            put(flux, row + 1, 2 * part, bx)
            put(flux, row + 1, 2 * part + 1, bz)
            result.append(
                (
                    (pbz - bz) - (sh.below(by) - by),
                    (sh.below(bx) - bx) - (sh.west(bz) - bz),
                    (sh.west(by) - by) - (pbx - bx),
                )
            )
        return [result[k % 2][k // 2] for k in range(6)]

    def tensor(row, e):
        s = [get(s2, row, c) for c in range(6)]
        return [
            s[0] * e[0] + s[3] * e[1] + s[4] * e[2],
            s[3] * e[0] + s[1] * e[1] + s[5] * e[2],
            s[4] * e[0] + s[5] * e[1] + s[2] * e[2],
        ]

    def operator(row, e, e_next):
        k = curl(row, e, e_next)
        si = tensor(row, e[1::2])
        sr = tensor(row, e[0::2])
        return [k[j] - si[j // 2] if j % 2 == 0 else k[j] + sr[j // 2] for j in range(6)]

    def jacobi(row, e, scale):
        result = []
        for c in range(3):
            alpha, beta = get(coef, row, c), get(coef, row, 3 + c)
            result.append(scale * (alpha * e[2 * c] + beta * e[2 * c + 1]))
            result.append(scale * (alpha * e[2 * c + 1] - beta * e[2 * c]))
        return result

    def nodal(row, q, scale):
        alpha, beta = get(coef, row, 6), get(coef, row, 7)
        return [scale * (alpha * q[0] + beta * q[1]), scale * (alpha * q[1] - beta * q[0])]

    def load(ref, row, n=6):
        return [get(ref, row, c) for c in range(n)]

    def store(ref, row, values, base=0):
        for c, value in enumerate(values):
            put(ref, row, base + c, value)

    def zeroth(y):
        store(z1, y, jacobi(y, load(v, y), 0.7))

    def first(y):
        ahead = jacobi(y + 1, load(v, y + 1), 0.7)
        store(z1, y + 1, ahead)
        applied = operator(y, load(z1, y), ahead)
        rest = [r - w for r, w in zip(load(v, y), applied)]
        store(t1, y, rest)
        store(p, y, jacobi(y, rest, 0.6))

    def second(y):
        applied = operator(y, load(p, y), load(p, y + 1))
        rest = [r - w for r, w in zip(load(t1, y), applied)]
        source = []
        for part in range(2):
            x, n, d = rest[part], rest[2 + part], rest[4 + part]
            before = get(node, y, 6 + part)
            put(node, y + 1, 6 + part, n)
            source.append(((sh.west(x) - x) + (before - n)) + (sh.below(d) - d))
        store(node, y, source)
        store(node, y, nodal(y, source, 0.8), 2)

    def third(y):
        w = [get(node, y, 2 + part) for part in range(2)]
        slopes = []
        for part in range(2):
            ahead = get(node, y + 1, 2 + part)
            slopes.append((sh.east(w[part]) - w[part], ahead - w[part], sh.above(w[part]) - w[part]))
        si = tensor(y, slopes[1])
        sr = tensor(y, slopes[0])
        rest = []
        for part in range(2):
            if part == 0:
                x, n, d = [g - s for g, s in zip(slopes[0], si)]
            else:
                x, n, d = [g + s for g, s in zip(slopes[1], sr)]
            before = get(node, y, 6 + part)
            put(node, y + 1, 6 + part, n)
            applied = ((sh.west(x) - x) + (before - n)) + (sh.below(d) - d)
            rest.append(get(node, y, part) - applied)
        fix = nodal(y, rest, 0.5)
        store(node, y, [w[part] + fix[part] for part in range(2)], 4)

    def lift(y):
        w = [get(node, y, 4 + part) for part in range(2)]
        result = []
        for c in range(3):
            for part in range(2):
                k = 2 * c + part
                if c == 0:
                    slope = sh.east(w[part]) - w[part]
                elif c == 1:
                    slope = get(node, y + 1, 4 + part) - w[part]
                else:
                    slope = sh.above(w[part]) - w[part]
                result.append((get(z1, y, k) + get(p, y, k)) + slope)
        store(u, y, result)
        for k in range(6):
            for z in range(2):
                keep[y, k, z] = result[k].parts[2 * z]
        return result

    def fourth(y):
        ahead = lift(y + 1)
        store(out, y, operator(y, load(u, y), ahead))

    return [
        (zeroth, a, a + 1, 0),
        (first, a, b - 1, 1),
        (second, a + 1, b - 2, 3),
        (third, a + 2, b - 3, 5),
        (lift, a + 3, a + 4, 7),
        (fourth, a + 3, b - 4, 8),
    ]


def two_sum(a, b):
    s = a + b
    t = s - a
    return s, (a - (s - t)) + (b - t)


def main_kernel(
    odd_ref, own_ref, first_ref, second_ref, own_pack_ref, first_pack_ref, second_pack_ref, last_ref, table_ref,
    a0_ref, a1_ref, sums_ref,
    v, c0, c1, u, mat, index, pair, s2, coef, z1, t1, p, node, flux,
    keep0, keep1, bulk, packs, last, table, arrived, left,
):
    sh = Shifts()
    lane = lax.broadcasted_iota(jnp.int32, (SUBS, LANES), 1)
    sub = lax.broadcasted_iota(jnp.int32, (SUBS, LANES), 0)
    odd = odd_ref[0]
    first, second = 2 - 2 * odd, 2 * odd
    for ref, slot in ((second_pack_ref, second), (first_pack_ref, first), (own_pack_ref, 1)):
        pltpu.make_async_copy(ref, packs.at[slot], arrived.at[slot]).start()
    for ref, slot in ((second_ref, second), (first_ref, first), (own_ref, 1)):
        pltpu.make_async_copy(ref, bulk.at[slot], arrived.at[3 + slot]).start()
    last_copy = pltpu.make_async_copy(last_ref, last, arrived.at[6])
    table_copy = pltpu.make_async_copy(table_ref, table, arrived.at[7])
    last_copy.start()
    table_copy.start()

    def await_group(slot):
        def body():
            pltpu.make_async_copy(own_pack_ref, packs.at[slot], arrived.at[slot]).wait()
            pltpu.make_async_copy(own_ref, bulk.at[slot], arrived.at[3 + slot]).wait()

        return body

    def spread(strip, r):
        return pltpu.roll(strip, lax.rem(2 * LANES - STRIP // 2 - STRIP * r, LANES), 1)

    def cell_halo(strip, beyond_strip, r):
        ninth = pltpu.roll(beyond_strip, lax.rem(LANES - STRIP * r, LANES), 1)
        return jnp.where(lane == STRIP // 2, ninth, spread(strip, r))

    def strip(group, k):
        return packs[group, pl.ds(SUBS * k, SUBS), :]

    def unpack(group):
        def body(y):
            r = y - group * SUBS
            for z in range(2):
                for c in range(6):
                    v[y, c, 2 * z] = bulk[group, c, depth_rows(r, z), :]
                    v[y, c, 2 * z + 1] = spread(strip(group, 2 * c + z), r)
                mat[y, 2 * z] = packs[group, depth_rows(r, 2 + z), :]
                mat[y, 2 * z + 1] = cell_halo(strip(group, 12 + z), strip(group, 14 + z), r)

        return (body, group * SUBS, group * SUBS + SUBS, 0)

    def beyond(y):
        for z in range(2):
            mat[y, 2 * z] = last[4 + z]
            mat[y, 2 * z + 1] = cell_halo(last[z], last[2 + z], 0)

    def indices(y):
        ids = Field(mat[y, k] for k in range(4))
        both = 8.0 * ids + sh.east(ids)
        for k in range(4):
            index[y, k] = both.parts[k].astype(jnp.int32)

    def pairs(y):
        for k in range(4):
            which = index[y, k]
            for c in range(6):
                pair[y, c, k] = jnp.take_along_axis(table[c], which, axis=1)

    def tensors(y):
        s = [get(pair, y, c) + get(pair, y + 1, c) for c in range(6)]
        for c in range(6):
            put(s2, y, c, s[c])
        for c in range(3):
            inverse = 1.0 / (s[c] * s[c] + 16.0)
            put(coef, y, c, 4.0 * inverse)
            put(coef, y, 3 + c, s[c] * inverse)
        shift = 2.0 * ((s[0] + s[1]) + s[2])
        inverse = 1.0 / (shift * shift + 36.0)
        put(coef, y, 6, 6.0 * inverse)
        put(coef, y, 7, shift * inverse)

    wavefront(
        [
            unpack(0),
            unpack(1),
            unpack(2),
            (beyond, ROWS, ROWS + 1, 0),
            (indices, 0, ROWS + 1, 1),
            (pairs, 0, ROWS + 1, 2),
            (tensors, 0, ROWS, 4),
        ],
        [
            (0, await_group(0)),
            (1, table_copy.wait),
            (SUBS, await_group(1)),
            (2 * SUBS, await_group(2)),
            (ROWS, last_copy.wait),
        ],
    )
    own = pl.ds(HALO, SUBS)
    wavefront(iterate(sh, v, c0, u, keep0, s2, coef, z1, t1, p, node, flux, 0, ROWS))
    first_out = pltpu.make_async_copy(keep0.at[own], a0_ref, left.at[0])
    first_out.start()
    wavefront(
        iterate(sh, c0, c1, u, keep1, s2, coef, z1, t1, p, node, flux, REACH, ROWS - REACH)
    )
    second_out = pltpu.make_async_copy(keep1.at[own], a1_ref, left.at[1])
    second_out.start()

    def dots(r, sums):
        y = HALO + r
        sums = list(sums)
        for c in range(6):
            for z in range(2):
                f, g, h = v[y, c, 2 * z], c0[y, c, 2 * z], c1[y, c, 2 * z]
                for k, term in enumerate((f * f, f * g, g * g, f * h, g * h, h * h)):
                    sums[k] = sums[k] + term
        return tuple(sums)

    zero = jnp.zeros((SUBS, LANES), jnp.float32)
    sums = lax.fori_loop(0, SUBS, dots, (zero,) * 6)
    row = zero
    for k, total in enumerate(sums):
        for step in (4, 2, 1):
            total = total + pltpu.roll(total, step, 0)
        row = jnp.where(sub == k, total, row)
    row = jnp.broadcast_to(jnp.sum(row, axis=1, keepdims=True), (SUBS, LANES))
    row = jnp.where(lane == sub, row, 0.0)
    for step in (4, 2, 1):
        row = row + pltpu.roll(row, step, 0)
    for k in range(16):
        sums_ref[pl.ds(k * SUBS, SUBS), :] = row
    first_out.wait()
    second_out.wait()


def two_sum(a, b):
    s = a + b
    t = s - a
    return s, (a - (s - t)) + (b - t)


def two_product(a, b):
    def split(x):
        t = 4097.0 * x
        high = t - (t - x)
        return high, x - high

    p = a * b
    ah, al = split(a)
    bh, bl = split(b)
    return p, ((ah * bh - p) + ah * bl + al * bh) + al * bl


def quick(s, e):
    t = s + e
    return t, e - (t - s)


def plus(x, y):
    s, e = two_sum(x[0], y[0])
    return quick(s, e + (x[1] + y[1]))


def minus(x, y):
    return plus(x, (-y[0], -y[1]))


def times(x, y):
    p, e = two_product(x[0], y[0])
    return quick(p, e + (x[0] * y[1] + x[1] * y[0]))


def scaled(x, factor):
    p, e = two_product(x[0], jnp.full_like(x[0], factor))
    return quick(p, e + x[1] * factor)


def over(x, y):
    q = x[0] / y[0]
    r = minus(x, times(y, (q, jnp.zeros_like(q))))
    return quick(q, (r[0] + r[1]) / y[0])


def final_kernel(sums_ref, a0_ref, a1_ref, result_ref, hess_ref, out, a0, a1, done):
    lane = lax.broadcasted_iota(jnp.int32, (SUBS, LANES), 1)
    sub = lax.broadcasted_iota(jnp.int32, (SUBS, LANES), 0)
    arriving = [
        pltpu.make_async_copy(a0_ref, a0, done.at[6]),
        pltpu.make_async_copy(a1_ref, a1, done.at[7]),
    ]
    for copy in arriving:
        copy.start()
    level = [(sums_ref[pl.ds(k * SUBS, SUBS), :], None) for k in range(16)]
    while len(level) > 1:
        pairs = []
        for (f, f_rest), (g, g_rest) in zip(level[::2], level[1::2]):
            total, error = two_sum(f, g)
            pairs.append((total, error if f_rest is None else error + (f_rest + g_rest)))
        level = pairs
    total, rest = level[0]
    for step in (4, 2, 1):
        total, error = two_sum(total, pltpu.roll(total, step, 0))
        rest = rest + pltpu.roll(rest, step, 0) + error

    def columns(values):
        picked = jnp.sum(jnp.where(lane == sub, values, 0.0), axis=1, keepdims=True)
        return [jnp.broadcast_to(picked[k : k + 1], (SUBS, LANES)) for k in range(6)]

    bb, bc, cc, bd, cd, dd = [quick(f, g) for f, g in zip(columns(total), columns(rest))]
    eps = (jnp.full((SUBS, LANES), epsilon, jnp.float32), jnp.zeros((SUBS, LANES), jnp.float32))
    beta2 = plus(bb, eps)
    h00 = over(bc, beta2)
    norm1 = minus(minus(cc, times(h00, bc)), times(eps, times(h00, h00)))
    norm1 = (jnp.maximum(norm1[0], 0.0), jnp.where(norm1[0] > 0.0, norm1[1], 0.0))
    tall = plus(norm1, times(eps, beta2))
    x = minus(bd, times(h00, bc))
    y = plus(minus(minus(cd, times(h00, cc)), times(h00, bd)), times(times(h00, h00), bc))
    x_over = over(x, beta2)
    y_over = over(y, tall)
    norm2 = plus(minus(dd, scaled(times(h00, cd), 2.0)), times(times(h00, h00), cc))
    norm2 = minus(norm2, plus(times(x, x_over), times(eps, times(x_over, x_over))))
    norm2 = minus(norm2, plus(times(y, y_over), times(times(eps, beta2), times(y_over, y_over))))
    norm2 = plus(norm2, scaled(times(times(x_over, y_over), times(eps, h00)), 2.0))
    norm2 = over(norm2, tall)

    beta = jnp.sqrt(beta2[0])
    e00 = h00[0]
    e10 = jnp.sqrt(tall[0] / beta2[0])
    e01 = x_over[0] / e10
    e11 = y_over[0]
    e21 = jnp.sqrt(jnp.maximum(norm2[0], 0.0) + epsilon)

    g00 = e00 * e00 + e10 * e10
    g01 = e00 * e01 + e10 * e11
    g11 = e01 * e01 + e11 * e11 + e21 * e21
    l00 = jnp.sqrt(g00)
    l10 = g01 / l00
    l11 = jnp.sqrt(g11 - l10 * l10)
    m0 = beta * e00 / l00
    m1 = (beta * e01 - l10 * m0) / l11
    y1 = m1 / l11
    y0 = (m0 - l10 * y1) / l00
    k0 = (y0 - y1 * e00 / e10) / beta
    k1 = y1 / (e10 * beta)

    table = jnp.where(lane == 0, e00, jnp.where(lane == 1, e10, 0.0))
    later = jnp.where(lane == 0, e01, jnp.where(lane == 1, e11, e21))
    hess_ref[...] = jnp.where(sub == 0, table, later)[:2, :3]
    for copy in arriving:
        copy.wait()
    copies = []
    for c in range(6):
        for row in range(SUBS):
            for z in range(2):
                out[c, depth_rows(row, z), :] = k0 * a0[row, c, z] + k1 * a1[row, c, z]
        copies.append(pltpu.make_async_copy(out.at[c], result_ref.at[c], done.at[c]))
        copies[-1].start()
    for copy in copies:
        copy.wait()


VMEM = pl.BlockSpec(memory_space=pltpu.VMEM)
ANY = pl.BlockSpec(memory_space=pl.ANY)
SMEM = pl.BlockSpec(memory_space=pltpu.SMEM)


def call(kernel, outs, ins, scratch=(), semaphores=(), limit=VMEM_LIMIT):
    return pl.pallas_call(
        kernel,
        out_shape=[jax.ShapeDtypeStruct(shape, jnp.float32) for shape, _ in outs],
        in_specs=ins,
        out_specs=[spec for _, spec in outs],
        scratch_shapes=[pltpu.VMEM(shape, dtype) for shape, dtype in scratch]
        + [pltpu.SemaphoreType.DMA((n,)) for n in semaphores],
        compiler_params=pltpu.CompilerParams(vmem_limit_bytes=limit),
    )


def moved(value, axis, step):
    size = lax.axis_size(axis)
    return lax.ppermute(value, axis, [(i, (i + step) % size) for i in range(size)])


TILE = (SUBS, LANES)
KEPT = (SUBS, 6, 2) + TILE
BLOCK = (6, LANES, LANES)


def floats(*shapes):
    return [(shape, jnp.float32) for shape in shapes]


def rows(n, extra=0):
    return (ROWS + extra, n, 4) + TILE


def strip_call():
    return call(
        strip_kernel,
        [((16,) + TILE, VMEM), ((6,) + TILE, VMEM), (BLOCK, ANY)],
        [ANY] * 4,
        floats(BLOCK) + [((LANES, LANES), jnp.int32)] + floats((3, SUBS), (3, SUBS)),
        (5,),
        60 * 2**20,
    )


def main_call():
    return call(
        main_kernel,
        [(KEPT, ANY), (KEPT, ANY), ((LANES, LANES), VMEM)],
        [SMEM] + [ANY] * 8,
        floats(*[rows(6)] * 4, (ROWS + 1, 4) + TILE)
        + [((ROWS + 1, 4) + TILE, jnp.int32)]
        + floats(rows(6, 1), rows(6), rows(8), *[rows(6)] * 3, rows(8, 1), rows(4, 1))
        + floats((ROWS, 6, 2) + TILE, (ROWS, 6, 2) + TILE)
        + floats((3,) + BLOCK, (3, SUBS * PACK, LANES), (6,) + TILE, (6,) + TILE),
        (8, 2),
    )


def final_call():
    return call(
        final_kernel,
        [(BLOCK, ANY), ((2, 3), VMEM)],
        [VMEM, ANY, ANY],
        floats(BLOCK, KEPT, KEPT),
        (8,),
    )


def swapped(value, axis):
    size = lax.axis_size(axis)
    pairs = [(i, i ^ 1) for i in range(size)]
    others = [((i + 1) % size, (j + 1) % size) for i, j in pairs]
    second = lax.ppermute(value, axis, others)
    return lax.ppermute(value, axis, pairs), second


def on_device(right_side, materials, sigma_diag, sigma_off):
    rhs = right_side.reshape(BLOCK)
    bulk = swapped(rhs, "gy")
    strips, table, own = strip_call()(
        rhs, materials.reshape(LANES, LANES), sigma_diag, sigma_off
    )
    first, second = swapped(strips, "gx")
    odd = lax.axis_index("gx") % 2 == 1
    lane = lax.broadcasted_iota(jnp.int32, (14,) + TILE, 2)
    mixed = jnp.where((lane % STRIP < STRIP // 2) == odd, first[:14], second[:14])
    beyond = jnp.where(odd, second[14:], first[14:])
    pack = jnp.concatenate([mixed, beyond, materials.astype(jnp.float32)])
    pack = pack.reshape(SUBS * PACK, LANES)
    packs = swapped(pack, "gy")
    first_row = materials[:, 0, :].astype(jnp.float32).reshape((2,) + TILE)
    last = moved(jnp.concatenate([mixed[12:], beyond, first_row]), "gy", -2)
    a0, a1, sums = main_call()(
        lax.axis_index("gy").reshape(1) % 2, own, *bulk, pack, *packs, last, table
    )
    gathered = lax.all_to_all(sums, ("gx", "gy"), 0, 0, tiled=True)
    result, hessenberg = final_call()(gathered, a0, a1)
    return result.reshape(right_side.shape), hessenberg.T


def solution(mesh):
    return jax.shard_map(
        on_device,
        mesh=mesh,
        in_specs=(P(None, None, None, "gy", "gx"), P(None, "gy", "gx"), P(), P()),
        out_specs=(P(None, None, None, "gy", "gx"), P()),
        check_vma=False,
    )
```

```python
import jax
import jax.numpy as jnp
from jax import lax
from jax.experimental import pallas as pl
from jax.experimental.pallas import tpu as pltpu
from jax.sharding import PartitionSpec as P

epsilon = 1e-06
LANES = 128
SUBS = 8
REACH = 4
HALO = 2 * REACH
ROWS = SUBS + 2 * HALO
STRIP = 16
PACK = 32
VMEM_LIMIT = 44 * 2**20


class Field:
    def __init__(self, parts):
        self.parts = tuple(parts)

    def zip(self, other, op):
        if isinstance(other, Field):
            return Field(op(a, b) for a, b in zip(self.parts, other.parts))
        return Field(op(a, other) for a in self.parts)

    def __add__(self, other):
        return self.zip(other, lambda a, b: a + b)

    def __sub__(self, other):
        return self.zip(other, lambda a, b: a - b)

    def __mul__(self, other):
        return self.zip(other, lambda a, b: a * b)

    __rmul__ = __mul__

    def __rtruediv__(self, top):
        return Field(top / a for a in self.parts)


class Shifts:
    def __init__(self):
        lane = lax.broadcasted_iota(jnp.int32, (SUBS, LANES), 1)
        sub = lax.broadcasted_iota(jnp.int32, (SUBS, LANES), 0)
        self.first_lane = lane == 0
        self.last_lane = lane == LANES - 1
        self.first_sub = sub == 0
        self.last_sub = sub == SUBS - 1

    def east(self, field):
        r = [pltpu.roll(t, LANES - 1, 1) for t in field.parts]
        return Field(jnp.where(self.last_lane, r[k ^ 1], r[k]) for k in range(4))

    def west(self, field):
        r = [pltpu.roll(t, 1, 1) for t in field.parts]
        return Field(jnp.where(self.first_lane, r[k ^ 1], r[k]) for k in range(4))

    def above(self, field):
        r = [pltpu.roll(t, SUBS - 1, 0) for t in field.parts]
        low = [jnp.where(self.last_sub, r[2 + k], r[k]) for k in range(2)]
        return Field(low + [jnp.where(self.last_sub, 0.0, r[2 + k]) for k in range(2)])

    def below(self, field):
        r = [pltpu.roll(t, 1, 0) for t in field.parts]
        low = [jnp.where(self.first_sub, 0.0, r[k]) for k in range(2)]
        return Field(low + [jnp.where(self.first_sub, r[k], r[2 + k]) for k in range(2)])


def get(ref, row, c):
    return Field(ref[row, c, k] for k in range(4))


def put(ref, row, c, field):
    for k in range(4):
        ref[row, c, k] = field.parts[k]


def loop(start, stop, body):
    lax.fori_loop(start, stop, lambda i, c: (body(i), c)[1], 0)


def depth_rows(y, z):
    return pl.ds(z * SUBS * SUBS + y, SUBS, stride=SUBS)


def strip_kernel(
    rhs_in, mat_in, diag_in, off_in, strip_ref, table_ref, own_ref,
    rhs_ref, mat_ref, diag_ref, off_ref, arrived,
):
    pairs = ((mat_in, mat_ref), (rhs_in, rhs_ref), (diag_in, diag_ref), (off_in, off_ref))
    copies = [pltpu.make_async_copy(f, t, arrived.at[k]) for k, (f, t) in enumerate(pairs)]
    own_copy = pltpu.make_async_copy(rhs_in, own_ref, arrived.at[4])
    for copy in copies + [own_copy]:
        copy.start()
    for copy in copies:
        copy.wait()
    lane = lax.broadcasted_iota(jnp.int32, (SUBS, LANES), 1)
    half = STRIP // 2

    def packed(tiles, offset):
        result = None
        for r, tile in enumerate(tiles):
            shift = (STRIP * r + offset) % LANES
            moved_tile = pltpu.roll(tile, shift, 1) if shift else tile
            result = moved_tile if r == 0 else jnp.where(lane >= STRIP * r, moved_tile, result)
        return result

    for z in range(2):
        cells = [mat_ref[depth_rows(r, z), :].astype(jnp.float32) for r in range(SUBS)]
        strip_ref[12 + z] = packed(cells, half)
        strip_ref[14 + z] = packed(cells, 0)
        for c in range(6):
            strip_ref[2 * c + z] = packed([rhs_ref[c, depth_rows(r, z), :] for r in range(SUBS)], half)
    x, n, d = [jnp.broadcast_to(0.5 * diag_ref[c : c + 1, :], (SUBS, SUBS)) for c in range(3)]
    entries = [x, n, d]
    for c, (f, g) in enumerate(((x, n), (x, d), (n, d))):
        entries.append(jnp.broadcast_to(off_ref[c : c + 1, :], (SUBS, SUBS)) * jnp.sqrt(f * g))
    for c in range(6):
        table_ref[c, :, :] = jnp.zeros((SUBS, LANES), jnp.float32)
        table_ref[c, :, :SUBS] = entries[c]
    for c in range(6):
        single = table_ref[c]
        table_ref[c] = jnp.take_along_axis(single, lane // SUBS, axis=1) + jnp.take_along_axis(
            single, lane % SUBS, axis=1
        )
    own_copy.wait()


def wavefront(stages, events=()):
    edges = {e + lag for _, start, stop, lag in stages for e in (start, stop)}
    edges = sorted(edges | {at for at, _ in events})
    for start, stop in zip(edges, edges[1:]):
        for at, body in events:
            if at == start:
                body()
        active = [st for st in stages if st[1] + st[3] <= start and stop <= st[2] + st[3]]

        def step(s, active=active):
            for body, _, _, lag in reversed(active):
                body(s - lag)

        loop(start, stop, step)


def iterate(sh, v, out, u, keep, s2, coef, z1, t1, p, node, flux, a, b):
    def fluxes(e, above_row):
        bx = (above_row[1] - e[2]) - (sh.above(e[1]) - e[1])
        by = (sh.above(e[0]) - e[0]) - (sh.east(e[2]) - e[2])
        bz = (sh.east(e[1]) - e[1]) - (above_row[0] - e[0])
        return bx, by, bz

    def curl(row, e, e_next):
        result = []
        for part in range(2):
            here = [e[2 * c + part] for c in range(3)]
            bx, by, bz = fluxes(here, (e_next[part], e_next[4 + part]))
            pbx, pbz = get(flux, row, 2 * part), get(flux, row, 2 * part + 1)
            put(flux, row + 1, 2 * part, bx)
            put(flux, row + 1, 2 * part + 1, bz)
            result.append(
                (
                    (pbz - bz) - (sh.below(by) - by),
                    (sh.below(bx) - bx) - (sh.west(bz) - bz),
                    (sh.west(by) - by) - (pbx - bx),
                )
            )
        return [result[k % 2][k // 2] for k in range(6)]

    def tensor(row, e):
        s = [get(s2, row, c) for c in range(6)]
        return [
            s[0] * e[0] + s[3] * e[1] + s[4] * e[2],
            s[3] * e[0] + s[1] * e[1] + s[5] * e[2],
            s[4] * e[0] + s[5] * e[1] + s[2] * e[2],
        ]

    def operator(row, e, e_next):
        k = curl(row, e, e_next)
        si = tensor(row, e[1::2])
        sr = tensor(row, e[0::2])
        return [k[j] - si[j // 2] if j % 2 == 0 else k[j] + sr[j // 2] for j in range(6)]

    def jacobi(row, e, scale):
        result = []
        for c in range(3):
            alpha, beta = get(coef, row, c), get(coef, row, 3 + c)
            result.append(scale * (alpha * e[2 * c] + beta * e[2 * c + 1]))
            result.append(scale * (alpha * e[2 * c + 1] - beta * e[2 * c]))
        return result

    def nodal(row, q, scale):
        alpha, beta = get(coef, row, 6), get(coef, row, 7)
        return [scale * (alpha * q[0] + beta * q[1]), scale * (alpha * q[1] - beta * q[0])]

    def load(ref, row, n=6):
        return [get(ref, row, c) for c in range(n)]

    def store(ref, row, values, base=0):
        for c, value in enumerate(values):
            put(ref, row, base + c, value)

    def zeroth(y):
        store(z1, y, jacobi(y, load(v, y), 0.7))

    def first(y):
        ahead = jacobi(y + 1, load(v, y + 1), 0.7)
        store(z1, y + 1, ahead)
        applied = operator(y, load(z1, y), ahead)
        rest = [r - w for r, w in zip(load(v, y), applied)]
        store(t1, y, rest)
        store(p, y, jacobi(y, rest, 0.6))

    def second(y):
        applied = operator(y, load(p, y), load(p, y + 1))
        rest = [r - w for r, w in zip(load(t1, y), applied)]
        source = []
        for part in range(2):
            x, n, d = rest[part], rest[2 + part], rest[4 + part]
            before = get(node, y, 6 + part)
            put(node, y + 1, 6 + part, n)
            source.append(((sh.west(x) - x) + (before - n)) + (sh.below(d) - d))
        store(node, y, source)
        store(node, y, nodal(y, source, 0.8), 2)

    def third(y):
        w = [get(node, y, 2 + part) for part in range(2)]
        slopes = []
        for part in range(2):
            ahead = get(node, y + 1, 2 + part)
            slopes.append((sh.east(w[part]) - w[part], ahead - w[part], sh.above(w[part]) - w[part]))
        si = tensor(y, slopes[1])
        sr = tensor(y, slopes[0])
        rest = []
        for part in range(2):
            if part == 0:
                x, n, d = [g - s for g, s in zip(slopes[0], si)]
            else:
                x, n, d = [g + s for g, s in zip(slopes[1], sr)]
            before = get(node, y, 6 + part)
            put(node, y + 1, 6 + part, n)
            applied = ((sh.west(x) - x) + (before - n)) + (sh.below(d) - d)
            rest.append(get(node, y, part) - applied)
        fix = nodal(y, rest, 0.5)
        store(node, y, [w[part] + fix[part] for part in range(2)], 4)

    def lift(y):
        w = [get(node, y, 4 + part) for part in range(2)]
        result = []
        for c in range(3):
            for part in range(2):
                k = 2 * c + part
                if c == 0:
                    slope = sh.east(w[part]) - w[part]
                elif c == 1:
                    slope = get(node, y + 1, 4 + part) - w[part]
                else:
                    slope = sh.above(w[part]) - w[part]
                result.append((get(z1, y, k) + get(p, y, k)) + slope)
        store(u, y, result)
        for k in range(6):
            for z in range(2):
                keep[y, k, z] = result[k].parts[2 * z]
        return result

    def fourth(y):
        ahead = lift(y + 1)
        store(out, y, operator(y, load(u, y), ahead))

    return [
        (zeroth, a, a + 1, 0),
        (first, a, b - 1, 1),
        (second, a + 1, b - 2, 3),
        (third, a + 2, b - 3, 5),
        (lift, a + 3, a + 4, 7),
        (fourth, a + 3, b - 4, 8),
    ]


def two_sum(a, b):
    s = a + b
    t = s - a
    return s, (a - (s - t)) + (b - t)


def main_kernel(
    odd_ref, own_ref, first_ref, second_ref, own_pack_ref, first_pack_ref, second_pack_ref, last_ref, table_ref,
    a0_ref, a1_ref, sums_ref,
    v, c0, c1, u, mat, index, pair, s2, coef, z1, t1, p, node, flux,
    keep0, keep1, bulk, packs, last, table, arrived, left,
):
    sh = Shifts()
    lane = lax.broadcasted_iota(jnp.int32, (SUBS, LANES), 1)
    sub = lax.broadcasted_iota(jnp.int32, (SUBS, LANES), 0)
    odd = odd_ref[0]
    first, second = 2 - 2 * odd, 2 * odd
    for ref, slot in ((second_pack_ref, second), (first_pack_ref, first), (own_pack_ref, 1)):
        pltpu.make_async_copy(ref, packs.at[slot], arrived.at[slot]).start()
    for ref, slot in ((second_ref, second), (first_ref, first), (own_ref, 1)):
        pltpu.make_async_copy(ref, bulk.at[slot], arrived.at[3 + slot]).start()
    last_copy = pltpu.make_async_copy(last_ref, last, arrived.at[6])
    table_copy = pltpu.make_async_copy(table_ref, table, arrived.at[7])
    last_copy.start()
    table_copy.start()

    def await_group(slot):
        def body():
            pltpu.make_async_copy(own_pack_ref, packs.at[slot], arrived.at[slot]).wait()
            pltpu.make_async_copy(own_ref, bulk.at[slot], arrived.at[3 + slot]).wait()

        return body

    def spread(strip, r):
        return pltpu.roll(strip, lax.rem(2 * LANES - STRIP // 2 - STRIP * r, LANES), 1)

    def cell_halo(strip, beyond_strip, r):
        ninth = pltpu.roll(beyond_strip, lax.rem(LANES - STRIP * r, LANES), 1)
        return jnp.where(lane == STRIP // 2, ninth, spread(strip, r))

    def strip(group, k):
        return packs[group, pl.ds(SUBS * k, SUBS), :]

    def unpack(group):
        def body(y):
            r = y - group * SUBS
            for z in range(2):
                for c in range(6):
                    v[y, c, 2 * z] = bulk[group, c, depth_rows(r, z), :]
                    v[y, c, 2 * z + 1] = spread(strip(group, 2 * c + z), r)
                mat[y, 2 * z] = packs[group, depth_rows(r, 2 + z), :]
                mat[y, 2 * z + 1] = cell_halo(strip(group, 12 + z), strip(group, 14 + z), r)

        return (body, group * SUBS, group * SUBS + SUBS, 0)

    def beyond(y):
        for z in range(2):
            mat[y, 2 * z] = last[4 + z]
            mat[y, 2 * z + 1] = cell_halo(last[z], last[2 + z], 0)

    def indices(y):
        ids = Field(mat[y, k] for k in range(4))
        both = 8.0 * ids + sh.east(ids)
        for k in range(4):
            index[y, k] = both.parts[k].astype(jnp.int32)

    def pairs(y):
        for k in range(4):
            which = index[y, k]
            for c in range(6):
                pair[y, c, k] = jnp.take_along_axis(table[c], which, axis=1)

    def tensors(y):
        s = [get(pair, y, c) + get(pair, y + 1, c) for c in range(6)]
        for c in range(6):
            put(s2, y, c, s[c])
        for c in range(3):
            inverse = 1.0 / (s[c] * s[c] + 16.0)
            put(coef, y, c, 4.0 * inverse)
            put(coef, y, 3 + c, s[c] * inverse)
        shift = 2.0 * ((s[0] + s[1]) + s[2])
        inverse = 1.0 / (shift * shift + 36.0)
        put(coef, y, 6, 6.0 * inverse)
        put(coef, y, 7, shift * inverse)

    wavefront(
        [
            unpack(0),
            unpack(1),
            unpack(2),
            (beyond, ROWS, ROWS + 1, 0),
            (indices, 0, ROWS + 1, 1),
            (pairs, 0, ROWS + 1, 2),
            (tensors, 0, ROWS, 4),
        ],
        [
            (0, await_group(0)),
            (1, table_copy.wait),
            (SUBS, await_group(1)),
            (2 * SUBS, await_group(2)),
            (ROWS, last_copy.wait),
        ],
    )
    own = pl.ds(HALO, SUBS)
    wavefront(iterate(sh, v, c0, u, keep0, s2, coef, z1, t1, p, node, flux, 0, ROWS))
    first_out = pltpu.make_async_copy(keep0.at[own], a0_ref, left.at[0])
    first_out.start()
    wavefront(
        iterate(sh, c0, c1, u, keep1, s2, coef, z1, t1, p, node, flux, REACH, ROWS - REACH)
    )
    second_out = pltpu.make_async_copy(keep1.at[own], a1_ref, left.at[1])
    second_out.start()

    def dots(r, sums):
        y = HALO + r
        sums = list(sums)
        for c in range(6):
            for z in range(2):
                f, g, h = v[y, c, 2 * z], c0[y, c, 2 * z], c1[y, c, 2 * z]
                for k, term in enumerate((f * f, f * g, g * g, f * h, g * h, h * h)):
                    sums[k] = sums[k] + term
        return tuple(sums)

    zero = jnp.zeros((SUBS, LANES), jnp.float32)
    sums = lax.fori_loop(0, SUBS, dots, (zero,) * 6)
    row = zero
    for k, total in enumerate(sums):
        for step in (4, 2, 1):
            total = total + pltpu.roll(total, step, 0)
        row = jnp.where(sub == k, total, row)
    row = jnp.broadcast_to(jnp.sum(row, axis=1, keepdims=True), (SUBS, LANES))
    row = jnp.where(lane == sub, row, 0.0)
    for step in (4, 2, 1):
        row = row + pltpu.roll(row, step, 0)
    for k in range(16):
        sums_ref[pl.ds(k * SUBS, SUBS), :] = row
    first_out.wait()
    second_out.wait()


def two_sum(a, b):
    s = a + b
    t = s - a
    return s, (a - (s - t)) + (b - t)


def two_product(a, b):
    def split(x):
        t = 4097.0 * x
        high = t - (t - x)
        return high, x - high

    p = a * b
    ah, al = split(a)
    bh, bl = split(b)
    return p, ((ah * bh - p) + ah * bl + al * bh) + al * bl


def quick(s, e):
    t = s + e
    return t, e - (t - s)


def plus(x, y):
    s, e = two_sum(x[0], y[0])
    return quick(s, e + (x[1] + y[1]))


def minus(x, y):
    return plus(x, (-y[0], -y[1]))


def times(x, y):
    p, e = two_product(x[0], y[0])
    return quick(p, e + (x[0] * y[1] + x[1] * y[0]))


def scaled(x, factor):
    p, e = two_product(x[0], jnp.full_like(x[0], factor))
    return quick(p, e + x[1] * factor)


def over(x, y):
    q = x[0] / y[0]
    r = minus(x, times(y, (q, jnp.zeros_like(q))))
    return quick(q, (r[0] + r[1]) / y[0])


def final_kernel(sums_ref, a0_ref, a1_ref, result_ref, hess_ref, out, a0, a1, done):
    lane = lax.broadcasted_iota(jnp.int32, (SUBS, LANES), 1)
    sub = lax.broadcasted_iota(jnp.int32, (SUBS, LANES), 0)
    arriving = [
        pltpu.make_async_copy(a0_ref, a0, done.at[6]),
        pltpu.make_async_copy(a1_ref, a1, done.at[7]),
    ]
    for copy in arriving:
        copy.start()
    level = [(sums_ref[pl.ds(k * SUBS, SUBS), :], None) for k in range(16)]
    while len(level) > 1:
        pairs = []
        for (f, f_rest), (g, g_rest) in zip(level[::2], level[1::2]):
            total, error = two_sum(f, g)
            pairs.append((total, error if f_rest is None else error + (f_rest + g_rest)))
        level = pairs
    total, rest = level[0]
    for step in (4, 2, 1):
        total, error = two_sum(total, pltpu.roll(total, step, 0))
        rest = rest + pltpu.roll(rest, step, 0) + error

    def columns(values):
        picked = jnp.sum(jnp.where(lane == sub, values, 0.0), axis=1, keepdims=True)
        return [jnp.broadcast_to(picked[k : k + 1], (SUBS, LANES)) for k in range(6)]

    bb, bc, cc, bd, cd, dd = [quick(f, g) for f, g in zip(columns(total), columns(rest))]
    eps = (jnp.full((SUBS, LANES), epsilon, jnp.float32), jnp.zeros((SUBS, LANES), jnp.float32))
    beta2 = plus(bb, eps)
    h00 = over(bc, beta2)
    norm1 = minus(minus(cc, times(h00, bc)), times(eps, times(h00, h00)))
    norm1 = (jnp.maximum(norm1[0], 0.0), jnp.where(norm1[0] > 0.0, norm1[1], 0.0))
    tall = plus(norm1, times(eps, beta2))
    x = minus(bd, times(h00, bc))
    y = plus(minus(minus(cd, times(h00, cc)), times(h00, bd)), times(times(h00, h00), bc))
    x_over = over(x, beta2)
    y_over = over(y, tall)
    norm2 = plus(minus(dd, scaled(times(h00, cd), 2.0)), times(times(h00, h00), cc))
    norm2 = minus(norm2, plus(times(x, x_over), times(eps, times(x_over, x_over))))
    norm2 = minus(norm2, plus(times(y, y_over), times(times(eps, beta2), times(y_over, y_over))))
    norm2 = plus(norm2, scaled(times(times(x_over, y_over), times(eps, h00)), 2.0))
    norm2 = over(norm2, tall)

    beta = jnp.sqrt(beta2[0])
    e00 = h00[0]
    e10 = jnp.sqrt(tall[0] / beta2[0])
    e01 = x_over[0] / e10
    e11 = y_over[0]
    e21 = jnp.sqrt(jnp.maximum(norm2[0], 0.0) + epsilon)

    g00 = e00 * e00 + e10 * e10
    g01 = e00 * e01 + e10 * e11
    g11 = e01 * e01 + e11 * e11 + e21 * e21
    l00 = jnp.sqrt(g00)
    l10 = g01 / l00
    l11 = jnp.sqrt(g11 - l10 * l10)
    m0 = beta * e00 / l00
    m1 = (beta * e01 - l10 * m0) / l11
    y1 = m1 / l11
    y0 = (m0 - l10 * y1) / l00
    k0 = (y0 - y1 * e00 / e10) / beta
    k1 = y1 / (e10 * beta)

    table = jnp.where(lane == 0, e00, jnp.where(lane == 1, e10, 0.0))
    later = jnp.where(lane == 0, e01, jnp.where(lane == 1, e11, e21))
    hess_ref[...] = jnp.where(sub == 0, table, later)[:2, :3]
    for copy in arriving:
        copy.wait()
    copies = []
    for c in range(6):
        for row in range(SUBS):
            for z in range(2):
                out[c, depth_rows(row, z), :] = k0 * a0[row, c, z] + k1 * a1[row, c, z]
        copies.append(pltpu.make_async_copy(out.at[c], result_ref.at[c], done.at[c]))
        copies[-1].start()
    for copy in copies:
        copy.wait()


VMEM = pl.BlockSpec(memory_space=pltpu.VMEM)
ANY = pl.BlockSpec(memory_space=pl.ANY)
SMEM = pl.BlockSpec(memory_space=pltpu.SMEM)


def call(kernel, outs, ins, scratch=(), semaphores=(), limit=VMEM_LIMIT):
    return pl.pallas_call(
        kernel,
        out_shape=[jax.ShapeDtypeStruct(shape, jnp.float32) for shape, _ in outs],
        in_specs=ins,
        out_specs=[spec for _, spec in outs],
        scratch_shapes=[pltpu.VMEM(shape, dtype) for shape, dtype in scratch]
        + [pltpu.SemaphoreType.DMA((n,)) for n in semaphores],
        compiler_params=pltpu.CompilerParams(vmem_limit_bytes=limit),
    )


def moved(value, axis, step):
    size = lax.axis_size(axis)
    return lax.ppermute(value, axis, [(i, (i + step) % size) for i in range(size)])


TILE = (SUBS, LANES)
KEPT = (SUBS, 6, 2) + TILE
BLOCK = (6, LANES, LANES)


def floats(*shapes):
    return [(shape, jnp.float32) for shape in shapes]


def rows(n, extra=0):
    return (ROWS + extra, n, 4) + TILE


def strip_call():
    return call(
        strip_kernel,
        [((16,) + TILE, VMEM), ((6,) + TILE, VMEM), (BLOCK, ANY)],
        [ANY] * 4,
        floats(BLOCK) + [((LANES, LANES), jnp.int32)] + floats((3, SUBS), (3, SUBS)),
        (5,),
        60 * 2**20,
    )


def main_call():
    return call(
        main_kernel,
        [(KEPT, ANY), (KEPT, ANY), ((LANES, LANES), VMEM)],
        [SMEM] + [ANY] * 8,
        floats(*[rows(6)] * 4, (ROWS + 1, 4) + TILE)
        + [((ROWS + 1, 4) + TILE, jnp.int32)]
        + floats(rows(6, 1), rows(6), rows(8), *[rows(6)] * 3, rows(8, 1), rows(4, 1))
        + floats((ROWS, 6, 2) + TILE, (ROWS, 6, 2) + TILE)
        + floats((3,) + BLOCK, (3, SUBS * PACK, LANES), (6,) + TILE, (6,) + TILE),
        (8, 2),
    )


def final_call():
    return call(
        final_kernel,
        [(BLOCK, ANY), ((2, 3), VMEM)],
        [VMEM, ANY, ANY],
        floats(BLOCK, KEPT, KEPT),
        (8,),
    )


def swapped(value, axis):
    size = lax.axis_size(axis)
    pairs = [(i, i ^ 1) for i in range(size)]
    others = [((i + 1) % size, (j + 1) % size) for i, j in pairs]
    second = lax.ppermute(value, axis, others)
    return lax.ppermute(value, axis, pairs), second


def on_device(right_side, materials, sigma_diag, sigma_off):
    rhs = right_side.reshape(BLOCK)
    bulk = swapped(rhs, "gy")
    strips, table, own = strip_call()(
        rhs, materials.reshape(LANES, LANES), sigma_diag, sigma_off
    )
    first, second = swapped(strips, "gx")
    odd = lax.axis_index("gx") % 2 == 1
    lane = lax.broadcasted_iota(jnp.int32, (14,) + TILE, 2)
    mixed = jnp.where((lane % STRIP < STRIP // 2) == odd, first[:14], second[:14])
    beyond = jnp.where(odd, second[14:], first[14:])
    pack = jnp.concatenate([mixed, beyond, materials.astype(jnp.float32)])
    pack = pack.reshape(SUBS * PACK, LANES)
    packs = swapped(pack, "gy")
    first_row = materials[:, 0, :].astype(jnp.float32).reshape((2,) + TILE)
    last = moved(jnp.concatenate([mixed[12:], beyond, first_row]), "gy", -2)
    a0, a1, sums = main_call()(
        lax.axis_index("gy").reshape(1) % 2, own, *bulk, pack, *packs, last, table
    )
    gathered = lax.all_to_all(sums, ("gx", "gy"), 0, 0, tiled=True)
    result, hessenberg = final_call()(gathered, a0, a1)
    return result.reshape(right_side.shape), hessenberg.T


def solution(mesh):
    return jax.shard_map(
        on_device,
        mesh=mesh,
        in_specs=(P(None, None, None, "gy", "gx"), P(None, "gy", "gx"), P(), P()),
        out_specs=(P(None, None, None, "gy", "gx"), P()),
        check_vma=False,
    )
```
